32 devices in a mesh: section: 4 (over y, x), orient: 8 (over z, core).
Axes of the slice: x: 2, y: 2, z: 4, core: 2. Of those that a mesh axis runs over, the one named last changes fastest.
Arguments:
- patterns: bfloat16 [4, 128, 65536], P('section', None, 'orient'), may hold values from -6 to 6
- detector_gain: float32 [65536], P('orient'), may hold values from 0.1 to 1.9
- background: float32 [65536], P('orient'), may hold values from -6 to 6
- bin_map: int32 [65536], P('orient'), may hold values from 0 to 12287, as said below
- templates: bfloat16 [12800, 12288], P(('section', 'orient')), may hold values from -0.0546875 to 0.0546875
- best_picks: int32 [4, 128], replicated, may hold values from 0 to 12799
Outputs:
- top_scores: float32 [4, 128, 8], P('section')
- refined: float32 [4, 128, 3], P('section', 'orient')
The draws below stay inside these ranges and needn't reach their ends.
Inputs may be any that keep to these rules, and one draw needn't show every extreme that they name: `bin_map`: each pixel's polar bin r * 192 + a, with r given by the pixel's distance and a by its direction from a beam centre near the middle of the square detector.
All inputs are finite; a program needn't handle non-finite values.
Results may differ from the reference program's by a relative error of at most 0.0065.
Values may be sent and summed in bfloat16 or wider, within the bound.
No kernel may reach another device: no remote copies, remote signals or barrier semaphores. Data moves between devices by JAX's collectives and lax.ppermute only.
A program may use at most 256 MiB of HBM per device.

```python
import math
import jax
import jax.numpy as jnp
import numpy as np
from jax import lax

NPIX = 65536
RAD = 64
ANG = 192
TOPK = 8
REACH = 1
PATTERNS = 128
MICRO = 4
TEMPLATES = 12800


def draw_bin_map(key, part):
    side = math.isqrt(NPIX)
    offsets = jax.random.randint(jax.random.fold_in(key, 11), (2,), 0, side // 16 + 1)
    pixel_ids = jnp.arange(NPIX, dtype=jnp.int32)
    across = 2 * (pixel_ids % side) + 1 - side - offsets[0]
    down = 2 * (pixel_ids // side) + 1 - side - offsets[1]
    distance = across * across + down * down
    limit = jnp.max(distance) + 1
    edges = jnp.arange(1, RAD, dtype=jnp.int32)
    radial = jnp.sum((RAD * RAD * distance[:, None] >= edges[None, :] * edges[None, :] * limit).astype(jnp.int32), axis=1)
    angles = 2.0 * np.pi * np.arange(ANG + 1) / ANG
    cos_table = jnp.asarray((4096.0 * np.cos(angles) + 8192.5).astype(np.int32) - 8192)
    sin_table = jnp.asarray((4096.0 * np.sin(angles) + 8192.5).astype(np.int32) - 8192)
    cross = cos_table[None, :] * down[:, None] - sin_table[None, :] * across[:, None]
    inside = (cross[:, :ANG] >= 0) & (cross[:, 1:] < 0)
    sector = jnp.sum(inside.astype(jnp.int32) * jnp.arange(ANG, dtype=jnp.int32)[None, :], axis=1)
    rotated = (sector - sector[0] + 2 * ANG - 1) % ANG
    return (radial * ANG + rotated).astype(jnp.int32)


def plant(drawn, key, low, largest):
    longest = drawn.shape.index(max(drawn.shape))
    spots = []
    for shift in (0, 1):
        where = [jax.random.randint(jax.random.fold_in(key, axis), (), 0, length) for axis, length in enumerate(drawn.shape)]
        where[longest] = (where[longest] + shift) % drawn.shape[longest]
        spots.append(tuple(where))
    return drawn.at[spots[0]].set(low).at[spots[1]].set(largest)


def levels(key, shape, pieces, least, high):
    level, own = 1.0, jax.random.fold_in(key, 6)
    for axis_at, parts in pieces:
        draws = jnp.exp(jax.random.uniform(jax.random.fold_in(own, axis_at), (parts,), jnp.float32, least / len(pieces), high / len(pieces)))
        level = level * jnp.repeat(draws, shape[axis_at] // parts).reshape([-1 if axis == axis_at else 1 for axis in range(len(shape))])
    return level


def rank_table(count, slope):
    weights = [(1 << 20) // math.isqrt(standing ** slope) + 1 for standing in range(1, count + 1)]
    scale = 1 + sum(weights) // (1 << 30)
    return np.cumsum(np.array([max(1, weight // scale) for weight in weights]))


def ranked_ids(key, extent, count, lean):
    listing = rank_table(count, lean)
    pick = jax.random.randint(jax.random.fold_in(key, 1), extent, 0, int(listing[count - 1]))
    grade = jnp.searchsorted(jnp.asarray(listing, jnp.int32), pick, side="right")
    return jax.random.permutation(jax.random.fold_in(key, 2), count)[grade].astype(jnp.int32)


def scatter_about(stream_key, dims, scale, most, shards=(), kind=jnp.bfloat16):
    drawn = jax.random.normal(stream_key, dims, jnp.float32) * scale
    if len(shards) > 0:
        drawn = levels(stream_key, dims, shards, -0.22, 0.18) * drawn
    return jnp.clip(drawn, min=-most, max=most).astype(kind)


def setup_inputs(seed: int = 0) -> dict:
    seeds = jax.random.split(jax.random.key(seed), 7)
    return {
        "patterns": scatter_about(seeds[0], (MICRO, PATTERNS, NPIX), 1.0, 6.0, ((0, 4), (2, 8))),
        "detector_gain": jnp.clip(1.0 + 0.18 * jax.random.normal(seeds[1], (NPIX,), jnp.float32), 0.1, 1.9),
        "background": scatter_about(seeds[2], (NPIX,), 1.0, 6.0, ((0, 8),), jnp.float32),
        "bin_map": draw_bin_map(jax.random.fold_in(seeds[6], 71), 0),
        "templates": scatter_about(seeds[4], (TEMPLATES, RAD * ANG), (RAD * ANG) ** -0.5, 0.0546875, ((0, 32),)),
        "best_picks": plant(ranked_ids(seeds[5], (MICRO, PATTERNS), TEMPLATES, 2), jax.random.fold_in(seeds[5], 3), 0, TEMPLATES - 1).astype(jnp.int32),
    }


EPS = 1e-06

def reference(patterns, detector_gain, background, bin_map, templates, best_picks):

    def one_batch(inputs):
        frames, wanted = inputs
        corrected = ((frames.astype(jnp.float32) - background) * detector_gain).astype(jnp.bfloat16)
        bins = jax.ops.segment_sum(corrected.astype(jnp.float32).T, bin_map, num_segments=RAD * ANG)
        squares = lax.optimization_barrier(jnp.sum(bins * bins, axis=0))
        features = (bins * lax.rsqrt(squares / (RAD * ANG) + EPS)).astype(jnp.bfloat16)
        scores = jnp.dot(features.T, templates.T, preferred_element_type=jnp.float32)
        best = lax.top_k(scores, TOPK)[0]
        chosen = jnp.take(templates, wanted, axis=0).reshape(PATTERNS, RAD, ANG).astype(jnp.float32)
        grid = features.reshape(RAD, ANG, PATTERNS).astype(jnp.float32)
        columns = [jnp.einsum('rap,pra->p', grid, jnp.roll(chosen, -offset, axis=2)) for offset in range(-REACH, REACH + 1)]
        return (best, jnp.stack(columns, axis=1))
    best, refined = lax.map(one_batch, (patterns, best_picks))
    return (best, refined)
```

```python
import functools

import jax
import jax.numpy as jnp
from jax import lax
from jax.experimental import pallas as pl
from jax.experimental.pallas import tpu as pltpu
from jax.sharding import PartitionSpec as P

RAD = 64
ANG = 192
TOPK = 8
REACH = 1


EPS = 1e-06
BLOCK_ROWS = 512


def shifted(x, axis, by):
    count = lax.axis_size(axis)
    return lax.ppermute(x, axis, [(i, (i + by) % count) for i in range(count)])


def merged_2(part, axis, combine):
    gathered = lax.all_gather(part, axis)

    def take(source):
        return lax.dynamic_index_in_dim(gathered, source, 0, False)

    return lax.fori_loop(
        1, lax.axis_size(axis), lambda source, state: combine(state, take(source)), take(0)
    )


def bin_block(corrected, bin_map, first, length):
    targets = first + lax.iota(jnp.int32, length)
    onehot = (bin_map[None, :] == targets[:, None]).astype(jnp.bfloat16)
    return lax.dot_general(
        onehot, corrected, (((1,), (1,)), ((), ())), preferred_element_type=jnp.float32
    )


def bin_rows(corrected, bin_map, length):
    blocks = 1
    while length // blocks > BLOCK_ROWS and length % (2 * blocks) == 0:
        blocks = blocks * 2
    height = length // blocks
    starts = height * lax.iota(jnp.int32, blocks)
    stacked = lax.map(lambda begin: bin_block(corrected, bin_map, begin, height), starts)
    return stacked.reshape(length, corrected.shape[0])


def merge_best(first_best, second_best):
    return lax.top_k(jnp.concatenate([first_best, second_best], axis=-1), TOPK)[0]


def score_batch(features, templates, wanted, group_base):
    scores = lax.dot_general(
        features, templates, (((0,), (1,)), ((), ())), preferred_element_type=jnp.float32
    )
    best = lax.top_k(scores, TOPK)[0]
    local = wanted - group_base
    count = templates.shape[0]
    owned = (local >= 0) & (local < count)
    chosen = jnp.take(templates, jnp.clip(local, 0, count - 1), axis=0)
    width = features.shape[1]
    chosen = chosen.reshape(width, RAD, ANG)
    grid = features.T.reshape(width, RAD, ANG)
    columns = []
    for offset in range(-REACH, REACH + 1):
        rolled = jnp.roll(chosen, -offset, axis=2)
        columns.append(jnp.sum(grid.astype(jnp.float32) * rolled.astype(jnp.float32), axis=(1, 2)))
    refined = jnp.where(owned[:, None], jnp.stack(columns, axis=1), 0.0)
    return (best, refined)


def dense_body(patterns, detector_gain, background, bin_map, templates, best_picks):
    sections = lax.axis_size("section")
    orients = lax.axis_size("orient")
    section_index = lax.axis_index("section")
    orient_index = lax.axis_index("orient")
    features_total = RAD * ANG
    corrected = ((patterns[0].astype(jnp.float32) - background) * detector_gain).astype(
        jnp.bfloat16
    )
    whole = lax.psum(bin_rows(corrected, bin_map, features_total), "orient")
    squares = jnp.sum(whole * whole, axis=0)
    features = (whole * lax.rsqrt(squares / features_total + EPS)).astype(jnp.bfloat16)
    group_base = (section_index * orients + orient_index) * templates.shape[0]
    held = features
    running_best = None
    running_refined = None
    for turn in range(sections):
        batch = (section_index + sections - turn) % sections
        wanted = lax.dynamic_index_in_dim(best_picks, batch, 0, keepdims=False)
        best, refined = score_batch(held, templates, wanted, group_base)
        if turn > 0:
            best = merge_best(running_best, best)
            refined = running_refined + refined
        packed = shifted(jnp.concatenate([best, refined], axis=1), "section", 1)
        running_best = packed[:, :TOPK]
        running_refined = packed[:, TOPK:]
        if turn + 1 < sections:
            held = shifted(held, "section", 1)
    merged = merged_2(running_best, "orient", merge_best)
    shares = lax.psum_scatter(running_refined, "orient", scatter_dimension=0, tiled=True)
    return (merged[None], shares[None])


BINS = RAD * ANG
SEG = 1792
SEGS = 6
ROOM = 2 * SEG
TILE = 256
WINDOW = 256
KEPT = 32
PAIR = 2 * ANG
MIB = 1 << 20
F32 = jnp.float32
BF16 = jnp.bfloat16


def vmem():
    return pl.BlockSpec(memory_space=pltpu.VMEM)


def smem():
    return pl.BlockSpec(memory_space=pltpu.SMEM)


def dot_nt(a, b):
    return lax.dot_general(a, b, (((1,), (1,)), ((), ())), preferred_element_type=F32)


def dot_nn(a, b):
    return lax.dot_general(a, b, (((1,), (0,)), ((), ())), preferred_element_type=F32)


def polar(row):
    value = row.astype(F32)
    radial = jnp.floor((value + 0.5) * (1.0 / ANG))
    return radial, value - radial * ANG


def members(values, count):
    ids = lax.broadcasted_iota(jnp.int32, (count, values.shape[1]), 0).astype(F32)
    return ids == values


def presence_kernel(bins_ref, counts_ref):
    counts = jnp.zeros((ANG, RAD), F32)
    for tile in range(bins_ref.shape[0]):
        radial, angle = polar(bins_ref[tile : tile + 1, :])
        counts += dot_nt(
            members(angle, ANG).astype(BF16), members(radial, RAD).astype(BF16)
        )
    counts_ref[...] = (counts > 0.5).astype(F32)


def below(size):
    rows = lax.broadcasted_iota(jnp.int32, (size, size), 0)
    cols = lax.broadcasted_iota(jnp.int32, (size, size), 1)
    return rows, cols


def slots_kernel(own_ref, other_ref, bins_ref, table_ref, rows_ref, span_ref):
    present = jnp.maximum(own_ref[...], other_ref[...])
    held = present.astype(BF16)
    rows, cols = below(ANG)
    within = dot_nn((cols < rows).astype(BF16), held)
    totals = dot_nn(jnp.ones((ANG, ANG), BF16), held)
    rows, cols = below(RAD)
    before = dot_nn(totals.astype(BF16), (rows < cols).astype(BF16))
    slots = within + before
    high = jnp.floor(slots * (1.0 / 64))
    low = slots - 64 * high
    high = high.astype(BF16)
    low = low.astype(BF16)
    eye = (rows == cols).astype(BF16)
    turned = 64 * dot_nt(eye, high) + dot_nt(eye, low)
    table_ref[...] = jnp.where(dot_nt(eye, held) > 0.5, turned, -1.0).astype(jnp.int32)
    for tile in range(bins_ref.shape[0]):
        radial, angle = polar(bins_ref[tile : tile + 1, :])
        ring = members(radial, RAD).astype(BF16)
        value = 64 * dot_nn(high, ring) + dot_nn(low, ring)
        value = jnp.sum(jnp.where(members(angle, ANG), value, 0.0), axis=0, keepdims=True)
        rows_ref[tile : tile + 1, :] = value.astype(jnp.int32)
    found = rows_ref[...]
    first = jnp.min(found, axis=1, keepdims=True)
    last = jnp.max(found, axis=1, keepdims=True)
    lane = lax.broadcasted_iota(jnp.int32, (found.shape[0], 128), 1)
    span_ref[...] = jnp.where(lane == 0, first, last)


def binning_kernel(core_ref, span_ref, rows_ref, pixels_ref, mine_ref, theirs_ref, sums, turned):
    sums[...] = jnp.zeros_like(sums)
    across = 256 // 16

    def one_tile(tile, _):
        down = (tile // across) * 16
        right = (tile % across) * 16
        block = pixels_ref[pl.ds(down, 16), pl.ds(right, 16), :].reshape(TILE, 128)
        row = rows_ref[pl.ds(tile, 1), :]
        base = jnp.minimum(span_ref[tile, 0], ROOM) // 8 * 8
        stop = jnp.minimum(span_ref[tile, 1] + 1, ROOM)

        def one_window(step, _):
            at = pl.multiple_of(base + step * WINDOW, 8)
            ids = lax.broadcasted_iota(jnp.int32, (WINDOW, TILE), 0) + at
            hits = (ids == row).astype(BF16)
            sums[pl.ds(at, WINDOW), :] += dot_nn(hits, block)
            return 0

        lax.fori_loop(0, (stop - base + WINDOW - 1) // WINDOW, one_window, 0)
        return 0

    lax.fori_loop(0, rows_ref.shape[0], one_tile, 0)
    for block in range(ROOM // 128):
        turned[:, block * 128 : (block + 1) * 128] = sums[
            block * 128 : (block + 1) * 128, :
        ].T
    core = core_ref[0]
    half = turned.shape[0] // 2
    mine_ref[...] = turned[pl.ds(pl.multiple_of(core * half, half), half), :]
    theirs_ref[...] = turned[
        pl.ds(pl.multiple_of((1 - core) * half, half), half), :
    ].astype(BF16)


def columns_kernel(first, count, range_ref, table_ref, templates_ref, turned_ref, out_ref):
    rows = templates_ref.shape[0]
    extra = turned_ref.shape[0]
    for seg in range(count):
        offset = 0 if first + seg < 4 else SEG

        def one_window(window, _):
            at = offset + window * 256

            def one_pair(pair, total):
                main, side = total
                col = pl.multiple_of(pair * PAIR, 128)
                row = table_ref[first + seg, pl.ds(pair, 1), :]
                ids = lax.broadcasted_iota(jnp.int32, (256, PAIR), 0) + at
                hits = (ids == row).astype(BF16)
                main = main + dot_nt(templates_ref[:, pl.ds(col, PAIR)], hits)
                side = side + dot_nt(turned_ref[:, pl.ds(col, PAIR)], hits)
                return main, side

            main, side = lax.fori_loop(
                range_ref[first + seg, 2 * window],
                range_ref[first + seg, 2 * window + 1],
                one_pair,
                (jnp.zeros((rows, 256), F32), jnp.zeros((extra, 256), F32)),
            )
            to = pl.multiple_of(window * 256, 256)
            out_ref[seg, :rows, pl.ds(to, 256)] = main.astype(BF16)
            out_ref[seg, rows:, pl.ds(to, 256)] = side.astype(BF16)
            return 0

        lax.fori_loop(0, SEG // 256, one_window, 0)


def columns(first, count, ranges, tables, templates, turned):
    height = templates.shape[0] + turned.shape[0]
    return pl.pallas_call(
        functools.partial(columns_kernel, first, count),
        out_shape=jax.ShapeDtypeStruct((count, height, SEG), BF16),
        in_specs=[smem(), vmem(), vmem(), vmem()],
        out_specs=vmem(),
        compiler_params=pltpu.CompilerParams(vmem_limit_bytes=48 * MIB),
        name="columns",
    )(ranges, tables, templates, turned)


def squares_kernel(place_ref, base_ref, start_ref, table_ref, *refs):
    lists, out_ref = refs[:-1], refs[-1]
    share = table_ref.shape[1] // 4
    total = jnp.zeros((8, 64), F32)

    def one_pair(step, total):
        pair = place_ref[0] * share + step
        dense = jnp.zeros((64, PAIR), F32)
        for seg in range(SEGS):
            ref, index = lists[seg // 2], seg % 2
            offset = 0 if seg < 4 else SEG
            row = table_ref[seg, pl.ds(pair, 1), :]
            width = 512
            at = pl.multiple_of(start_ref[seg, pair], 128)
            ids = lax.broadcasted_iota(jnp.int32, (width, PAIR), 0) + at + offset
            hits = (ids == row).astype(BF16)
            dense = dense + dot_nn(ref[index, :, pl.ds(at, width)], hits)
        square = dense * dense
        high = square.astype(BF16)
        low = (square - high.astype(F32)).astype(BF16)
        ones = jnp.ones((8, PAIR), BF16)
        return total + dot_nt(ones, high) + dot_nt(ones, low)

    out_ref[...] = lax.fori_loop(0, share, one_pair, total)


def insert_sorted(best, value):
    out = []
    for held in best:
        out.append(jnp.maximum(held, value))
        value = jnp.minimum(held, value)
    return out


def merge_sorted(first, second):
    count = len(first)
    both = [jnp.maximum(first[i], second[count - 1 - i]) for i in range(count)]
    gap = count // 2
    while gap:
        for i in range(count):
            if i & gap == 0:
                high = jnp.maximum(both[i], both[i + gap])
                low = jnp.minimum(both[i], both[i + gap])
                both[i], both[i + gap] = high, low
        gap //= 2
    return both


def score_kernel(first, last, rows, *refs):
    count = 0 if first else 1
    own_ref, pair_ref, z_ref, x_ref, y_ref, d_ref, e_ref = refs[:7]
    rest = refs[7:]
    if not first:
        so_far_ref, rest = rest[0], rest[1:]
    if last:
        local_ref, rank_ref, out_ref, total, lists = rest
    else:
        out_ref, lists = rest
        total = out_ref
    half = z_ref.shape[1]
    for seg in range(z_ref.shape[0]):
        lists[0:half, :] = z_ref[seg]
        lists[half : 2 * half, :] = x_ref[seg]
        lists[2 * half : 3 * half, :] = y_ref[seg]
        lists[3 * half : 3 * half + half // 2, :] = d_ref[seg]
        lists[3 * half + half // 2 :, :] = e_ref[seg]
        for side, ref in enumerate((own_ref, pair_ref)):
            term = dot_nt(ref[seg], lists[...])
            if seg == 0 and first:
                total[side] = term
            elif seg == 0:
                total[side] = so_far_ref[side] + term
            else:
                total[side] = total[side] + term
    if not last:
        return
    width = total.shape[2]
    low = jnp.full((8, width), -jnp.inf, F32)
    best = [low] * TOPK
    for side in range(2):
        def step(at, best):
            return tuple(
                insert_sorted(best, total[side, pl.ds(pl.multiple_of(at * 8, 8), 8), :])
            )

        best = lax.fori_loop(0, rows // 8, step, tuple(best), unroll=2)
    for turn in (4, 2, 1):
        best = merge_sorted(best, [pltpu.roll(part, turn, 0) for part in best])
    for place in range(TOPK):
        out_ref[place : place + 1, :] = best[place][0:1, :]
    picked = [jnp.zeros((1, width), F32) for _ in range(3)]
    for side in range(2):
        ids = lax.broadcasted_iota(jnp.int32, (rows, width), 0)
        picked[1] += jnp.sum(
            jnp.where(ids == local_ref[side : side + 1, :], total[side, :rows, :], 0.0),
            axis=0,
            keepdims=True,
        )
        ids = lax.broadcasted_iota(jnp.int32, (KEPT, width), 0)
        hit = ids == rank_ref[side : side + 1, :]
        picked[0] += jnp.sum(
            jnp.where(hit, total[side, rows : rows + KEPT, :], 0.0), axis=0, keepdims=True
        )
        picked[2] += jnp.sum(
            jnp.where(hit, total[side, rows + KEPT :, :], 0.0), axis=0, keepdims=True
        )
    for place in range(3):
        out_ref[TOPK + place : TOPK + place + 1, :] = picked[place]
    out_ref[TOPK + 3 :, :] = jnp.zeros((16 - TOPK - 3, width), F32)


def score(first, last, rows, own, pair, lists, so_far, extra):
    height = own.shape[1]
    width = 4 * lists[0].shape[1]
    scratch = [pltpu.VMEM((width, SEG), BF16)]
    if last:
        scratch = [pltpu.VMEM((2, height, width), F32)] + scratch
        shape = (16, width)
    else:
        shape = (2, height, width)
    args = [own, pair, *lists]
    if not first:
        args.append(so_far)
    args.extend(extra)
    return pl.pallas_call(
        functools.partial(score_kernel, first, last, rows),
        out_shape=jax.ShapeDtypeStruct(shape, F32),
        in_specs=[vmem()] * len(args),
        out_specs=vmem(),
        scratch_shapes=scratch,
        compiler_params=pltpu.CompilerParams(vmem_limit_bytes=48 * MIB),
        name="score",
    )(*args)


def merge_kernel(scale, *refs):
    parts, out_ref = refs[:-1], refs[-1]
    best = None
    for ref in parts:
        rows = [ref[place : place + 1, :] for place in range(TOPK)]
        best = rows if best is None else merge_sorted(best, rows)
    rest = (parts[0][TOPK:, :] + parts[2][TOPK:, :]) + (
        parts[1][TOPK:, :] + parts[3][TOPK:, :]
    )
    factor = lax.rsqrt(rest[3:4, :] / BINS + EPS) if scale else 1.0
    for place in range(TOPK):
        out_ref[place : place + 1, :] = best[place] * factor
    out_ref[TOPK:, :] = rest * factor


def merge(scale, parts):
    return pl.pallas_call(
        functools.partial(merge_kernel, scale),
        out_shape=jax.ShapeDtypeStruct(parts[0].shape, F32),
        in_specs=[vmem()] * len(parts),
        out_specs=vmem(),
        name="merge",
    )(*parts)


def compact_body(patterns, detector_gain, background, bin_map, templates, best_picks):
    orients = lax.axis_size("orient")
    chips = orients // 2
    section = lax.axis_index("section")
    orient = lax.axis_index("orient")
    core = orient % 2
    chip = orient // 2
    rows = templates.shape[0]
    count = patterns.shape[1]
    half = count // 2
    pixels = patterns.shape[2]

    def swap(x):
        return lax.ppermute(x, "orient", [(i, i ^ 1) for i in range(orients)])

    def along(x, by):
        return lax.ppermute(x, "orient", [(i, (i + 2 * by) % orients) for i in range(orients)])

    def hops(x, pairs):
        return lax.ppermute(
            x, "orient", [(2 * i + c, 2 * j + c) for i, j in pairs for c in range(2)]
        )

    def across(x, by):
        return lax.ppermute(x, "section", [(i, i ^ by) for i in range(4)])

    tiles = pixels // TILE
    bins = bin_map.reshape(tiles // 16, 16, 16, 16).transpose(0, 2, 1, 3).reshape(tiles, TILE)
    present = pl.pallas_call(
        presence_kernel,
        out_shape=jax.ShapeDtypeStruct((ANG, RAD), F32),
        in_specs=[vmem()],
        out_specs=vmem(),
        name="presence",
    )(bins)
    other = swap(present)
    corrected = ((patterns[0].astype(F32) - background) * detector_gain).astype(BF16)
    corrected = corrected.T.reshape(tiles, TILE, count)
    table, slot_rows, span = pl.pallas_call(
        slots_kernel,
        out_shape=(
            jax.ShapeDtypeStruct((RAD, ANG), jnp.int32),
            jax.ShapeDtypeStruct((tiles, TILE), jnp.int32),
            jax.ShapeDtypeStruct((tiles, 128), jnp.int32),
        ),
        in_specs=[vmem()] * 3,
        out_specs=(vmem(),) * 3,
        name="slots",
    )(present, other, bins)
    mine, theirs = pl.pallas_call(
        binning_kernel,
        out_shape=(
            jax.ShapeDtypeStruct((half, ROOM), F32),
            jax.ShapeDtypeStruct((half, ROOM), BF16),
        ),
        in_specs=[smem(), smem(), vmem(), vmem()],
        out_specs=(vmem(), vmem()),
        scratch_shapes=[pltpu.VMEM((ROOM + WINDOW, count), F32), pltpu.VMEM((count, ROOM), F32)],
        compiler_params=pltpu.CompilerParams(vmem_limit_bytes=24 * MIB),
        name="binning",
    )(core.reshape(1).astype(jnp.int32), span, slot_rows, corrected)
    received = swap(theirs)
    summed = (mine + received.astype(F32)).astype(BF16)
    base = summed[:, :SEG]
    spare = summed[:, SEG:]

    table = table.reshape(RAD // 2, PAIR)
    tables = jnp.stack([table] + [along(table, by) for by in range(1, chips)])
    near = jnp.where(chip < 2, (chip - 1) % chips, (chip - 2) % chips)
    far = jnp.where(chip < 2, (chip - 2) % chips, (chip - 1) % chips)
    tables = jnp.concatenate(
        [
            tables,
            lax.dynamic_index_in_dim(tables, near, 0),
            lax.dynamic_index_in_dim(tables, far, 0),
        ]
    )
    valid = jnp.sum((tables >= 0).astype(jnp.int32), axis=2)
    ends = jnp.cumsum(valid, axis=1)
    begins = ends - valid
    offsets = jnp.array([0] * 4 + [SEG] * 2, jnp.int32)
    at = offsets[:, None] + 256 * lax.iota(jnp.int32, SEG // 256)[None, :]
    low = jnp.sum((ends[:, None, :] <= at[:, :, None]).astype(jnp.int32), axis=2)
    high = jnp.sum((begins[:, None, :] < at[:, :, None] + 256).astype(jnp.int32), axis=2)
    ranges = jnp.stack([low, high], axis=2).reshape(SEGS, -1)
    starts = jnp.clip((begins - offsets[:, None]) // 128 * 128, 0, SEG - 512)
    held_chip = (chip - lax.iota(jnp.int32, chips)) % chips
    room = jnp.where((held_chip == 1) | (held_chip == 2), ROOM, SEG)
    crowded = jnp.any(ends[:chips, -1] > room)

    picks = best_picks.reshape(-1)
    owner = picks // rows
    ids = lax.iota(jnp.int32, picks.shape[0])
    earlier = ids[:, None] < ids[None, :]
    first = ~jnp.any(earlier & (picks[:, None] == picks[None, :]), axis=0)
    rank = jnp.sum(
        (earlier & first[:, None] & (owner[:, None] == owner[None, :])).astype(jnp.int32), axis=0
    )
    crowded = crowded | jnp.any(first & (rank >= KEPT))
    me = section * orients + orient
    chosen = first & (owner == me)
    wanted = jnp.sum(
        jnp.where(
            chosen[None, :] & (rank[None, :] == lax.iota(jnp.int32, KEPT)[:, None]),
            (picks - me * rows)[None, :] + 1,
            0,
        ),
        axis=1,
    )
    select = (wanted[:, None] - 1 == lax.iota(jnp.int32, rows)[None, :]).astype(BF16)
    taken = lax.dot_general(
        select, templates, (((1,), (0,)), ((), ())), preferred_element_type=BF16
    ).reshape(KEPT, RAD, ANG)
    turned = jnp.concatenate([jnp.roll(taken, 1, axis=2), jnp.roll(taken, -1, axis=2)])
    turned = turned.reshape(2 * KEPT, BINS)
    first_rank = jnp.sum(
        jnp.where(first[:, None] & (picks[:, None] == picks[None, :]), rank[:, None], 0), axis=0
    )
    order = [section ^ by for by in range(4)]

    def arranged(values):
        values = values.reshape(best_picks.shape)
        return jnp.concatenate(
            [lax.dynamic_slice(values, (s, core * half), (1, half))[0] for s in order]
        )

    picks_here = arranged(picks)
    rank_here = arranged(first_rank)
    bases = jnp.stack([me * rows, (section * orients + (orient ^ 1)) * rows])
    local = picks_here[None, :] - bases[:, None]
    held = (local >= 0) & (local < rows)
    local = jnp.where(held, local, -1)
    ranks = jnp.where(held, rank_here[None, :], -1)

    bases_z = [base] + [along(base, by) for by in range(1, chips)]
    step = hops(spare, [(1, 0), (2, 3)])
    inner = (chip == 1) | (chip == 2)
    traded = hops(spare, [(1, 2), (2, 1)])
    far_part = hops(spare, [(1, 3), (2, 0)])
    spare_near = jnp.where(inner, spare, step)
    spare_far = jnp.where(inner, traded, far_part)
    groups = [
        jnp.stack([bases_z[0], bases_z[1]]),
        jnp.stack([bases_z[2], bases_z[3]]),
        jnp.stack([spare_near, spare_far]),
    ]
    lists = []
    for group in groups:
        x = across(group, 1)
        y = across(group, 2)
        d = across(x[:, : half // 2], 2)
        e = across(y[:, half // 2 :], 1)
        lists.append((group, x, y, d, e))

    own = [columns(2 * i, 2, ranges, tables, templates, turned) for i in range(3)]
    pair = [swap(part) for part in own]
    squares = pl.pallas_call(
        squares_kernel,
        out_shape=jax.ShapeDtypeStruct((8, half), F32),
        in_specs=[smem(), smem(), smem(), vmem()] + [vmem()] * 3,
        out_specs=vmem(),
        name="squares",
    )(
        chip.reshape(1).astype(jnp.int32),
        offsets,
        starts,
        tables,
        *groups,
    )
    total = score(True, False, rows, own[0], pair[0], lists[0], None, ())
    total = score(False, False, rows, own[1], pair[1], lists[1], total, ())
    pack = score(False, True, rows, own[2], pair[2], lists[2], total, (local, ranks))
    parts = [pack[:, :half]]
    for by in range(1, 4):
        parts.append(across(pack[:, by * half : (by + 1) * half], by))
    part = merge(False, parts)
    part = lax.dynamic_update_slice(part, squares[:1], (TOPK + 3, 0))
    part = merge(True, [part] + [along(part, by) for by in range(1, chips)])
    partner = swap(part)
    both = jnp.where(
        core == 0,
        jnp.concatenate([part, partner], axis=1),
        jnp.concatenate([partner, part], axis=1),
    ).T
    mine_rows = lax.dynamic_slice(both, (orient * (count // orients), TOPK), (count // orients, 3))
    sparse = (both[None, :, :TOPK], mine_rows[None])
    return lax.cond(
        crowded,
        lambda: dense_body(
            patterns, detector_gain, background, bin_map, templates, best_picks
        ),
        lambda: sparse,
    )


def solution(mesh):
    sizes = dict(mesh.shape)
    fits = sizes["section"] == 4 and sizes["orient"] == 8
    return jax.shard_map(
        compact_body if fits else dense_body,
        mesh=mesh,
        in_specs=(
            P("section", None, "orient"),
            P("orient"),
            P("orient"),
            P("orient"),
            P(("section", "orient"), None),
            P(),
        ),
        out_specs=(P("section", None, None), P("section", "orient", None)),
        check_vma=False,
    )
```

```python
import functools

import jax
import jax.numpy as jnp
from jax import lax
from jax.experimental import pallas as pl
from jax.experimental.pallas import tpu as pltpu
from jax.sharding import PartitionSpec as P

RAD = 64
ANG = 192
TOPK = 8
REACH = 1


EPS = 1e-06
BLOCK_ROWS = 512


def shifted(x, axis, by):
    count = lax.axis_size(axis)
    return lax.ppermute(x, axis, [(i, (i + by) % count) for i in range(count)])


def merged_2(part, axis, combine):
    gathered = lax.all_gather(part, axis)

    def take(source):
        return lax.dynamic_index_in_dim(gathered, source, 0, False)

    return lax.fori_loop(
        1, lax.axis_size(axis), lambda source, state: combine(state, take(source)), take(0)
    )


def bin_block(corrected, bin_map, first, length):
    targets = first + lax.iota(jnp.int32, length)
    onehot = (bin_map[None, :] == targets[:, None]).astype(jnp.bfloat16)
    return lax.dot_general(
        onehot, corrected, (((1,), (1,)), ((), ())), preferred_element_type=jnp.float32
    )


def bin_rows(corrected, bin_map, length):
    blocks = 1
    while length // blocks > BLOCK_ROWS and length % (2 * blocks) == 0:
        blocks = blocks * 2
    height = length // blocks
    starts = height * lax.iota(jnp.int32, blocks)
    stacked = lax.map(lambda begin: bin_block(corrected, bin_map, begin, height), starts)
    return stacked.reshape(length, corrected.shape[0])


def merge_best(first_best, second_best):
    return lax.top_k(jnp.concatenate([first_best, second_best], axis=-1), TOPK)[0]


def score_batch(features, templates, wanted, group_base):
    scores = lax.dot_general(
        features, templates, (((0,), (1,)), ((), ())), preferred_element_type=jnp.float32
    )
    best = lax.top_k(scores, TOPK)[0]
    local = wanted - group_base
    count = templates.shape[0]
    owned = (local >= 0) & (local < count)
    chosen = jnp.take(templates, jnp.clip(local, 0, count - 1), axis=0)
    width = features.shape[1]
    chosen = chosen.reshape(width, RAD, ANG)
    grid = features.T.reshape(width, RAD, ANG)
    columns = []
    for offset in range(-REACH, REACH + 1):
        rolled = jnp.roll(chosen, -offset, axis=2)
        columns.append(jnp.sum(grid.astype(jnp.float32) * rolled.astype(jnp.float32), axis=(1, 2)))
    refined = jnp.where(owned[:, None], jnp.stack(columns, axis=1), 0.0)
    return (best, refined)


def dense_body(patterns, detector_gain, background, bin_map, templates, best_picks):
    sections = lax.axis_size("section")
    orients = lax.axis_size("orient")
    section_index = lax.axis_index("section")
    orient_index = lax.axis_index("orient")
    features_total = RAD * ANG
    corrected = ((patterns[0].astype(jnp.float32) - background) * detector_gain).astype(
        jnp.bfloat16
    )
    whole = lax.psum(bin_rows(corrected, bin_map, features_total), "orient")
    squares = jnp.sum(whole * whole, axis=0)
    features = (whole * lax.rsqrt(squares / features_total + EPS)).astype(jnp.bfloat16)
    group_base = (section_index * orients + orient_index) * templates.shape[0]
    held = features
    running_best = None
    running_refined = None
    for turn in range(sections):
        batch = (section_index + sections - turn) % sections
        wanted = lax.dynamic_index_in_dim(best_picks, batch, 0, keepdims=False)
        best, refined = score_batch(held, templates, wanted, group_base)
        if turn > 0:
            best = merge_best(running_best, best)
            refined = running_refined + refined
        packed = shifted(jnp.concatenate([best, refined], axis=1), "section", 1)
        running_best = packed[:, :TOPK]
        running_refined = packed[:, TOPK:]
        if turn + 1 < sections:
            held = shifted(held, "section", 1)
    merged = merged_2(running_best, "orient", merge_best)
    shares = lax.psum_scatter(running_refined, "orient", scatter_dimension=0, tiled=True)
    return (merged[None], shares[None])


BINS = RAD * ANG
SEG = 1792
SEGS = 6
ROOM = 2 * SEG
TILE = 256
WINDOW = 512
GROUPS = ((0,), (1, 3, 4), (2, 5))
KEPT = 32
GRANT = 24
PAIR = 2 * ANG
MIB = 1 << 20
F32 = jnp.float32
BF16 = jnp.bfloat16


def vmem():
    return pl.BlockSpec(memory_space=pltpu.VMEM)


def smem():
    return pl.BlockSpec(memory_space=pltpu.SMEM)


def anywhere():
    return pl.BlockSpec(memory_space=pl.ANY)


def cost(micros):
    return pl.CostEstimate(
        flops=int(micros * 1e10), bytes_accessed=int(micros * 1e6), transcendentals=0
    )


def dot_nt(a, b):
    return lax.dot_general(a, b, (((1,), (1,)), ((), ())), preferred_element_type=F32)


def dot_nn(a, b):
    return lax.dot_general(a, b, (((1,), (0,)), ((), ())), preferred_element_type=F32)


def polar(row):
    value = row.astype(F32)
    radial = jnp.floor((value + 0.5) * (1.0 / ANG))
    return radial, value - radial * ANG


def members(values, count):
    ids = lax.broadcasted_iota(jnp.int32, (count, values.shape[1]), 0).astype(F32)
    return ids == values


def presence_kernel(bins_ref, counts_ref):
    counts = jnp.zeros((ANG, RAD), F32)
    for tile in range(bins_ref.shape[0]):
        radial, angle = polar(bins_ref[tile : tile + 1, :])
        counts += dot_nt(
            members(angle, ANG).astype(BF16), members(radial, RAD).astype(BF16)
        )
    counts_ref[...] = (counts > 0.5).astype(F32)


def below(size):
    rows = lax.broadcasted_iota(jnp.int32, (size, size), 0)
    cols = lax.broadcasted_iota(jnp.int32, (size, size), 1)
    return rows, cols


def edges(table, offset):
    pairs = table.shape[0]
    valid = (table >= 0).astype(F32).astype(BF16)
    count = dot_nn(valid, jnp.ones((PAIR, 128), BF16))
    rows, cols = below(pairs)
    low_end = count - 256 * jnp.floor(count * (1.0 / 256))
    high_end = jnp.floor(count * (1.0 / 256))
    sums = (cols <= rows).astype(BF16)
    ends = 256 * dot_nn(sums, high_end.astype(BF16)) + dot_nn(sums, low_end.astype(BF16))
    begins = ends - count
    lane = lax.broadcasted_iota(jnp.int32, count.shape, 1)
    wide = SEG // 256
    first = jnp.clip(jnp.floor((begins - offset) * (1.0 / 256)), 0, wide)
    last = jnp.clip(jnp.floor((ends - offset + 255) * (1.0 / 256)), 0, wide)
    windows = jnp.where(lane == 0, first, jnp.where(count > 0, last, 0.0))
    at = (lane % 64).astype(F32) * 256 + offset
    found = jnp.where(lane < 64, (ends <= at).astype(F32), (begins < at + 256).astype(F32))
    ranges = jnp.sum(found, axis=0, keepdims=True)
    ranges = jnp.where(lane[:1] == 127, ends[pairs - 1 :], ranges)
    return windows.astype(jnp.int32), ranges.astype(jnp.int32), ends


def slots_kernel(own_ref, other_ref, bins_ref, table_ref, rows_ref, span_ref, range_ref, window_ref):
    present = jnp.maximum(own_ref[...], other_ref[...])
    held = present.astype(BF16)
    rows, cols = below(ANG)
    within = dot_nn((cols < rows).astype(BF16), held)
    totals = dot_nn(jnp.ones((ANG, ANG), BF16), held)
    rows, cols = below(RAD)
    before = dot_nn(totals.astype(BF16), (rows < cols).astype(BF16))
    slots = within + before
    high = jnp.floor(slots * (1.0 / 64))
    low = slots - 64 * high
    high = high.astype(BF16)
    low = low.astype(BF16)
    both = jnp.concatenate([high, low])
    line = lax.broadcasted_iota(jnp.int32, (RAD // 2, RAD), 0)
    ring = lax.broadcasted_iota(jnp.int32, (RAD // 2, RAD), 1)
    for side in range(2):
        pick = (ring == 2 * line + side).astype(BF16)
        turned = 64 * dot_nt(pick, high) + dot_nt(pick, low)
        table_ref[:, side * ANG : (side + 1) * ANG] = jnp.where(
            dot_nt(pick, held) > 0.5, turned, -1.0
        ).astype(jnp.int32)
    own_windows, own_ranges, _ = edges(table_ref[...], 0)
    window_ref[0] = own_windows
    range_ref[...] = jnp.broadcast_to(own_ranges, range_ref.shape)
    for tile in range(bins_ref.shape[0]):
        radial, angle = polar(bins_ref[tile : tile + 1, :])
        ring = members(radial, RAD).astype(BF16)
        value = dot_nn(both, ring)
        value = 64 * value[:ANG] + value[ANG:]
        value = jnp.sum(jnp.where(members(angle, ANG), value, 0.0), axis=0, keepdims=True)
        rows_ref[tile : tile + 1, :] = value.astype(jnp.int32)
    found = rows_ref[...]
    first = jnp.min(found, axis=1, keepdims=True)
    last = jnp.max(found, axis=1, keepdims=True)
    lane = lax.broadcasted_iota(jnp.int32, (found.shape[0], 128), 1)
    span_ref[...] = jnp.where(lane == 0, first, last)


def pixels_kernel(patterns_ref, gain_ref, background_ref, out_ref):
    value = (patterns_ref[0].astype(F32) - background_ref[...]) * gain_ref[...]
    out_ref[...] = value.astype(BF16).T


def binning_kernel(
    core_ref, span_ref, rows_ref, pixels_ref, mine_ref, theirs_ref, sums, turned
):
    sums[...] = jnp.zeros_like(sums)
    across = 256 // 16

    def add(tile, at):
        down = (tile // across) * 16
        right = (tile % across) * 16
        block = pixels_ref[pl.ds(down, 16), pl.ds(right, 16), :].reshape(TILE, 128)
        row = rows_ref[pl.ds(tile, 1), :]
        ids = lax.broadcasted_iota(jnp.int32, (WINDOW, TILE), 0)
        hits = (ids == row - at).astype(BF16)
        sums[pl.ds(at, WINDOW), :] += dot_nn(hits, block)

    def base_of(tile):
        return pl.multiple_of(jnp.minimum(span_ref[tile, 0], ROOM) // 8 * 8, 8)

    tiles = rows_ref.shape[0]
    for tile in range(tiles):
        add(tile, base_of(tile))

    def one_tile(tile, _):
        base = base_of(tile)
        stop = jnp.minimum(span_ref[tile, 1] + 1, ROOM)

        def one_window(step, _):
            add(tile, pl.multiple_of(base + step * WINDOW, 8))
            return 0

        lax.fori_loop(1, (stop - base + WINDOW - 1) // WINDOW, one_window, 0)
        return 0

    lax.fori_loop(0, tiles, one_tile, 0)
    for block in range(ROOM // 128):
        turned[:, block * 128 : (block + 1) * 128] = sums[
            block * 128 : (block + 1) * 128, :
        ].T
    core = core_ref[0]
    half = turned.shape[0] // 2
    mine_ref[...] = turned[pl.ds(pl.multiple_of(core * half, half), half), :]
    theirs_ref[...] = turned[
        pl.ds(pl.multiple_of((1 - core) * half, half), half), :
    ].astype(BF16)


def combine_kernel(
    mine_ref, theirs_ref, table_ref, message_ref, base_ref, spare_ref
):
    total = (mine_ref[...] + theirs_ref[...].astype(F32)).astype(BF16)
    base_ref[0] = total[:, :SEG]
    spare_ref[...] = total[:, SEG:]
    message_ref[:, :SEG] = total[:, :SEG]
    table = table_ref[...].astype(F32)
    high = jnp.floor(table * (1.0 / 64))
    pairs = table.shape[0]
    message_ref[:pairs, SEG:] = high.astype(BF16)
    message_ref[pairs:, SEG:] = (table - 64 * high).astype(BF16)


def sum_rows(mask, value):
    return jnp.sum(jnp.where(mask, value, 0.0), axis=0, keepdims=True)


def sum_lanes(mask, value):
    return jnp.sum(jnp.where(mask, value, 0.0), axis=1, keepdims=True)


def place_picks(place_ref, row_ref, col_ref, rows, local_ref, rank_ref, crowd_ref):
    section, orient, orients = place_ref[0], place_ref[1], place_ref[2]
    row = row_ref[...].astype(F32)
    col = col_ref[...].astype(F32)
    size = row.shape[1]
    i = lax.broadcasted_iota(jnp.int32, (size, size), 0)
    j = lax.broadcasted_iota(jnp.int32, (size, size), 1)
    equal = col == row
    first_row = (sum_rows(equal & (i < j), 1.0) == 0).astype(F32)
    first_col = (sum_lanes(equal & (j < i), 1.0) == 0).astype(F32)
    owner_row = jnp.floor((row + 0.5) * (1.0 / rows))
    owner_col = jnp.floor((col + 0.5) * (1.0 / rows))
    same = owner_col == owner_row
    rank_row = sum_rows(same & (i < j), first_col)
    rank_col = sum_lanes(same & (j < i), first_row)
    rank_of = sum_rows(equal, first_col * rank_col)
    crowd_ref[...] = jnp.broadcast_to(
        jnp.max(rank_of, axis=1, keepdims=True), crowd_ref.shape
    ).astype(jnp.int32)
    me = section * orients + orient
    base = (me * rows).astype(F32)
    ids = lax.broadcasted_iota(jnp.int32, (KEPT, size), 0).astype(F32)
    chosen = (first_row > 0) & (owner_row == me.astype(F32)) & (rank_row == ids)
    wanted = sum_lanes(chosen, row - base + 1) - 1
    half = 64
    core = orient % 2
    local_ref[...] = jnp.zeros_like(local_ref)
    rank_ref[...] = jnp.zeros_like(rank_ref)
    lanes = lax.broadcasted_iota(jnp.int32, (1, size), 1)
    for by in range(4):
        start = (section ^ by) * 2 * half + core * half
        shift = (size - start) % size
        there = slice(by * half, (by + 1) * half)
        local_ref[2:3, there] = pltpu.roll(row, shift, 1)[:, :half].astype(jnp.int32)
        rank_ref[2:3, there] = pltpu.roll(rank_of, shift, 1)[:, :half].astype(jnp.int32)
    for side in range(2):
        owner = section * orients + (orient ^ side)
        local = local_ref[2:3, :] - owner * rows
        held = (local >= 0) & (local < rows)
        local_ref[side : side + 1, :] = jnp.where(held, local, -1)
        rank_ref[side : side + 1, :] = jnp.where(held, rank_ref[2:3, :], -1)
    return wanted


def turn_picks(wanted, templates_ref, out_ref):
    rows = templates_ref.shape[0]
    ids = lax.broadcasted_iota(jnp.int32, (KEPT, rows), 1).astype(F32)
    select = (ids == wanted).astype(BF16)
    lane = lax.broadcasted_iota(jnp.int32, (KEPT, PAIR), 1)
    for pair in range(RAD // 2):
        cols = slice(pair * PAIR, (pair + 1) * PAIR)
        taken = dot_nn(select, templates_ref[:, cols])
        later = jnp.where(
            lane % ANG == 0, pltpu.roll(taken, ANG + 1, 1), pltpu.roll(taken, 1, 1)
        )
        sooner = jnp.where(
            lane % ANG == ANG - 1,
            pltpu.roll(taken, ANG - 1, 1),
            pltpu.roll(taken, PAIR - 1, 1),
        )
        out_ref[:KEPT, cols] = later.astype(BF16)
        out_ref[KEPT:, cols] = sooner.astype(BF16)


def permute_columns(offsets, range_ref, table_ref, templates_ref, turned_ref, out_ref):
    wide = 4

    def block(pair, pairs):
        col = pl.ds(pl.multiple_of(pair * PAIR, 128), pairs * PAIR)
        return jnp.concatenate([templates_ref[:, col], turned_ref[:, col]], axis=0)

    def hits(seg, pair, at):
        row = table_ref[seg, pl.ds(pair, 1), :]
        ids = lax.broadcasted_iota(jnp.int32, (256, PAIR), 0)
        return (ids == row - at).astype(BF16)

    def start_of(seg, window):
        return jnp.minimum(range_ref[seg, window], RAD // 2 - wide)

    for seg, offset in enumerate(offsets):
        for window in range(SEG // 256):
            at = offset + window * 256
            start = start_of(seg, window)
            mask = jnp.concatenate([hits(seg, start + i, at) for i in range(wide)], axis=1)
            out_ref[seg, :, window * 256 : (window + 1) * 256] = dot_nt(
                block(start, wide), mask
            ).astype(BF16)

    for seg, offset in enumerate(offsets):

        def one_window(window, _):
            to = pl.ds(pl.multiple_of(window * 256, 256), 256)

            def one_pair(pair, _):
                more = dot_nt(block(pair, 1), hits(seg, pair, offset + window * 256))
                out_ref[seg, :, to] = (out_ref[seg, :, to].astype(F32) + more).astype(BF16)
                return 0

            lax.fori_loop(start_of(seg, window) + wide, range_ref[seg, 64 + window], one_pair, 0)
            return 0

        lax.fori_loop(0, SEG // 256, one_window, 0)


def first_kernel(
    place_ref, range_ref, table_ref, row_ref, col_ref, templates_ref, _,
    out_ref, turned_ref, local_ref, rank_ref, crowd_ref,
):
    rows = templates_ref.shape[0]
    wanted = place_picks(place_ref, row_ref, col_ref, rows, local_ref, rank_ref, crowd_ref)
    turn_picks(wanted, templates_ref, turned_ref)
    permute_columns((0,), range_ref, table_ref, templates_ref, turned_ref, out_ref)


def columns_kernel(offsets, range_ref, table_ref, templates_ref, turned_ref, *refs):
    permute_columns(offsets, range_ref, table_ref, templates_ref, turned_ref, refs[-1])


def columns(segs, ranges, tables, templates, turned, after):
    height = templates.shape[0] + turned.shape[0]
    offsets = tuple(0 if seg < 4 else SEG for seg in segs)
    return pl.pallas_call(
        functools.partial(columns_kernel, offsets),
        out_shape=jax.ShapeDtypeStruct((len(segs), height, SEG), BF16),
        in_specs=[smem(), vmem(), vmem(), vmem()] + [anywhere()] * len(after),
        out_specs=vmem(),
        compiler_params=pltpu.CompilerParams(vmem_limit_bytes=GRANT * MIB),
        cost_estimate=cost(5 * len(segs)),
        name="columns",
    )(ranges, tables, templates, turned, *after)


def arrive_kernel(first, chip_ref, held_ref, *refs):
    group_ref, table_ref, window_ref, range_ref = refs[-4:]
    messages = refs[:2] if first else refs[:1]
    mine_ref, came_ref = refs[len(messages) : len(messages) + 2]
    pairs = table_ref.shape[1]
    chip = chip_ref[0]
    inner = (chip == 1) | (chip == 2)
    for at, ref in enumerate(messages):
        group_ref[at] = ref[:, :SEG]
        high = ref[:pairs, SEG:].astype(F32)
        low = ref[pairs:, SEG:].astype(F32)
        table_ref[at] = (64 * high + low).astype(jnp.int32)
    last = len(messages)

    @pl.when(inner)
    def _():
        group_ref[last] = mine_ref[...]

    @pl.when(jnp.logical_not(inner))
    def _():
        group_ref[last] = came_ref[...]

    if first:
        table = jnp.where(chip == 0, table_ref[1], jnp.where(chip == 3, table_ref[0], held_ref[...]))
    else:
        table = jnp.where(chip == 1, held_ref[1], jnp.where(chip == 2, held_ref[0], table_ref[0]))
    table_ref[last] = table
    range_ref[...] = jnp.zeros_like(range_ref)
    for at in range(last + 1):
        windows, ranges, _ = edges(table_ref[at], SEG if at == last else 0)
        window_ref[at] = windows
        range_ref[at : at + 1, :] = ranges


def arrive(first, chip, held, messages, mine, came, after):
    count = len(messages) + 1
    half = mine.shape[0]
    pairs = RAD // 2
    return pl.pallas_call(
        functools.partial(arrive_kernel, first),
        out_shape=(
            jax.ShapeDtypeStruct((count, half, SEG), BF16),
            jax.ShapeDtypeStruct((count, pairs, PAIR), jnp.int32),
            jax.ShapeDtypeStruct((count, pairs, 128), jnp.int32),
            jax.ShapeDtypeStruct((8, 128), jnp.int32),
        ),
        in_specs=[smem()] + [vmem()] * (len(messages) + 3) + [anywhere()] * len(after),
        out_specs=(vmem(),) * 4,
        cost_estimate=cost(2),
        name="arrive",
    )(chip, held, *messages, mine, came, *after)


def squares_kernel(place_ref, *refs):
    count = len(GROUPS)
    windows, tables, lists = refs[:count], refs[count : 2 * count], refs[2 * count : 3 * count]
    out_ref = refs[-1]
    share = tables[0].shape[1] // 4
    half = lists[0].shape[1]
    ones = jnp.ones((8, PAIR), BF16)

    def one_pair(step, total):
        pair = place_ref[1] // 2 * share + step
        dense = jnp.zeros((half, PAIR), F32)
        for group, segs in enumerate(GROUPS):
            for at, seg in enumerate(segs):
                offset = 0 if seg < 4 else SEG
                row = tables[group][at, pl.ds(pair, 1), :] - offset

                def one_window(window, dense):
                    begin = pl.multiple_of(window * 256, 256)
                    ids = lax.broadcasted_iota(jnp.int32, (256, PAIR), 0)
                    hits = (ids == row - begin).astype(BF16)
                    return dense + dot_nn(lists[group][at, :, pl.ds(begin, 256)], hits)

                dense = lax.fori_loop(
                    windows[group][at, pair, 0], windows[group][at, pair, 1], one_window, dense
                )
        square = dense * dense
        high = square.astype(BF16)
        low = (square - high.astype(F32)).astype(BF16)
        return total + dot_nt(ones, high) + dot_nt(ones, low)

    out_ref[...] = lax.fori_loop(0, share, one_pair, jnp.zeros(out_ref.shape, F32))


def insert_sorted(best, value):
    out = []
    for held in best:
        out.append(jnp.maximum(held, value))
        value = jnp.minimum(held, value)
    return out


def merge_sorted(first, second):
    count = len(first)
    both = [jnp.maximum(first[i], second[count - 1 - i]) for i in range(count)]
    gap = count // 2
    while gap:
        for i in range(count):
            if i & gap == 0:
                high = jnp.maximum(both[i], both[i + gap])
                low = jnp.minimum(both[i], both[i + gap])
                both[i], both[i + gap] = high, low
        gap //= 2
    return both


def score_kernel(first, last, rows, *refs):
    count = 0 if first else 1
    own_ref, pair_ref, z_ref, x_ref, y_ref, d_ref, e_ref = refs[:7]
    rest = refs[7:]
    if not first:
        so_far_ref, rest = rest[0], rest[1:]
    if last:
        place_ref, local_ref, rank_ref, squares_ref, out_ref, total, lists, packed = rest
    else:
        out_ref, lists = rest[-2:]
        total = out_ref
    half = z_ref.shape[1]
    for seg in range(z_ref.shape[0]):
        lists[0:half, :] = z_ref[seg]
        lists[half : 2 * half, :] = x_ref[seg]
        lists[2 * half : 3 * half, :] = y_ref[seg]
        lists[3 * half : 3 * half + half // 2, :] = d_ref[seg]
        lists[3 * half + half // 2 :, :] = e_ref[seg]
        for side, ref in enumerate((own_ref, pair_ref)):
            term = dot_nt(ref[seg], lists[...])
            if seg == 0 and first:
                total[side] = term
            elif seg == 0:
                total[side] = so_far_ref[side] + term
            else:
                total[side] = total[side] + term
    if not last:
        return
    width = total.shape[2]
    low = jnp.full((8, width), -jnp.inf, F32)
    best = [low] * TOPK
    for side in range(2):
        def step(at, best):
            return tuple(
                insert_sorted(best, total[side, pl.ds(pl.multiple_of(at * 8, 8), 8), :])
            )

        best = lax.fori_loop(0, rows // 8, step, tuple(best), unroll=2)
    for turn in (4, 2, 1):
        best = merge_sorted(best, [pltpu.roll(part, turn, 0) for part in best])
    for place in range(TOPK):
        packed[place : place + 1, :] = best[place][0:1, :]
    picked = [jnp.zeros((1, width), F32) for _ in range(3)]
    for side in range(2):
        ids = lax.broadcasted_iota(jnp.int32, (rows, width), 0)
        picked[1] += jnp.sum(
            jnp.where(ids == local_ref[side : side + 1, :], total[side, :rows, :], 0.0),
            axis=0,
            keepdims=True,
        )
        ids = lax.broadcasted_iota(jnp.int32, (KEPT, width), 0)
        hit = ids == rank_ref[side : side + 1, :]
        picked[0] += jnp.sum(
            jnp.where(hit, total[side, rows : rows + KEPT, :], 0.0), axis=0, keepdims=True
        )
        picked[2] += jnp.sum(
            jnp.where(hit, total[side, rows + KEPT :, :], 0.0), axis=0, keepdims=True
        )
    packed[TOPK:, :] = jnp.zeros((8, width), F32)
    for place in range(3):
        packed[TOPK + place : TOPK + place + 1, :] = picked[place]
    packed[TOPK + 3 : TOPK + 4, :half] = squares_ref[0:1, :]
    section, core, orients = place_ref[0], place_ref[1] % 2, place_ref[2]
    for by in range(4):
        there = slice(by * half, (by + 1) * half)
        block = jnp.concatenate([packed[:TOPK, there], packed[TOPK:, there]], axis=1)
        block = pltpu.roll(block, core * half, 1)
        for orient in range(8):
            out_ref[(section ^ by) * orients + orient] = block


def score(first, last, rows, own, pair, lists, so_far, extra, after):
    height = own.shape[1]
    width = 4 * lists[0].shape[1]
    scratch = [pltpu.VMEM((width, SEG), BF16)]
    if last:
        scratch = [pltpu.VMEM((2, height, width), F32)] + scratch
        scratch.append(pltpu.VMEM((16, width), F32))
        shape = (32, TOPK, 128)
    else:
        shape = (2, height, width)
    args = [own, pair, *lists]
    if not first:
        args.append(so_far)
    specs = [vmem()] * len(args)
    if last:
        specs = specs + [smem()] + [vmem()] * 3
    args.extend(extra)
    return pl.pallas_call(
        functools.partial(score_kernel, first, last, rows),
        out_shape=jax.ShapeDtypeStruct(shape, F32),
        in_specs=specs + [anywhere()] * len(after),
        out_specs=vmem(),
        scratch_shapes=scratch,
        compiler_params=pltpu.CompilerParams(vmem_limit_bytes=GRANT * MIB),
        cost_estimate=cost(2 * own.shape[0]),
        name="score",
    )(*args, *after)


def final_kernel(place_ref, blocks_ref, top_ref, refined_ref, lines, turned):
    count = blocks_ref.shape[0]
    source = lax.broadcasted_iota(jnp.int32, (count, 128), 0)
    lane = lax.broadcasted_iota(jnp.int32, (count, 128), 1)
    best_here = (source % 2) == (lane // 64)
    best = []
    rest = []
    for place in range(TOPK):
        row = blocks_ref[:, place, :]
        best.append(jnp.where(best_here, row, -jnp.inf))
        if place < 4:
            rest.append(jnp.sum(jnp.where(best_here, 0.0, row), axis=0, keepdims=True))
    while count > 8:
        count //= 2
        best = merge_sorted([part[:count] for part in best], [part[count:] for part in best])
    for turn in (4, 2, 1):
        best = merge_sorted(best, [pltpu.roll(part, turn, 0) for part in best])
    rest = [pltpu.roll(row, 64, 1) for row in rest]
    factor = lax.rsqrt(rest[3] / BINS + EPS)
    for place in range(TOPK):
        lines[place : place + 1, :] = best[place][0:1, :] * factor
    top_ref[0] = lines[...].T
    for place in range(3):
        lines[place : place + 1, :] = rest[place] * factor
    turned[...] = lines[...].T
    share = refined_ref.shape[1]
    first = pl.multiple_of(place_ref[1] * share, share)
    refined_ref[0] = turned[pl.ds(first, share), :3]


def compact_body(patterns, detector_gain, background, bin_map, templates, best_picks):
    orients = lax.axis_size("orient")
    chips = orients // 2
    section = lax.axis_index("section")
    orient = lax.axis_index("orient")
    place = jnp.stack([section, orient, jnp.full_like(orient, orients)]).astype(jnp.int32)
    core = (orient % 2).reshape(1).astype(jnp.int32)
    chip = (orient // 2).reshape(1).astype(jnp.int32)
    rows = templates.shape[0]
    count = patterns.shape[1]
    half = count // 2
    pixels = patterns.shape[2]

    def swap(x):
        return lax.ppermute(x, "orient", [(i, i ^ 1) for i in range(orients)])

    def along(x, by):
        return lax.ppermute(x, "orient", [(i, (i + 2 * by) % orients) for i in range(orients)])

    def hops(x, pairs):
        return lax.ppermute(
            x, "orient", [(2 * i + c, 2 * j + c) for i, j in pairs for c in range(2)]
        )

    def across(x, by):
        return lax.ppermute(x, "section", [(i, i ^ by) for i in range(4)])

    tiles = pixels // TILE
    lines = bin_map.reshape(tiles, TILE)
    present = pl.pallas_call(
        presence_kernel,
        out_shape=jax.ShapeDtypeStruct((ANG, RAD), F32),
        in_specs=[vmem()],
        out_specs=vmem(),
        cost_estimate=cost(2),
        name="presence",
    )(lines)
    other = swap(present)
    steps = 8
    corrected = pl.pallas_call(
        pixels_kernel,
        grid=(steps,),
        out_shape=jax.ShapeDtypeStruct((pixels, count), BF16),
        in_specs=[
            pl.BlockSpec((1, count, pixels // steps), lambda i: (0, 0, i)),
            pl.BlockSpec((1, pixels // steps), lambda i: (0, i)),
            pl.BlockSpec((1, pixels // steps), lambda i: (0, i)),
        ],
        out_specs=pl.BlockSpec((pixels // steps, count), lambda i: (i, 0)),
        cost_estimate=cost(4),
        name="pixels",
    )(patterns, detector_gain.reshape(1, pixels), background.reshape(1, pixels))
    corrected = corrected.reshape(tiles, TILE, count)
    bins = bin_map.reshape(tiles // 16, 16, 16, 16).transpose(0, 2, 1, 3).reshape(tiles, TILE)
    table, slot_rows, span, own_ranges, own_windows = pl.pallas_call(
        slots_kernel,
        out_shape=(
            jax.ShapeDtypeStruct((RAD // 2, PAIR), jnp.int32),
            jax.ShapeDtypeStruct((tiles, TILE), jnp.int32),
            jax.ShapeDtypeStruct((tiles, 128), jnp.int32),
            jax.ShapeDtypeStruct((8, 128), jnp.int32),
            jax.ShapeDtypeStruct((1, RAD // 2, 128), jnp.int32),
        ),
        in_specs=[vmem()] * 3,
        out_specs=(vmem(),) * 5,
        cost_estimate=cost(3),
        name="slots",
    )(present, other, bins)
    mine, theirs = pl.pallas_call(
        binning_kernel,
        out_shape=(
            jax.ShapeDtypeStruct((half, ROOM), F32),
            jax.ShapeDtypeStruct((half, ROOM), BF16),
        ),
        in_specs=[smem(), smem(), vmem(), vmem()],
        out_specs=(vmem(),) * 2,
        scratch_shapes=[pltpu.VMEM((ROOM + WINDOW, count), F32), pltpu.VMEM((count, ROOM), F32)],
        compiler_params=pltpu.CompilerParams(vmem_limit_bytes=24 * MIB),
        cost_estimate=cost(6),
        name="binning",
    )(core, span, slot_rows, corrected)
    message, base, spare = pl.pallas_call(
        combine_kernel,
        out_shape=(
            jax.ShapeDtypeStruct((half, SEG + PAIR), BF16),
            jax.ShapeDtypeStruct((1, half, SEG), BF16),
            jax.ShapeDtypeStruct((half, ROOM - SEG), BF16),
        ),
        in_specs=[vmem()] * 3,
        out_specs=(vmem(),) * 3,
        cost_estimate=cost(1),
        name="combine",
    )(mine, swap(theirs), table)

    messages = [along(message, by) for by in range(1, chips)]
    step = hops(spare, [(1, 0), (2, 3)])
    traded = hops(spare, [(1, 2), (2, 1)])
    far_part = hops(spare, [(1, 3), (2, 0)])

    def spread(group):
        x = across(group, 1)
        y = across(group, 2)
        d = across(x[:, : half // 2], 2)
        e = across(y[:, half // 2 :], 1)
        return group, x, y, d, e

    own = [None] * 3
    lists = [spread(base), None, None]
    size = best_picks.shape[0] * count
    height = rows + 2 * KEPT
    own[0], turned, local, ranks, crowd = pl.pallas_call(
        first_kernel,
        out_shape=(
            jax.ShapeDtypeStruct((1, height, SEG), BF16),
            jax.ShapeDtypeStruct((2 * KEPT, BINS), BF16),
            jax.ShapeDtypeStruct((8, 4 * half), jnp.int32),
            jax.ShapeDtypeStruct((8, 4 * half), jnp.int32),
            jax.ShapeDtypeStruct((8, 128), jnp.int32),
        ),
        in_specs=[smem(), smem()] + [vmem()] * 4 + [anywhere()],
        out_specs=(vmem(),) * 5,
        compiler_params=pltpu.CompilerParams(vmem_limit_bytes=GRANT * MIB),
        cost_estimate=cost(10),
        name="first",
    )(
        place,
        own_ranges,
        table[None],
        best_picks.reshape(1, size),
        best_picks.reshape(size, 1),
        templates,
        base,
    )
    group, tables_near, windows_near, ranges_near = arrive(
        True, chip, table, [messages[0], messages[2]], spare, step, [own[0]]
    )
    lists[1] = spread(group)
    own[1] = columns(GROUPS[1], ranges_near, tables_near, templates, turned, lists[0][1:3])
    group, tables_far, windows_far, ranges_far = arrive(
        False, chip, tables_near, [messages[1]], traded, far_part, [own[1]]
    )
    lists[2] = spread(group)
    own[2] = columns(GROUPS[2], ranges_far, tables_far, templates, turned, lists[1][1:3])
    pair = [swap(part) for part in own]
    squares = pl.pallas_call(
        squares_kernel,
        out_shape=jax.ShapeDtypeStruct((8, half), F32),
        in_specs=[smem()] * 4 + [vmem()] * 6 + [anywhere()] * 2,
        out_specs=vmem(),
        cost_estimate=cost(5),
        name="squares",
    )(
        place, own_windows, windows_near, windows_far, table[None], tables_near, tables_far,
        lists[0][0], lists[1][0], lists[2][0], *lists[1][1:3],
    )
    total = score(True, False, rows, own[0], pair[0], lists[0], None, (), lists[1][1:3])
    total = score(False, False, rows, own[1], pair[1], lists[1], total, (), lists[2][1:3])
    blocks = score(
        False, True, rows, own[2], pair[2], lists[2], total, (place, local, ranks, squares), ()
    )
    blocks = lax.all_to_all(blocks, ("section", "orient"), 0, 0)
    top, refined = pl.pallas_call(
        final_kernel,
        out_shape=(
            jax.ShapeDtypeStruct((1, count, TOPK), F32),
            jax.ShapeDtypeStruct((1, count // orients, 3), F32),
        ),
        in_specs=[smem(), vmem()],
        out_specs=(vmem(), vmem()),
        scratch_shapes=[pltpu.VMEM((TOPK, count), F32), pltpu.VMEM((count, TOPK), F32)],
        cost_estimate=cost(2),
        name="final",
    )(place, blocks)

    chip_ids = (chip - lax.iota(jnp.int32, chips)) % chips
    totals = jnp.stack(
        [own_ranges[0, 127], ranges_near[0, 127], ranges_far[0, 127], ranges_near[1, 127]]
    )
    room = jnp.where((chip_ids == 1) | (chip_ids == 2), ROOM, SEG)
    crowded = jnp.any(totals > room) | (crowd[0, 0] >= KEPT)
    return lax.cond(
        crowded,
        lambda: dense_body(
            patterns, detector_gain, background, bin_map, templates, best_picks
        ),
        lambda: (top, refined),
    )


def solution(mesh):
    sizes = dict(mesh.shape)
    fits = sizes["section"] == 4 and sizes["orient"] == 8
    return jax.shard_map(
        compact_body if fits else dense_body,
        mesh=mesh,
        in_specs=(
            P("section", None, "orient"),
            P("orient"),
            P("orient"),
            P("orient"),
            P(("section", "orient"), None),
            P(),
        ),
        out_specs=(P("section", None, None), P("section", "orient", None)),
        check_vma=False,
    )
```

```python
import functools

import jax
import jax.numpy as jnp
from jax import lax
from jax.experimental import pallas as pl
from jax.experimental.pallas import tpu as pltpu
from jax.sharding import PartitionSpec as P

RAD = 64
ANG = 192
TOPK = 8
REACH = 1


EPS = 1e-06
BLOCK_ROWS = 512


def shifted(x, axis, by):
    count = lax.axis_size(axis)
    return lax.ppermute(x, axis, [(i, (i + by) % count) for i in range(count)])


def merged_2(part, axis, combine):
    gathered = lax.all_gather(part, axis)

    def take(source):
        return lax.dynamic_index_in_dim(gathered, source, 0, False)

    return lax.fori_loop(
        1, lax.axis_size(axis), lambda source, state: combine(state, take(source)), take(0)
    )


def bin_block(corrected, bin_map, first, length):
    targets = first + lax.iota(jnp.int32, length)
    onehot = (bin_map[None, :] == targets[:, None]).astype(jnp.bfloat16)
    return lax.dot_general(
        onehot, corrected, (((1,), (1,)), ((), ())), preferred_element_type=jnp.float32
    )


def bin_rows(corrected, bin_map, length):
    blocks = 1
    while length // blocks > BLOCK_ROWS and length % (2 * blocks) == 0:
        blocks = blocks * 2
    height = length // blocks
    starts = height * lax.iota(jnp.int32, blocks)
    stacked = lax.map(lambda begin: bin_block(corrected, bin_map, begin, height), starts)
    return stacked.reshape(length, corrected.shape[0])


def merge_best(first_best, second_best):
    return lax.top_k(jnp.concatenate([first_best, second_best], axis=-1), TOPK)[0]


def score_batch(features, templates, wanted, group_base):
    scores = lax.dot_general(
        features, templates, (((0,), (1,)), ((), ())), preferred_element_type=jnp.float32
    )
    best = lax.top_k(scores, TOPK)[0]
    local = wanted - group_base
    count = templates.shape[0]
    owned = (local >= 0) & (local < count)
    chosen = jnp.take(templates, jnp.clip(local, 0, count - 1), axis=0)
    width = features.shape[1]
    chosen = chosen.reshape(width, RAD, ANG)
    grid = features.T.reshape(width, RAD, ANG)
    columns = []
    for offset in range(-REACH, REACH + 1):
        rolled = jnp.roll(chosen, -offset, axis=2)
        columns.append(jnp.sum(grid.astype(jnp.float32) * rolled.astype(jnp.float32), axis=(1, 2)))
    refined = jnp.where(owned[:, None], jnp.stack(columns, axis=1), 0.0)
    return (best, refined)


def dense_body(patterns, detector_gain, background, bin_map, templates, best_picks):
    sections = lax.axis_size("section")
    orients = lax.axis_size("orient")
    section_index = lax.axis_index("section")
    orient_index = lax.axis_index("orient")
    features_total = RAD * ANG
    corrected = ((patterns[0].astype(jnp.float32) - background) * detector_gain).astype(
        jnp.bfloat16
    )
    whole = lax.psum(bin_rows(corrected, bin_map, features_total), "orient")
    squares = jnp.sum(whole * whole, axis=0)
    features = (whole * lax.rsqrt(squares / features_total + EPS)).astype(jnp.bfloat16)
    group_base = (section_index * orients + orient_index) * templates.shape[0]
    held = features
    running_best = None
    running_refined = None
    for turn in range(sections):
        batch = (section_index + sections - turn) % sections
        wanted = lax.dynamic_index_in_dim(best_picks, batch, 0, keepdims=False)
        best, refined = score_batch(held, templates, wanted, group_base)
        if turn > 0:
            best = merge_best(running_best, best)
            refined = running_refined + refined
        packed = shifted(jnp.concatenate([best, refined], axis=1), "section", 1)
        running_best = packed[:, :TOPK]
        running_refined = packed[:, TOPK:]
        if turn + 1 < sections:
            held = shifted(held, "section", 1)
    merged = merged_2(running_best, "orient", merge_best)
    shares = lax.psum_scatter(running_refined, "orient", scatter_dimension=0, tiled=True)
    return (merged[None], shares[None])


BINS = RAD * ANG
SEG = 1792
SEGS = 6
ROOM = 2 * SEG
TILE = 256
WINDOW = 512
GROUPS = ((0, 1, 3, 4), (2, 5))
KEPT = 32
SQUARE = 384
GRANT = 22
PAIR = 2 * ANG
MIB = 1 << 20
F32 = jnp.float32
BF16 = jnp.bfloat16


def vmem():
    return pl.BlockSpec(memory_space=pltpu.VMEM)


def smem():
    return pl.BlockSpec(memory_space=pltpu.SMEM)


def cost(micros):
    return pl.CostEstimate(
        flops=int(micros * 1.1e9), bytes_accessed=int(micros * 1e6), transcendentals=0
    )


def dot_nt(a, b):
    return lax.dot_general(a, b, (((1,), (1,)), ((), ())), preferred_element_type=F32)


def dot_nn(a, b):
    return lax.dot_general(a, b, (((1,), (0,)), ((), ())), preferred_element_type=F32)


def polar(row):
    value = row.astype(F32)
    radial = jnp.floor((value + 0.5) * (1.0 / ANG))
    return radial, value - radial * ANG


def members(values, count):
    ids = lax.broadcasted_iota(jnp.int32, (count, values.shape[1]), 0).astype(F32)
    return ids == values


def presence_kernel(bins_ref, counts_ref):
    counts = jnp.zeros((ANG, RAD), F32)
    for line in range(0, bins_ref.shape[0], 2):
        parts = [bins_ref[line : line + 1, :], bins_ref[line + 1 : line + 2, :]]
        radial, angle = polar(jnp.concatenate(parts, axis=1))
        counts += dot_nt(
            members(angle, ANG).astype(BF16), members(radial, RAD).astype(BF16)
        )
    counts_ref[...] = (counts > 0.5).astype(F32)


def below(size):
    rows = lax.broadcasted_iota(jnp.int32, (size, size), 0)
    cols = lax.broadcasted_iota(jnp.int32, (size, size), 1)
    return rows, cols


def edges(table, offset):
    pairs = table.shape[0]
    valid = (table >= 0).astype(F32).astype(BF16)
    count = dot_nn(valid, jnp.ones((PAIR, 128), BF16))
    rows, cols = below(pairs)
    low_end = count - 256 * jnp.floor(count * (1.0 / 256))
    high_end = jnp.floor(count * (1.0 / 256))
    sums = (cols <= rows).astype(BF16)
    ends = 256 * dot_nn(sums, high_end.astype(BF16)) + dot_nn(sums, low_end.astype(BF16))
    begins = ends - count
    lane = lax.broadcasted_iota(jnp.int32, count.shape, 1)
    wide = SEG // 128
    first = jnp.clip(jnp.floor((begins - offset) * (1.0 / 128)), 0, wide - SQUARE // 128)
    last = jnp.clip(jnp.floor((ends - offset + 127) * (1.0 / 128)), 0, wide)
    windows = jnp.where(lane == 0, first, jnp.where(count > 0, last, 0.0))
    at = (lane % 64).astype(F32) * 256 + offset
    found = jnp.where(lane < 64, (ends <= at).astype(F32), (begins < at + 256).astype(F32))
    ranges = jnp.sum(found, axis=0, keepdims=True)
    ranges = jnp.where(lane[:1] == 127, ends[pairs - 1 :], ranges)
    return windows.astype(jnp.int32), ranges.astype(jnp.int32), ends


def slots_kernel(own_ref, other_ref, bins_ref, table_ref, rows_ref, span_ref):
    present = jnp.maximum(own_ref[...], other_ref[...])
    held = present.astype(BF16)
    rows, cols = below(ANG)
    within = dot_nn((cols < rows).astype(BF16), held)
    totals = dot_nn(jnp.ones((ANG, ANG), BF16), held)
    rows, cols = below(RAD)
    before = dot_nn(totals.astype(BF16), (rows < cols).astype(BF16))
    slots = within + before
    high = jnp.floor(slots * (1.0 / 64))
    low = slots - 64 * high
    high = high.astype(BF16)
    low = low.astype(BF16)
    both = jnp.concatenate([high, low])
    line = lax.broadcasted_iota(jnp.int32, (RAD // 2, RAD), 0)
    ring = lax.broadcasted_iota(jnp.int32, (RAD // 2, RAD), 1)
    for side in range(2):
        pick = (ring == 2 * line + side).astype(BF16)
        turned = 64 * dot_nt(pick, high) + dot_nt(pick, low)
        table_ref[:, side * ANG : (side + 1) * ANG] = jnp.where(
            dot_nt(pick, held) > 0.5, turned, -1.0
        ).astype(jnp.int32)
    for tile in range(bins_ref.shape[0]):
        radial, angle = polar(bins_ref[tile : tile + 1, :])
        ring = members(radial, RAD).astype(BF16)
        value = dot_nn(both, ring)
        value = 64 * value[:ANG] + value[ANG:]
        value = jnp.sum(jnp.where(members(angle, ANG), value, 0.0), axis=0, keepdims=True)
        rows_ref[tile : tile + 1, :] = value.astype(jnp.int32)
    found = rows_ref[...]
    first = jnp.min(found, axis=1, keepdims=True)
    last = jnp.max(found, axis=1, keepdims=True)
    lane = lax.broadcasted_iota(jnp.int32, (found.shape[0], 128), 1)
    span_ref[...] = jnp.where(lane == 0, first, last)


def pixels_kernel(patterns_ref, gain_ref, background_ref, out_ref):
    value = (patterns_ref[0].astype(F32) - background_ref[...]) * gain_ref[...]
    out_ref[...] = value.astype(BF16).T


def binning_kernel(
    core_ref, span_ref, rows_ref, pixels_ref, mine_ref, theirs_ref, sums, turned
):
    sums[...] = jnp.zeros_like(sums)
    across = 256 // 16

    def add(tile, at):
        down = (tile // across) * 16
        right = (tile % across) * 16
        block = pixels_ref[pl.ds(down, 16), pl.ds(right, 16), :].reshape(TILE, 128)
        row = rows_ref[pl.ds(tile, 1), :]
        ids = lax.broadcasted_iota(jnp.int32, (WINDOW, TILE), 0)
        hits = (ids == row - at).astype(BF16)
        sums[pl.ds(at, WINDOW), :] += dot_nn(hits, block)

    def base_of(tile):
        return pl.multiple_of(jnp.minimum(span_ref[tile, 0], ROOM) // 8 * 8, 8)

    tiles = rows_ref.shape[0]
    for tile in range(tiles):
        add(tile, base_of(tile))

    def one_tile(tile, _):
        base = base_of(tile)
        stop = jnp.minimum(span_ref[tile, 1] + 1, ROOM)

        def one_window(step, _):
            add(tile, pl.multiple_of(base + step * WINDOW, 8))
            return 0

        lax.fori_loop(1, (stop - base + WINDOW - 1) // WINDOW, one_window, 0)
        return 0

    lax.fori_loop(0, tiles, one_tile, 0)
    for block in range(ROOM // 128):
        turned[:, block * 128 : (block + 1) * 128] = sums[
            block * 128 : (block + 1) * 128, :
        ].T
    core = core_ref[0]
    half = turned.shape[0] // 2
    mine_ref[...] = turned[pl.ds(pl.multiple_of(core * half, half), half), :]
    theirs_ref[...] = turned[
        pl.ds(pl.multiple_of((1 - core) * half, half), half), :
    ].astype(BF16)


def combine_kernel(
    mine_ref, theirs_ref, table_ref, message_ref, spare_ref
):
    total = (mine_ref[...] + theirs_ref[...].astype(F32)).astype(BF16)
    spare_ref[...] = total[:, SEG:]
    message_ref[:, :SEG] = total[:, :SEG]
    table = table_ref[...].astype(F32)
    high = jnp.floor(table * (1.0 / 64))
    pairs = table.shape[0]
    message_ref[:pairs, SEG:] = high.astype(BF16)
    message_ref[pairs:, SEG:] = (table - 64 * high).astype(BF16)


def sum_rows(mask, value):
    return jnp.sum(jnp.where(mask, value, 0.0), axis=0, keepdims=True)


def sum_lanes(mask, value):
    return jnp.sum(jnp.where(mask, value, 0.0), axis=1, keepdims=True)


def place_picks(place_ref, row_ref, col_ref, rows, local_ref, rank_ref, crowd_ref):
    section, orient, orients = place_ref[0], place_ref[1], place_ref[2]
    row = row_ref[...].astype(F32)
    col = col_ref[...].astype(F32)
    size = row.shape[1]
    i = lax.broadcasted_iota(jnp.int32, (size, size), 0)
    j = lax.broadcasted_iota(jnp.int32, (size, size), 1)
    equal = col == row
    first_row = (sum_rows(equal & (i < j), 1.0) == 0).astype(F32)
    first_col = (sum_lanes(equal & (j < i), 1.0) == 0).astype(F32)
    owner_row = jnp.floor((row + 0.5) * (1.0 / rows))
    owner_col = jnp.floor((col + 0.5) * (1.0 / rows))
    same = owner_col == owner_row
    rank_row = sum_rows(same & (i < j), first_col)
    rank_col = sum_lanes(same & (j < i), first_row)
    rank_of = sum_rows(equal, first_col * rank_col)
    crowd_ref[...] = jnp.broadcast_to(
        jnp.max(rank_of, axis=1, keepdims=True), crowd_ref.shape
    ).astype(jnp.int32)
    me = section * orients + orient
    base = (me * rows).astype(F32)
    ids = lax.broadcasted_iota(jnp.int32, (KEPT, size), 0).astype(F32)
    chosen = (first_row > 0) & (owner_row == me.astype(F32)) & (rank_row == ids)
    wanted = sum_lanes(chosen, row - base + 1) - 1
    half = 64
    core = orient % 2
    local_ref[...] = jnp.zeros_like(local_ref)
    rank_ref[...] = jnp.zeros_like(rank_ref)
    lanes = lax.broadcasted_iota(jnp.int32, (1, size), 1)
    for by in range(4):
        start = (section ^ by) * 2 * half + core * half
        shift = (size - start) % size
        there = slice(by * half, (by + 1) * half)
        local_ref[2:3, there] = pltpu.roll(row, shift, 1)[:, :half].astype(jnp.int32)
        rank_ref[2:3, there] = pltpu.roll(rank_of, shift, 1)[:, :half].astype(jnp.int32)
    for side in range(2):
        owner = section * orients + (orient ^ side)
        local = local_ref[2:3, :] - owner * rows
        held = (local >= 0) & (local < rows)
        local_ref[side : side + 1, :] = jnp.where(held, local, -1)
        rank_ref[side : side + 1, :] = jnp.where(held, rank_ref[2:3, :], -1)
    return wanted


def turn_picks(wanted, templates_ref, out_ref):
    rows = templates_ref.shape[0]
    ids = lax.broadcasted_iota(jnp.int32, (KEPT, rows), 1).astype(F32)
    select = (ids == wanted).astype(BF16)
    lane = lax.broadcasted_iota(jnp.int32, (KEPT, PAIR), 1)
    for pair in range(RAD // 2):
        cols = slice(pair * PAIR, (pair + 1) * PAIR)
        taken = dot_nn(select, templates_ref[:, cols])
        later = jnp.where(
            lane % ANG == 0, pltpu.roll(taken, ANG + 1, 1), pltpu.roll(taken, 1, 1)
        )
        sooner = jnp.where(
            lane % ANG == ANG - 1,
            pltpu.roll(taken, ANG - 1, 1),
            pltpu.roll(taken, PAIR - 1, 1),
        )
        out_ref[:KEPT, cols] = later.astype(BF16)
        out_ref[KEPT:, cols] = sooner.astype(BF16)


def permute_columns(seg, offset, range_ref, table_ref, templates_ref, turned_ref, out_ref):
    wide = 5

    def block(pair, pairs):
        col = pl.ds(pl.multiple_of(pair * PAIR, 128), pairs * PAIR)
        return jnp.concatenate([templates_ref[:, col], turned_ref[:, col]], axis=0)

    def hits(pair, at):
        row = table_ref[seg, pl.ds(pair, 1), :]
        ids = lax.broadcasted_iota(jnp.int32, (256, PAIR), 0)
        return (ids == row - at).astype(BF16)

    def start_of(window):
        return jnp.minimum(range_ref[seg, window], RAD // 2 - wide)

    for window in range(SEG // 256):
        at = offset + window * 256
        start = start_of(window)
        mask = jnp.concatenate([hits(start + i, at) for i in range(wide)], axis=1)
        out_ref[0, :, window * 256 : (window + 1) * 256] = dot_nt(
            block(start, wide), mask
        ).astype(BF16)

    def one_window(window, _):
        to = pl.ds(pl.multiple_of(window * 256, 256), 256)

        def one_pair(pair, _):
            more = dot_nt(block(pair, 1), hits(pair, offset + window * 256))
            out_ref[0, :, to] = (out_ref[0, :, to].astype(F32) + more).astype(BF16)
            return 0

        lax.fori_loop(start_of(window) + wide, range_ref[seg, 64 + window], one_pair, 0)
        return 0

    more = 0
    for window in range(SEG // 256):
        more = jnp.maximum(more, range_ref[seg, 64 + window] - start_of(window))

    @pl.when(more > wide)
    def _():
        lax.fori_loop(0, SEG // 256, one_window, 0)


def picks_kernel(
    place_ref, row_ref, col_ref, templates_ref, _, turned_ref, local_ref, rank_ref, crowd_ref
):
    rows = templates_ref.shape[0]
    wanted = place_picks(place_ref, row_ref, col_ref, rows, local_ref, rank_ref, crowd_ref)
    turn_picks(wanted, templates_ref, turned_ref)


def columns_kernel(range_ref, table_ref, templates_ref, turned_ref, *refs):
    out_ref, token_ref, held_ref, arrived = refs[-4:]
    seg = pl.program_id(0)

    @pl.when(seg == 0)
    def _():
        copy = pltpu.make_async_copy(templates_ref, held_ref, arrived)
        copy.start()
        token_ref[...] = jnp.zeros_like(token_ref)
        copy.wait()

    offset = jnp.where(seg == pl.num_programs(0) - 1, SEG, 0)
    permute_columns(seg, offset, range_ref, table_ref, held_ref, turned_ref, out_ref)


def whole(shape):
    return pl.BlockSpec(shape, lambda i: (0,) * len(shape))


def each(shape):
    return pl.BlockSpec((1, *shape), lambda i: (i,) + (0,) * len(shape))


def columns(count, ranges, tables, templates, turned, after):
    height = templates.shape[0] + turned.shape[0]
    return pl.pallas_call(
        columns_kernel,
        grid=(count,),
        out_shape=(
            jax.ShapeDtypeStruct((count, height, SEG), BF16),
            jax.ShapeDtypeStruct((8, 128), F32),
        ),
        in_specs=[
            smem(),
            whole(tables.shape),
            pl.BlockSpec(memory_space=pl.ANY),
            whole(turned.shape),
        ]
        + [vmem()] * len(after),
        out_specs=(each((height, SEG)), whole((8, 128))),
        scratch_shapes=[pltpu.VMEM(templates.shape, BF16), pltpu.SemaphoreType.DMA],
        compiler_params=pltpu.CompilerParams(vmem_limit_bytes=GRANT * MIB),
        cost_estimate=cost(30 * count),
        name="columns",
    )(ranges, tables, templates, turned, *after)


def arrive_kernel(first, chip_ref, held_ref, *refs):
    group_ref, table_ref, window_ref, range_ref, full_ref = refs[-5:]
    messages = refs[:3] if first else refs[:1]
    mine_ref, came_ref = refs[len(messages) : len(messages) + 2]
    pairs = table_ref.shape[1]
    chip = chip_ref[0]
    inner = (chip == 1) | (chip == 2)
    for at, ref in enumerate(messages):
        group_ref[at] = ref[:, :SEG]
        high = ref[:pairs, SEG:].astype(F32)
        low = ref[pairs:, SEG:].astype(F32)
        table_ref[at] = (64 * high + low).astype(jnp.int32)
    last = len(messages)

    @pl.when(inner)
    def _():
        group_ref[last] = mine_ref[...]

    @pl.when(jnp.logical_not(inner))
    def _():
        group_ref[last] = came_ref[...]

    if first:
        table = jnp.where(chip == 0, table_ref[2], jnp.where(chip == 3, table_ref[1], table_ref[0]))
    else:
        table = jnp.where(chip == 1, held_ref[2], jnp.where(chip == 2, held_ref[1], table_ref[0]))
    table_ref[last] = table
    range_ref[...] = jnp.zeros_like(range_ref)
    for at in range(last + 1):
        windows, ranges, _ = edges(table_ref[at], SEG if at == last else 0)
        window_ref[at] = windows
        range_ref[at : at + 1, :] = ranges
    chips = [chip, (chip + 3) % 4, (chip + 1) % 4] if first else [(chip + 2) % 4]
    totals = [range_ref[at : at + 1, :] for at in range(len(chips))]
    full = jnp.zeros((1, 128), jnp.int32)
    for held, total in zip(chips, totals, strict=True):
        room = jnp.where((held == 1) | (held == 2), ROOM, SEG)
        full = jnp.maximum(full, (total > room).astype(jnp.int32))
    if not first:
        near_ref, crowd_ref = refs[len(messages) + 2 : len(messages) + 4]
        full = jnp.maximum(full, near_ref[0:1, :])
        full = jnp.maximum(full, (crowd_ref[0:1, :] >= KEPT).astype(jnp.int32))
    lane = lax.broadcasted_iota(jnp.int32, (8, 128), 1)
    full = jnp.where(lane == 127, jnp.broadcast_to(full, (8, 128)), 0)
    full_ref[...] = jnp.broadcast_to(jnp.max(full, axis=1, keepdims=True), (8, 128))


def arrive(first, chip, held, messages, mine, came, extra, after):
    count = len(messages) + 1
    half = mine.shape[0]
    pairs = RAD // 2
    return pl.pallas_call(
        functools.partial(arrive_kernel, first),
        out_shape=(
            jax.ShapeDtypeStruct((count, half, SEG), BF16),
            jax.ShapeDtypeStruct((count, pairs, PAIR), jnp.int32),
            jax.ShapeDtypeStruct((count, pairs, 128), jnp.int32),
            jax.ShapeDtypeStruct((8, 128), jnp.int32),
            jax.ShapeDtypeStruct((8, 128), jnp.int32),
        ),
        in_specs=[smem()]
        + [vmem()] * (len(messages) + 3 + len(extra))
        + [vmem()] * len(after),
        out_specs=(vmem(),) * 5,
        cost_estimate=cost(1),
        name="arrive",
    )(chip, held, *messages, mine, came, *extra, *after)


def halves_kernel(x_ref, y_ref, *refs):
    upper_ref, lower_ref = refs[-2:]
    size = upper_ref.shape[1]
    upper_ref[...] = x_ref[:, :size]
    lower_ref[...] = y_ref[:, size:]


def halves(x, y, after):
    shape = jax.ShapeDtypeStruct((x.shape[0], x.shape[1] // 2, x.shape[2]), x.dtype)
    return pl.pallas_call(
        halves_kernel,
        out_shape=(shape, shape),
        in_specs=[vmem(), vmem()] + [vmem()] * len(after),
        out_specs=(vmem(), vmem()),
        cost_estimate=cost(1),
        name="halves",
    )(x, y, *after)


def squares_kernel(place_ref, *refs):
    count = len(GROUPS)
    windows, tables, lists = refs[:count], refs[count : 2 * count], refs[2 * count : 3 * count]
    out_ref, dense_ref = refs[-2:]
    share = tables[0].shape[1] // 4
    half = lists[0].shape[1]
    first = place_ref[1] // 2 * share
    parts = [
        (windows[group], tables[group], lists[group], at, 0 if seg < 4 else SEG)
        for group, segs in enumerate(GROUPS)
        for at, seg in enumerate(segs)
    ]

    def hits(table, at, offset, pair, begin, size):
        ids = lax.broadcasted_iota(jnp.int32, (size, PAIR), 0)
        return (ids == table[at, pl.ds(pair, 1), :] - offset - begin).astype(BF16)

    for step in range(share):
        pair = first + step
        masks = []
        values = []
        for window, table, ref, at, offset in parts:
            begin = pl.multiple_of(window[at, pair, 0] * 128, 128)
            masks.append(hits(table, at, offset, pair, begin, SQUARE))
            values.append(ref[at, :, pl.ds(begin, SQUARE)])
        dense_ref[step] = dot_nn(jnp.concatenate(values, axis=1), jnp.concatenate(masks, axis=0))

    def one_pair(step, _):
        pair = first + step
        more = 0
        for window, _, _, at, _ in parts:
            more = jnp.maximum(more, window[at, pair, 1] - window[at, pair, 0])

        @pl.when(more > SQUARE // 128)
        def _():
            for window, table, ref, at, offset in parts:

                def one_window(index, _):
                    begin = pl.multiple_of(index * 128, 128)
                    dense_ref[step] += dot_nn(
                        ref[at, :, pl.ds(begin, 128)], hits(table, at, offset, pair, begin, 128)
                    )
                    return 0

                lax.fori_loop(
                    window[at, pair, 0] + SQUARE // 128, window[at, pair, 1], one_window, 0
                )

        return 0

    lax.fori_loop(0, share, one_pair, 0)
    ones = jnp.ones((8, PAIR), BF16)
    total = jnp.zeros((8, half), F32)
    for step in range(share):
        square = dense_ref[step] * dense_ref[step]
        high = square.astype(BF16)
        low = (square - high.astype(F32)).astype(BF16)
        total = total + dot_nt(ones, high) + dot_nt(ones, low)
    out_ref[...] = total


def insert_sorted(best, value):
    out = []
    for held in best:
        out.append(jnp.maximum(held, value))
        value = jnp.minimum(held, value)
    return out


def merge_sorted(first, second):
    count = len(first)
    both = [jnp.maximum(first[i], second[count - 1 - i]) for i in range(count)]
    gap = count // 2
    while gap:
        for i in range(count):
            if i & gap == 0:
                high = jnp.maximum(both[i], both[i + gap])
                low = jnp.minimum(both[i], both[i + gap])
                both[i], both[i + gap] = high, low
        gap //= 2
    return both


def score_kernel(first, last, rows, *refs):
    count = 0 if first else 1
    own_ref, pair_ref, z_ref, x_ref, y_ref, d_ref, e_ref = refs[:7]
    rest = refs[7:]
    if not first:
        so_far_ref, rest = rest[0], rest[1:]
    if last:
        place_ref, local_ref, rank_ref, squares_ref, out_ref, total, lists, packed = rest
    else:
        out_ref, lists = rest[-2:]
        total = out_ref
    half = z_ref.shape[1]
    lists[0:half, :] = z_ref[0]
    lists[half : 2 * half, :] = x_ref[0]
    lists[2 * half : 3 * half, :] = y_ref[0]
    lists[3 * half : 3 * half + half // 2, :] = d_ref[0]
    lists[3 * half + half // 2 :, :] = e_ref[0]

    @pl.when(pl.program_id(0) == 0)
    def _():
        total[...] = jnp.zeros_like(total) if first else so_far_ref[...]

    for side, ref in enumerate((own_ref, pair_ref)):
        total[side] += dot_nt(ref[0], lists[...])
    if last:

        @pl.when(pl.program_id(0) == pl.num_programs(0) - 1)
        def _():
            pick_out(
                rows, half, total, place_ref, local_ref, rank_ref, squares_ref, out_ref, packed
            )


def pick_out(rows, half, total, place_ref, local_ref, rank_ref, squares_ref, out_ref, packed):
    width = total.shape[2]
    low = jnp.full((8, width), -jnp.inf, F32)
    best = [low] * TOPK
    for side in range(2):
        def step(at, best):
            return tuple(
                insert_sorted(best, total[side, pl.ds(pl.multiple_of(at * 8, 8), 8), :])
            )

        best = lax.fori_loop(0, rows // 8, step, tuple(best), unroll=2)
    for turn in (4, 2, 1):
        best = merge_sorted(best, [pltpu.roll(part, turn, 0) for part in best])
    for place in range(TOPK):
        packed[place : place + 1, :] = best[place][0:1, :]
    picked = [jnp.zeros((1, width), F32) for _ in range(3)]
    for side in range(2):
        ids = lax.broadcasted_iota(jnp.int32, (rows, width), 0)
        picked[1] += jnp.sum(
            jnp.where(ids == local_ref[side : side + 1, :], total[side, :rows, :], 0.0),
            axis=0,
            keepdims=True,
        )
        ids = lax.broadcasted_iota(jnp.int32, (KEPT, width), 0)
        hit = ids == rank_ref[side : side + 1, :]
        picked[0] += jnp.sum(
            jnp.where(hit, total[side, rows : rows + KEPT, :], 0.0), axis=0, keepdims=True
        )
        picked[2] += jnp.sum(
            jnp.where(hit, total[side, rows + KEPT :, :], 0.0), axis=0, keepdims=True
        )
    packed[TOPK:, :] = jnp.zeros((8, width), F32)
    for place in range(3):
        packed[TOPK + place : TOPK + place + 1, :] = picked[place]
    packed[TOPK + 3 : TOPK + 4, :half] = squares_ref[0:1, :]
    section, core, orients = place_ref[0], place_ref[1] % 2, place_ref[2]
    for by in range(4):
        there = slice(by * half, (by + 1) * half)
        block = jnp.concatenate([packed[:TOPK, there], packed[TOPK:, there]], axis=1)
        block = pltpu.roll(block, core * half, 1)
        for orient in range(8):
            out_ref[(section ^ by) * orients + orient] = block


def score(first, last, rows, own, pair, lists, so_far, extra, after, micros):
    count, height, _ = own.shape
    width = 4 * lists[0].shape[1]
    scratch = [pltpu.VMEM((width, SEG), BF16)]
    if last:
        scratch = [pltpu.VMEM((2, height, width), F32)] + scratch
        scratch.append(pltpu.VMEM((16, width), F32))
        shape = (32, TOPK, 128)
    else:
        shape = (2, height, width)
    args = [own, pair, *lists]
    specs = [each(arg.shape[1:]) for arg in args]
    if not first:
        args.append(so_far)
        specs.append(whole(so_far.shape))
    if last:
        specs = specs + [smem()] + [vmem()] * 3
    args.extend(extra)
    return pl.pallas_call(
        functools.partial(score_kernel, first, last, rows),
        grid=(count,),
        out_shape=jax.ShapeDtypeStruct(shape, F32),
        in_specs=specs + [vmem()] * len(after),
        out_specs=whole(shape),
        scratch_shapes=scratch,
        compiler_params=pltpu.CompilerParams(vmem_limit_bytes=GRANT * MIB),
        cost_estimate=cost(micros),
        name="score",
    )(*args, *after)


def final_kernel(place_ref, blocks_ref, top_ref, refined_ref, lines, turned):
    count = blocks_ref.shape[0]
    source = lax.broadcasted_iota(jnp.int32, (count, 128), 0)
    lane = lax.broadcasted_iota(jnp.int32, (count, 128), 1)
    best_here = (source % 2) == (lane // 64)
    best = []
    rest = []
    for place in range(TOPK):
        row = blocks_ref[:, place, :]
        best.append(jnp.where(best_here, row, -jnp.inf))
        if place < 4:
            rest.append(jnp.sum(jnp.where(best_here, 0.0, row), axis=0, keepdims=True))
    while count > 8:
        count //= 2
        best = merge_sorted([part[:count] for part in best], [part[count:] for part in best])
    for turn in (4, 2, 1):
        best = merge_sorted(best, [pltpu.roll(part, turn, 0) for part in best])
    rest = [pltpu.roll(row, 64, 1) for row in rest]
    factor = lax.rsqrt(rest[3] / BINS + EPS)
    for place in range(TOPK):
        lines[place : place + 1, :] = best[place][0:1, :] * factor
    top_ref[0] = lines[...].T
    for place in range(3):
        lines[place : place + 1, :] = rest[place] * factor
    turned[...] = lines[...].T
    share = refined_ref.shape[1]
    first = pl.multiple_of(place_ref[1] * share, share)
    refined_ref[0] = turned[pl.ds(first, share), :3]


def compact_body(patterns, detector_gain, background, bin_map, templates, best_picks):
    orients = lax.axis_size("orient")
    chips = orients // 2
    section = lax.axis_index("section")
    orient = lax.axis_index("orient")
    place = jnp.stack([section, orient, jnp.full_like(orient, orients)]).astype(jnp.int32)
    core = (orient % 2).reshape(1).astype(jnp.int32)
    chip = (orient // 2).reshape(1).astype(jnp.int32)
    rows = templates.shape[0]
    count = patterns.shape[1]
    half = count // 2
    pixels = patterns.shape[2]

    def swap(x):
        return lax.ppermute(x, "orient", [(i, i ^ 1) for i in range(orients)])

    def along(x, by):
        return lax.ppermute(x, "orient", [(i, (i + 2 * by) % orients) for i in range(orients)])

    def hops(x, pairs):
        return lax.ppermute(
            x, "orient", [(2 * i + c, 2 * j + c) for i, j in pairs for c in range(2)]
        )

    def across(x, by):
        return lax.ppermute(x, "section", [(i, i ^ by) for i in range(4)])

    tiles = pixels // TILE
    lines = bin_map.reshape(2 * tiles, TILE // 2)
    present = pl.pallas_call(
        presence_kernel,
        out_shape=jax.ShapeDtypeStruct((ANG, RAD), F32),
        in_specs=[vmem()],
        out_specs=vmem(),
        cost_estimate=cost(2),
        name="presence",
    )(lines)
    other = swap(present)
    steps = 8
    corrected = pl.pallas_call(
        pixels_kernel,
        grid=(steps,),
        out_shape=jax.ShapeDtypeStruct((pixels, count), BF16),
        in_specs=[
            pl.BlockSpec((1, count, pixels // steps), lambda i: (0, 0, i)),
            pl.BlockSpec((1, pixels // steps), lambda i: (0, i)),
            pl.BlockSpec((1, pixels // steps), lambda i: (0, i)),
        ],
        out_specs=pl.BlockSpec((pixels // steps, count), lambda i: (i, 0)),
        cost_estimate=cost(4),
        name="pixels",
    )(patterns, detector_gain.reshape(1, pixels), background.reshape(1, pixels))
    corrected = corrected.reshape(tiles, TILE, count)
    bins = bin_map.reshape(tiles // 16, 16, 16, 16).transpose(0, 2, 1, 3).reshape(tiles, TILE)
    table, slot_rows, span = pl.pallas_call(
        slots_kernel,
        out_shape=(
            jax.ShapeDtypeStruct((RAD // 2, PAIR), jnp.int32),
            jax.ShapeDtypeStruct((tiles, TILE), jnp.int32),
            jax.ShapeDtypeStruct((tiles, 128), jnp.int32),
        ),
        in_specs=[vmem()] * 3,
        out_specs=(vmem(),) * 3,
        cost_estimate=cost(3),
        name="slots",
    )(present, other, bins)
    mine, theirs = pl.pallas_call(
        binning_kernel,
        out_shape=(
            jax.ShapeDtypeStruct((half, ROOM), F32),
            jax.ShapeDtypeStruct((half, ROOM), BF16),
        ),
        in_specs=[smem(), smem(), vmem(), vmem()],
        out_specs=(vmem(),) * 2,
        scratch_shapes=[pltpu.VMEM((ROOM + WINDOW, count), F32), pltpu.VMEM((count, ROOM), F32)],
        compiler_params=pltpu.CompilerParams(vmem_limit_bytes=24 * MIB),
        cost_estimate=cost(6),
        name="binning",
    )(core, span, slot_rows, corrected)
    message, spare = pl.pallas_call(
        combine_kernel,
        out_shape=(
            jax.ShapeDtypeStruct((half, SEG + PAIR), BF16),
            jax.ShapeDtypeStruct((half, ROOM - SEG), BF16),
        ),
        in_specs=[vmem()] * 3,
        out_specs=(vmem(),) * 2,
        cost_estimate=cost(1),
        name="combine",
    )(mine, swap(theirs), table)

    messages = [along(message, by) for by in range(1, chips)]
    step = hops(spare, [(1, 0), (2, 3)])
    traded = hops(spare, [(1, 2), (2, 1)])
    far_part = hops(spare, [(1, 3), (2, 0)])

    def spread(group):
        return group, across(group, 1), across(group, 2)

    def diagonal(held, after):
        upper, lower = halves(held[1], held[2], after)
        return (*held, across(upper, 2), across(lower, 1)), [upper, lower]

    size = best_picks.shape[0] * count
    turned, local, ranks, crowd = pl.pallas_call(
        picks_kernel,
        out_shape=(
            jax.ShapeDtypeStruct((2 * KEPT, BINS), BF16),
            jax.ShapeDtypeStruct((8, 4 * half), jnp.int32),
            jax.ShapeDtypeStruct((8, 4 * half), jnp.int32),
            jax.ShapeDtypeStruct((8, 128), jnp.int32),
        ),
        in_specs=[smem()] + [vmem()] * 4,
        out_specs=(vmem(),) * 4,
        compiler_params=pltpu.CompilerParams(vmem_limit_bytes=GRANT * MIB),
        cost_estimate=cost(30),
        name="picks",
    )(place, best_picks.reshape(1, size), best_picks.reshape(size, 1), templates, spare)
    group, tables, windows, ranges, full = arrive(
        True, chip, table, [message, messages[0], messages[2]], spare, step, [], [crowd]
    )
    near = spread(group)
    own, token = columns(len(GROUPS[0]), ranges, tables, templates, turned, [])
    near, gate = diagonal(near, [token])
    group, tables_far, windows_far, ranges, full = arrive(
        False, chip, tables, [messages[1]], traded, far_part, [full, crowd], [token]
    )
    far = spread(group)
    own_far, token = columns(len(GROUPS[1]), ranges, tables_far, templates, turned, gate)
    squares = pl.pallas_call(
        squares_kernel,
        out_shape=jax.ShapeDtypeStruct((8, half), F32),
        in_specs=[smem()] * 3 + [vmem()] * 5,
        out_specs=vmem(),
        scratch_shapes=[pltpu.VMEM((RAD // 8, half, PAIR), F32)],
        compiler_params=pltpu.CompilerParams(vmem_limit_bytes=GRANT * MIB),
        cost_estimate=cost(2),
        name="squares",
    )(place, windows, windows_far, tables, tables_far, near[0], far[0], token)
    far, gate = diagonal(far, [squares])
    total = score(True, False, rows, own, swap(own), near, None, (), gate, 60)
    blocks = score(
        False, True, rows, own_far, swap(own_far), far, total, (place, local, ranks, squares), (), 5
    )
    blocks = lax.all_to_all(blocks, ("section", "orient"), 0, 0)
    top, refined = pl.pallas_call(
        final_kernel,
        out_shape=(
            jax.ShapeDtypeStruct((1, count, TOPK), F32),
            jax.ShapeDtypeStruct((1, count // orients, 3), F32),
        ),
        in_specs=[smem(), vmem()],
        out_specs=(vmem(), vmem()),
        scratch_shapes=[pltpu.VMEM((TOPK, count), F32), pltpu.VMEM((count, TOPK), F32)],
        cost_estimate=cost(2),
        name="final",
    )(place, blocks)

    return lax.cond(
        full[0, 0] > 0,
        lambda: dense_body(
            patterns, detector_gain, background, bin_map, templates, best_picks
        ),
        lambda: (top, refined),
    )


def solution(mesh):
    sizes = dict(mesh.shape)
    fits = sizes["section"] == 4 and sizes["orient"] == 8
    return jax.shard_map(
        compact_body if fits else dense_body,
        mesh=mesh,
        in_specs=(
            P("section", None, "orient"),
            P("orient"),
            P("orient"),
            P("orient"),
            P(("section", "orient"), None),
            P(),
        ),
        out_specs=(P("section", None, None), P("section", "orient", None)),
        check_vma=False,
    )
```

```python
import functools

import jax
import jax.numpy as jnp
from jax import lax
from jax.experimental import pallas as pl
from jax.experimental.pallas import tpu as pltpu
from jax.sharding import PartitionSpec as P

RAD = 64
ANG = 192
TOPK = 8
REACH = 1


EPS = 1e-06
BLOCK_ROWS = 512


def shifted(x, axis, by):
    count = lax.axis_size(axis)
    return lax.ppermute(x, axis, [(i, (i + by) % count) for i in range(count)])


def merged_2(part, axis, combine):
    gathered = lax.all_gather(part, axis)

    def take(source):
        return lax.dynamic_index_in_dim(gathered, source, 0, False)

    return lax.fori_loop(
        1, lax.axis_size(axis), lambda source, state: combine(state, take(source)), take(0)
    )


def bin_block(corrected, bin_map, first, length):
    targets = first + lax.iota(jnp.int32, length)
    onehot = (bin_map[None, :] == targets[:, None]).astype(jnp.bfloat16)
    return lax.dot_general(
        onehot, corrected, (((1,), (1,)), ((), ())), preferred_element_type=jnp.float32
    )


def bin_rows(corrected, bin_map, length):
    blocks = 1
    while length // blocks > BLOCK_ROWS and length % (2 * blocks) == 0:
        blocks = blocks * 2
    height = length // blocks
    starts = height * lax.iota(jnp.int32, blocks)
    stacked = lax.map(lambda begin: bin_block(corrected, bin_map, begin, height), starts)
    return stacked.reshape(length, corrected.shape[0])


def merge_best(first_best, second_best):
    return lax.top_k(jnp.concatenate([first_best, second_best], axis=-1), TOPK)[0]


def score_batch(features, templates, wanted, group_base):
    scores = lax.dot_general(
        features, templates, (((0,), (1,)), ((), ())), preferred_element_type=jnp.float32
    )
    best = lax.top_k(scores, TOPK)[0]
    local = wanted - group_base
    count = templates.shape[0]
    owned = (local >= 0) & (local < count)
    chosen = jnp.take(templates, jnp.clip(local, 0, count - 1), axis=0)
    width = features.shape[1]
    chosen = chosen.reshape(width, RAD, ANG)
    grid = features.T.reshape(width, RAD, ANG)
    columns = []
    for offset in range(-REACH, REACH + 1):
        rolled = jnp.roll(chosen, -offset, axis=2)
        columns.append(jnp.sum(grid.astype(jnp.float32) * rolled.astype(jnp.float32), axis=(1, 2)))
    refined = jnp.where(owned[:, None], jnp.stack(columns, axis=1), 0.0)
    return (best, refined)


def dense_body(patterns, detector_gain, background, bin_map, templates, best_picks):
    sections = lax.axis_size("section")
    orients = lax.axis_size("orient")
    section_index = lax.axis_index("section")
    orient_index = lax.axis_index("orient")
    features_total = RAD * ANG
    corrected = ((patterns[0].astype(jnp.float32) - background) * detector_gain).astype(
        jnp.bfloat16
    )
    whole = lax.psum(bin_rows(corrected, bin_map, features_total), "orient")
    squares = jnp.sum(whole * whole, axis=0)
    features = (whole * lax.rsqrt(squares / features_total + EPS)).astype(jnp.bfloat16)
    group_base = (section_index * orients + orient_index) * templates.shape[0]
    held = features
    running_best = None
    running_refined = None
    for turn in range(sections):
        batch = (section_index + sections - turn) % sections
        wanted = lax.dynamic_index_in_dim(best_picks, batch, 0, keepdims=False)
        best, refined = score_batch(held, templates, wanted, group_base)
        if turn > 0:
            best = merge_best(running_best, best)
            refined = running_refined + refined
        packed = shifted(jnp.concatenate([best, refined], axis=1), "section", 1)
        running_best = packed[:, :TOPK]
        running_refined = packed[:, TOPK:]
        if turn + 1 < sections:
            held = shifted(held, "section", 1)
    merged = merged_2(running_best, "orient", merge_best)
    shares = lax.psum_scatter(running_refined, "orient", scatter_dimension=0, tiled=True)
    return (merged[None], shares[None])


BINS = RAD * ANG
SEG = 1792
SEGS = 6
ROOM = 2 * SEG
TILE = 256
WINDOW = 512
GROUPS = ((0, 1, 3, 4), (2, 5))
KEPT = 32
SQUARE = 384
GRANT = 22
SMALL = 10
PAIR = 2 * ANG
MIB = 1 << 20
F32 = jnp.float32
BF16 = jnp.bfloat16


def vmem():
    return pl.BlockSpec(memory_space=pltpu.VMEM)


def smem():
    return pl.BlockSpec(memory_space=pltpu.SMEM)


def cost(micros):
    return pl.CostEstimate(
        flops=int(micros * 1.1e9), bytes_accessed=int(micros * 1e6), transcendentals=0
    )


def dot_nt(a, b):
    return lax.dot_general(a, b, (((1,), (1,)), ((), ())), preferred_element_type=F32)


def dot_nn(a, b):
    return lax.dot_general(a, b, (((1,), (0,)), ((), ())), preferred_element_type=F32)


def polar(row):
    value = row.astype(F32)
    radial = jnp.floor((value + 0.5) * (1.0 / ANG))
    return radial, value - radial * ANG


def members(values, count):
    ids = lax.broadcasted_iota(jnp.int32, (count, values.shape[1]), 0).astype(F32)
    return ids == values


def presence_kernel(bins_ref, counts_ref):
    counts = jnp.zeros((ANG, RAD), F32)
    for line in range(0, bins_ref.shape[0], 2):
        parts = [bins_ref[line : line + 1, :], bins_ref[line + 1 : line + 2, :]]
        radial, angle = polar(jnp.concatenate(parts, axis=1))
        counts += dot_nt(
            members(angle, ANG).astype(BF16), members(radial, RAD).astype(BF16)
        )
    counts_ref[...] = (counts > 0.5).astype(F32)


def below(size):
    rows = lax.broadcasted_iota(jnp.int32, (size, size), 0)
    cols = lax.broadcasted_iota(jnp.int32, (size, size), 1)
    return rows, cols


def edges(table, offset):
    pairs = table.shape[0]
    valid = (table >= 0).astype(F32).astype(BF16)
    count = dot_nn(valid, jnp.ones((PAIR, 128), BF16))
    rows, cols = below(pairs)
    low_end = count - 256 * jnp.floor(count * (1.0 / 256))
    high_end = jnp.floor(count * (1.0 / 256))
    sums = (cols <= rows).astype(BF16)
    ends = 256 * dot_nn(sums, high_end.astype(BF16)) + dot_nn(sums, low_end.astype(BF16))
    begins = ends - count
    lane = lax.broadcasted_iota(jnp.int32, count.shape, 1)
    wide = SEG // 128
    first = jnp.clip(jnp.floor((begins - offset) * (1.0 / 128)), 0, wide - SQUARE // 128)
    last = jnp.clip(jnp.floor((ends - offset + 127) * (1.0 / 128)), 0, wide)
    windows = jnp.where(lane == 0, first, jnp.where(count > 0, last, 0.0))
    at = (lane % 64).astype(F32) * 256 + offset
    found = jnp.where(lane < 64, (ends <= at).astype(F32), (begins < at + 256).astype(F32))
    ranges = jnp.sum(found, axis=0, keepdims=True)
    ranges = jnp.where(lane[:1] == 127, ends[pairs - 1 :], ranges)
    return windows.astype(jnp.int32), ranges.astype(jnp.int32), ends


def slots_kernel(own_ref, other_ref, bins_ref, table_ref, rows_ref, span_ref):
    present = jnp.maximum(own_ref[...], other_ref[...])
    held = present.astype(BF16)
    rows, cols = below(ANG)
    within = dot_nn((cols < rows).astype(BF16), held)
    totals = dot_nn(jnp.ones((ANG, ANG), BF16), held)
    rows, cols = below(RAD)
    before = dot_nn(totals.astype(BF16), (rows < cols).astype(BF16))
    slots = within + before
    high = jnp.floor(slots * (1.0 / 64))
    low = slots - 64 * high
    high = high.astype(BF16)
    low = low.astype(BF16)
    both = jnp.concatenate([high, low])
    line = lax.broadcasted_iota(jnp.int32, (RAD // 2, RAD), 0)
    ring = lax.broadcasted_iota(jnp.int32, (RAD // 2, RAD), 1)
    for side in range(2):
        pick = (ring == 2 * line + side).astype(BF16)
        turned = 64 * dot_nt(pick, high) + dot_nt(pick, low)
        table_ref[:, side * ANG : (side + 1) * ANG] = jnp.where(
            dot_nt(pick, held) > 0.5, turned, -1.0
        ).astype(jnp.int32)
    for tile in range(bins_ref.shape[0]):
        radial, angle = polar(bins_ref[tile : tile + 1, :])
        ring = members(radial, RAD).astype(BF16)
        value = dot_nn(both, ring)
        value = 64 * value[:ANG] + value[ANG:]
        value = jnp.sum(jnp.where(members(angle, ANG), value, 0.0), axis=0, keepdims=True)
        rows_ref[tile : tile + 1, :] = value.astype(jnp.int32)
    found = rows_ref[...]
    first = jnp.min(found, axis=1, keepdims=True)
    last = jnp.max(found, axis=1, keepdims=True)
    lane = lax.broadcasted_iota(jnp.int32, (found.shape[0], 128), 1)
    span_ref[...] = jnp.where(lane == 0, first, last)


def pixels_kernel(patterns_ref, gain_ref, background_ref, out_ref):
    value = (patterns_ref[0].astype(F32) - background_ref[...]) * gain_ref[...]
    out_ref[...] = value.astype(BF16).T


def binning_kernel(
    core_ref, span_ref, rows_ref, pixels_ref, mine_ref, theirs_ref, sums, turned
):
    sums[...] = jnp.zeros_like(sums)
    across = 256 // 16

    def add(tile, at):
        down = (tile // across) * 16
        right = (tile % across) * 16
        block = pixels_ref[pl.ds(down, 16), pl.ds(right, 16), :].reshape(TILE, 128)
        row = rows_ref[pl.ds(tile, 1), :]
        ids = lax.broadcasted_iota(jnp.int32, (WINDOW, TILE), 0)
        hits = (ids == row - at).astype(BF16)
        sums[pl.ds(at, WINDOW), :] += dot_nn(hits, block)

    def base_of(tile):
        return pl.multiple_of(jnp.minimum(span_ref[tile, 0], ROOM) // 8 * 8, 8)

    tiles = rows_ref.shape[0]
    for tile in range(tiles):
        add(tile, base_of(tile))

    def one_tile(tile, _):
        base = base_of(tile)
        stop = jnp.minimum(span_ref[tile, 1] + 1, ROOM)

        def one_window(step, _):
            add(tile, pl.multiple_of(base + step * WINDOW, 8))
            return 0

        lax.fori_loop(1, (stop - base + WINDOW - 1) // WINDOW, one_window, 0)
        return 0

    lax.fori_loop(0, tiles, one_tile, 0)
    for block in range(ROOM // 128):
        turned[:, block * 128 : (block + 1) * 128] = sums[
            block * 128 : (block + 1) * 128, :
        ].T
    core = core_ref[0]
    half = turned.shape[0] // 2
    mine_ref[...] = turned[pl.ds(pl.multiple_of(core * half, half), half), :]
    theirs_ref[...] = turned[
        pl.ds(pl.multiple_of((1 - core) * half, half), half), :
    ].astype(BF16)


def combine_kernel(
    mine_ref, theirs_ref, table_ref, message_ref, spare_ref
):
    total = (mine_ref[...] + theirs_ref[...].astype(F32)).astype(BF16)
    spare_ref[...] = total[:, SEG:]
    message_ref[:, :SEG] = total[:, :SEG]
    table = table_ref[...].astype(F32)
    high = jnp.floor(table * (1.0 / 64))
    pairs = table.shape[0]
    message_ref[:pairs, SEG:] = high.astype(BF16)
    message_ref[pairs:, SEG:] = (table - 64 * high).astype(BF16)


def sum_rows(mask, value):
    return jnp.sum(jnp.where(mask, value, 0.0), axis=0, keepdims=True)


def sum_lanes(mask, value):
    return jnp.sum(jnp.where(mask, value, 0.0), axis=1, keepdims=True)


def place_picks(place_ref, row_ref, col_ref, rows, local_ref, rank_ref, crowd_ref):
    section, orient, orients = place_ref[0], place_ref[1], place_ref[2]
    row = row_ref[...].astype(F32)
    col = col_ref[...].astype(F32)
    size = row.shape[1]
    i = lax.broadcasted_iota(jnp.int32, (size, size), 0)
    j = lax.broadcasted_iota(jnp.int32, (size, size), 1)
    equal = col == row
    first_row = (sum_rows(equal & (i < j), 1.0) == 0).astype(F32)
    first_col = (sum_lanes(equal & (j < i), 1.0) == 0).astype(F32)
    owner_row = jnp.floor((row + 0.5) * (1.0 / rows))
    owner_col = jnp.floor((col + 0.5) * (1.0 / rows))
    same = owner_col == owner_row
    rank_row = sum_rows(same & (i < j), first_col)
    rank_col = sum_lanes(same & (j < i), first_row)
    rank_of = sum_rows(equal, first_col * rank_col)
    crowd_ref[...] = jnp.broadcast_to(
        jnp.max(rank_of, axis=1, keepdims=True), crowd_ref.shape
    ).astype(jnp.int32)
    me = section * orients + orient
    base = (me * rows).astype(F32)
    ids = lax.broadcasted_iota(jnp.int32, (KEPT, size), 0).astype(F32)
    chosen = (first_row > 0) & (owner_row == me.astype(F32)) & (rank_row == ids)
    wanted = sum_lanes(chosen, row - base + 1) - 1
    half = 64
    core = orient % 2
    local_ref[...] = jnp.zeros_like(local_ref)
    rank_ref[...] = jnp.zeros_like(rank_ref)
    lanes = lax.broadcasted_iota(jnp.int32, (1, size), 1)
    for by in range(4):
        start = (section ^ by) * 2 * half + core * half
        shift = (size - start) % size
        there = slice(by * half, (by + 1) * half)
        local_ref[2:3, there] = pltpu.roll(row, shift, 1)[:, :half].astype(jnp.int32)
        rank_ref[2:3, there] = pltpu.roll(rank_of, shift, 1)[:, :half].astype(jnp.int32)
    for side in range(2):
        owner = section * orients + (orient ^ side)
        local = local_ref[2:3, :] - owner * rows
        held = (local >= 0) & (local < rows)
        local_ref[side : side + 1, :] = jnp.where(held, local, -1)
        rank_ref[side : side + 1, :] = jnp.where(held, rank_ref[2:3, :], -1)
    return wanted


def turn_picks(wanted, templates_ref, out_ref):
    rows = templates_ref.shape[0]
    ids = lax.broadcasted_iota(jnp.int32, (KEPT, rows), 1).astype(F32)
    select = (ids == wanted).astype(BF16)
    lane = lax.broadcasted_iota(jnp.int32, (KEPT, PAIR), 1)
    for pair in range(RAD // 2):
        cols = slice(pair * PAIR, (pair + 1) * PAIR)
        taken = dot_nn(select, templates_ref[:, cols])
        later = jnp.where(
            lane % ANG == 0, pltpu.roll(taken, ANG + 1, 1), pltpu.roll(taken, 1, 1)
        )
        sooner = jnp.where(
            lane % ANG == ANG - 1,
            pltpu.roll(taken, ANG - 1, 1),
            pltpu.roll(taken, PAIR - 1, 1),
        )
        out_ref[:KEPT, cols] = later.astype(BF16)
        out_ref[KEPT:, cols] = sooner.astype(BF16)


def permute_columns(seg, offset, range_ref, table_ref, templates_ref, turned_ref, out_ref):
    wide = 5

    def block(pair, pairs):
        col = pl.ds(pl.multiple_of(pair * PAIR, 128), pairs * PAIR)
        return jnp.concatenate([templates_ref[:, col], turned_ref[:, col]], axis=0)

    def hits(pair, at):
        row = table_ref[seg, pl.ds(pair, 1), :]
        ids = lax.broadcasted_iota(jnp.int32, (256, PAIR), 0)
        return (ids == row - at).astype(BF16)

    def start_of(window):
        return jnp.minimum(range_ref[seg, window], RAD // 2 - wide)

    for window in range(SEG // 256):
        at = offset + window * 256
        start = start_of(window)
        mask = jnp.concatenate([hits(start + i, at) for i in range(wide)], axis=1)
        out_ref[0, :, window * 256 : (window + 1) * 256] = dot_nt(
            block(start, wide), mask
        ).astype(BF16)

    def one_window(window, _):
        to = pl.ds(pl.multiple_of(window * 256, 256), 256)

        def one_pair(pair, _):
            more = dot_nt(block(pair, 1), hits(pair, offset + window * 256))
            out_ref[0, :, to] = (out_ref[0, :, to].astype(F32) + more).astype(BF16)
            return 0

        lax.fori_loop(start_of(window) + wide, range_ref[seg, 64 + window], one_pair, 0)
        return 0

    more = 0
    for window in range(SEG // 256):
        more = jnp.maximum(more, range_ref[seg, 64 + window] - start_of(window))

    @pl.when(more > wide)
    def _():
        lax.fori_loop(0, SEG // 256, one_window, 0)


def picks_kernel(
    place_ref, row_ref, col_ref, templates_ref, _, turned_ref, local_ref, rank_ref, crowd_ref
):
    rows = templates_ref.shape[0]
    wanted = place_picks(place_ref, row_ref, col_ref, rows, local_ref, rank_ref, crowd_ref)
    turn_picks(wanted, templates_ref, turned_ref)


def columns_kernel(range_ref, table_ref, templates_ref, turned_ref, *refs):
    out_ref, token_ref, held_ref, arrived = refs[-4:]
    seg = pl.program_id(0)

    @pl.when(seg == 0)
    def _():
        copy = pltpu.make_async_copy(templates_ref, held_ref, arrived)
        copy.start()
        token_ref[...] = jnp.zeros_like(token_ref)
        copy.wait()

    offset = jnp.where(seg == pl.num_programs(0) - 1, SEG, 0)
    permute_columns(seg, offset, range_ref, table_ref, held_ref, turned_ref, out_ref)


def whole(shape):
    return pl.BlockSpec(shape, lambda i: (0,) * len(shape))


def each(shape):
    return pl.BlockSpec((1, *shape), lambda i: (i,) + (0,) * len(shape))


def columns(count, ranges, tables, templates, turned, after):
    height = templates.shape[0] + turned.shape[0]
    return pl.pallas_call(
        columns_kernel,
        grid=(count,),
        out_shape=(
            jax.ShapeDtypeStruct((count, height, SEG), BF16),
            jax.ShapeDtypeStruct((8, 128), F32),
        ),
        in_specs=[
            smem(),
            whole(tables.shape),
            pl.BlockSpec(memory_space=pl.ANY),
            whole(turned.shape),
        ]
        + [vmem()] * len(after),
        out_specs=(each((height, SEG)), whole((8, 128))),
        scratch_shapes=[pltpu.VMEM(templates.shape, BF16), pltpu.SemaphoreType.DMA],
        compiler_params=pltpu.CompilerParams(vmem_limit_bytes=GRANT * MIB),
        cost_estimate=cost(30 * count),
        name="columns",
    )(ranges, tables, templates, turned, *after)


def arrive_kernel(first, chip_ref, held_ref, *refs):
    group_ref, table_ref, window_ref, range_ref, full_ref = refs[-5:]
    messages = refs[:3] if first else refs[:1]
    mine_ref, came_ref = refs[len(messages) : len(messages) + 2]
    pairs = table_ref.shape[1]
    chip = chip_ref[0]
    inner = (chip == 1) | (chip == 2)
    for at, ref in enumerate(messages):
        group_ref[at] = ref[:, :SEG]
        high = ref[:pairs, SEG:].astype(F32)
        low = ref[pairs:, SEG:].astype(F32)
        table_ref[at] = (64 * high + low).astype(jnp.int32)
    last = len(messages)

    @pl.when(inner)
    def _():
        group_ref[last] = mine_ref[...]

    @pl.when(jnp.logical_not(inner))
    def _():
        group_ref[last] = came_ref[...]

    if first:
        table = jnp.where(chip == 0, table_ref[2], jnp.where(chip == 3, table_ref[1], table_ref[0]))
    else:
        table = jnp.where(chip == 1, held_ref[2], jnp.where(chip == 2, held_ref[1], table_ref[0]))
    table_ref[last] = table
    range_ref[...] = jnp.zeros_like(range_ref)
    for at in range(last + 1):
        windows, ranges, _ = edges(table_ref[at], SEG if at == last else 0)
        window_ref[at] = windows
        range_ref[at : at + 1, :] = ranges
    chips = [chip, (chip + 3) % 4, (chip + 1) % 4] if first else [(chip + 2) % 4]
    totals = [range_ref[at : at + 1, :] for at in range(len(chips))]
    full = jnp.zeros((1, 128), jnp.int32)
    for held, total in zip(chips, totals, strict=True):
        room = jnp.where((held == 1) | (held == 2), ROOM, SEG)
        full = jnp.maximum(full, (total > room).astype(jnp.int32))
    if not first:
        near_ref, crowd_ref = refs[len(messages) + 2 : len(messages) + 4]
        full = jnp.maximum(full, near_ref[0:1, :])
        full = jnp.maximum(full, (crowd_ref[0:1, :] >= KEPT).astype(jnp.int32))
    lane = lax.broadcasted_iota(jnp.int32, (8, 128), 1)
    full = jnp.where(lane == 127, jnp.broadcast_to(full, (8, 128)), 0)
    full_ref[...] = jnp.broadcast_to(jnp.max(full, axis=1, keepdims=True), (8, 128))


def arrive(first, chip, held, messages, mine, came, extra, after):
    count = len(messages) + 1
    half = mine.shape[0]
    pairs = RAD // 2
    return pl.pallas_call(
        functools.partial(arrive_kernel, first),
        out_shape=(
            jax.ShapeDtypeStruct((count, half, SEG), BF16),
            jax.ShapeDtypeStruct((count, pairs, PAIR), jnp.int32),
            jax.ShapeDtypeStruct((count, pairs, 128), jnp.int32),
            jax.ShapeDtypeStruct((8, 128), jnp.int32),
            jax.ShapeDtypeStruct((8, 128), jnp.int32),
        ),
        in_specs=[smem()]
        + [vmem()] * (len(messages) + 3 + len(extra))
        + [vmem()] * len(after),
        out_specs=(vmem(),) * 5,
        cost_estimate=cost(1),
        compiler_params=pltpu.CompilerParams(vmem_limit_bytes=SMALL * MIB),
        name="arrive",
    )(chip, held, *messages, mine, came, *extra, *after)


def halves_kernel(x_ref, y_ref, *refs):
    upper_ref, lower_ref = refs[-2:]
    size = upper_ref.shape[1]
    upper_ref[...] = x_ref[:, :size]
    lower_ref[...] = y_ref[:, size:]


def halves(x, y, after):
    shape = jax.ShapeDtypeStruct((x.shape[0], x.shape[1] // 2, x.shape[2]), x.dtype)
    return pl.pallas_call(
        halves_kernel,
        out_shape=(shape, shape),
        in_specs=[vmem(), vmem()] + [vmem()] * len(after),
        out_specs=(vmem(), vmem()),
        cost_estimate=cost(1),
        compiler_params=pltpu.CompilerParams(vmem_limit_bytes=SMALL * MIB),
        name="halves",
    )(x, y, *after)


def squares_kernel(place_ref, *refs):
    count = len(GROUPS)
    windows, tables, lists = refs[:count], refs[count : 2 * count], refs[2 * count : 3 * count]
    out_ref, dense_ref = refs[-2:]
    share = tables[0].shape[1] // 4
    half = lists[0].shape[1]
    first = place_ref[1] // 2 * share
    parts = [
        (windows[group], tables[group], lists[group], at, 0 if seg < 4 else SEG)
        for group, segs in enumerate(GROUPS)
        for at, seg in enumerate(segs)
    ]

    def hits(table, at, offset, pair, begin, size):
        ids = lax.broadcasted_iota(jnp.int32, (size, PAIR), 0)
        return (ids == table[at, pl.ds(pair, 1), :] - offset - begin).astype(BF16)

    for step in range(share):
        pair = first + step
        masks = []
        values = []
        for window, table, ref, at, offset in parts:
            begin = pl.multiple_of(window[at, pair, 0] * 128, 128)
            masks.append(hits(table, at, offset, pair, begin, SQUARE))
            values.append(ref[at, :, pl.ds(begin, SQUARE)])
        dense_ref[step] = dot_nn(jnp.concatenate(values, axis=1), jnp.concatenate(masks, axis=0))

    def one_pair(step, _):
        pair = first + step
        more = 0
        for window, _, _, at, _ in parts:
            more = jnp.maximum(more, window[at, pair, 1] - window[at, pair, 0])

        @pl.when(more > SQUARE // 128)
        def _():
            for window, table, ref, at, offset in parts:

                def one_window(index, _):
                    begin = pl.multiple_of(index * 128, 128)
                    dense_ref[step] += dot_nn(
                        ref[at, :, pl.ds(begin, 128)], hits(table, at, offset, pair, begin, 128)
                    )
                    return 0

                lax.fori_loop(
                    window[at, pair, 0] + SQUARE // 128, window[at, pair, 1], one_window, 0
                )

        return 0

    lax.fori_loop(0, share, one_pair, 0)
    ones = jnp.ones((8, PAIR), BF16)
    total = jnp.zeros((8, half), F32)
    for step in range(share):
        square = dense_ref[step] * dense_ref[step]
        high = square.astype(BF16)
        low = (square - high.astype(F32)).astype(BF16)
        total = total + dot_nt(ones, high) + dot_nt(ones, low)
    out_ref[...] = total


def insert_sorted(best, value):
    out = []
    for held in best:
        out.append(jnp.maximum(held, value))
        value = jnp.minimum(held, value)
    return out


def merge_sorted(first, second):
    count = len(first)
    both = [jnp.maximum(first[i], second[count - 1 - i]) for i in range(count)]
    gap = count // 2
    while gap:
        for i in range(count):
            if i & gap == 0:
                high = jnp.maximum(both[i], both[i + gap])
                low = jnp.minimum(both[i], both[i + gap])
                both[i], both[i + gap] = high, low
        gap //= 2
    return both


def score_kernel(first, last, rows, *refs):
    count = 0 if first else 1
    own_ref, pair_ref, z_ref, x_ref, y_ref, d_ref, e_ref = refs[:7]
    rest = refs[7:]
    if not first:
        so_far_ref, rest = rest[0], rest[1:]
    if last:
        place_ref, local_ref, rank_ref, squares_ref, out_ref, total, lists, packed = rest
    else:
        out_ref, lists = rest[-2:]
        total = out_ref
    half = z_ref.shape[1]
    lists[0:half, :] = z_ref[0]
    lists[half : 2 * half, :] = x_ref[0]
    lists[2 * half : 3 * half, :] = y_ref[0]
    lists[3 * half : 3 * half + half // 2, :] = d_ref[0]
    lists[3 * half + half // 2 :, :] = e_ref[0]

    @pl.when(pl.program_id(0) == 0)
    def _():
        total[...] = jnp.zeros_like(total) if first else so_far_ref[...]

    for side, ref in enumerate((own_ref, pair_ref)):
        total[side] += dot_nt(ref[0], lists[...])
    if last:

        @pl.when(pl.program_id(0) == pl.num_programs(0) - 1)
        def _():
            pick_out(
                rows, half, total, place_ref, local_ref, rank_ref, squares_ref, out_ref, packed
            )


def pick_out(rows, half, total, place_ref, local_ref, rank_ref, squares_ref, out_ref, packed):
    width = total.shape[2]
    low = jnp.full((8, width), -jnp.inf, F32)
    best = [low] * TOPK
    for side in range(2):
        def step(at, best):
            return tuple(
                insert_sorted(best, total[side, pl.ds(pl.multiple_of(at * 8, 8), 8), :])
            )

        best = lax.fori_loop(0, rows // 8, step, tuple(best), unroll=2)
    for turn in (4, 2, 1):
        best = merge_sorted(best, [pltpu.roll(part, turn, 0) for part in best])
    for place in range(TOPK):
        packed[place : place + 1, :] = best[place][0:1, :]
    picked = [jnp.zeros((1, width), F32) for _ in range(3)]
    for side in range(2):
        ids = lax.broadcasted_iota(jnp.int32, (rows, width), 0)
        picked[1] += jnp.sum(
            jnp.where(ids == local_ref[side : side + 1, :], total[side, :rows, :], 0.0),
            axis=0,
            keepdims=True,
        )
        ids = lax.broadcasted_iota(jnp.int32, (KEPT, width), 0)
        hit = ids == rank_ref[side : side + 1, :]
        picked[0] += jnp.sum(
            jnp.where(hit, total[side, rows : rows + KEPT, :], 0.0), axis=0, keepdims=True
        )
        picked[2] += jnp.sum(
            jnp.where(hit, total[side, rows + KEPT :, :], 0.0), axis=0, keepdims=True
        )
    packed[TOPK:, :] = jnp.zeros((8, width), F32)
    for place in range(3):
        packed[TOPK + place : TOPK + place + 1, :] = picked[place]
    packed[TOPK + 3 : TOPK + 4, :half] = squares_ref[0:1, :]
    section, core, orients = place_ref[0], place_ref[1] % 2, place_ref[2]
    for by in range(4):
        there = slice(by * half, (by + 1) * half)
        block = jnp.concatenate([packed[:TOPK, there], packed[TOPK:, there]], axis=1)
        block = pltpu.roll(block, core * half, 1)
        for orient in range(8):
            out_ref[(section ^ by) * orients + orient] = block


def score(first, last, rows, own, pair, lists, so_far, extra, after, micros):
    count, height, _ = own.shape
    width = 4 * lists[0].shape[1]
    scratch = [pltpu.VMEM((width, SEG), BF16)]
    if last:
        scratch = [pltpu.VMEM((2, height, width), F32)] + scratch
        scratch.append(pltpu.VMEM((16, width), F32))
        shape = (32, TOPK, 128)
    else:
        shape = (2, height, width)
    args = [own, pair, *lists]
    specs = [each(arg.shape[1:]) for arg in args]
    if not first:
        args.append(so_far)
        specs.append(whole(so_far.shape))
    if last:
        specs = specs + [smem()] + [vmem()] * 3
    args.extend(extra)
    return pl.pallas_call(
        functools.partial(score_kernel, first, last, rows),
        grid=(count,),
        out_shape=jax.ShapeDtypeStruct(shape, F32),
        in_specs=specs + [vmem()] * len(after),
        out_specs=whole(shape),
        scratch_shapes=scratch,
        compiler_params=pltpu.CompilerParams(vmem_limit_bytes=GRANT * MIB),
        cost_estimate=cost(micros),
        name="score",
    )(*args, *after)


def final_kernel(place_ref, blocks_ref, top_ref, refined_ref, lines, turned):
    count = blocks_ref.shape[0]
    source = lax.broadcasted_iota(jnp.int32, (count, 128), 0)
    lane = lax.broadcasted_iota(jnp.int32, (count, 128), 1)
    best_here = (source % 2) == (lane // 64)
    best = []
    rest = []
    for place in range(TOPK):
        row = blocks_ref[:, place, :]
        best.append(jnp.where(best_here, row, -jnp.inf))
        if place < 4:
            rest.append(jnp.sum(jnp.where(best_here, 0.0, row), axis=0, keepdims=True))
    while count > 8:
        count //= 2
        best = merge_sorted([part[:count] for part in best], [part[count:] for part in best])
    for turn in (4, 2, 1):
        best = merge_sorted(best, [pltpu.roll(part, turn, 0) for part in best])
    rest = [pltpu.roll(row, 64, 1) for row in rest]
    factor = lax.rsqrt(rest[3] / BINS + EPS)
    for place in range(TOPK):
        lines[place : place + 1, :] = best[place][0:1, :] * factor
    top_ref[0] = lines[...].T
    for place in range(3):
        lines[place : place + 1, :] = rest[place] * factor
    turned[...] = lines[...].T
    share = refined_ref.shape[1]
    first = pl.multiple_of(place_ref[1] * share, share)
    refined_ref[0] = turned[pl.ds(first, share), :3]


def compact_body(patterns, detector_gain, background, bin_map, templates, best_picks):
    orients = lax.axis_size("orient")
    chips = orients // 2
    section = lax.axis_index("section")
    orient = lax.axis_index("orient")
    place = jnp.stack([section, orient, jnp.full_like(orient, orients)]).astype(jnp.int32)
    core = (orient % 2).reshape(1).astype(jnp.int32)
    chip = (orient // 2).reshape(1).astype(jnp.int32)
    rows = templates.shape[0]
    count = patterns.shape[1]
    half = count // 2
    pixels = patterns.shape[2]

    def swap(x):
        return lax.ppermute(x, "orient", [(i, i ^ 1) for i in range(orients)])

    def along(x, by):
        return lax.ppermute(x, "orient", [(i, (i + 2 * by) % orients) for i in range(orients)])

    def hops(x, pairs):
        return lax.ppermute(
            x, "orient", [(2 * i + c, 2 * j + c) for i, j in pairs for c in range(2)]
        )

    def across(x, by):
        return lax.ppermute(x, "section", [(i, i ^ by) for i in range(4)])

    tiles = pixels // TILE
    lines = bin_map.reshape(2 * tiles, TILE // 2)
    present = pl.pallas_call(
        presence_kernel,
        out_shape=jax.ShapeDtypeStruct((ANG, RAD), F32),
        in_specs=[vmem()],
        out_specs=vmem(),
        cost_estimate=cost(2),
        compiler_params=pltpu.CompilerParams(vmem_limit_bytes=SMALL * MIB),
        name="presence",
    )(lines)
    other = swap(present)
    steps = 8
    corrected = pl.pallas_call(
        pixels_kernel,
        grid=(steps,),
        out_shape=jax.ShapeDtypeStruct((pixels, count), BF16),
        in_specs=[
            pl.BlockSpec((1, count, pixels // steps), lambda i: (0, 0, i)),
            pl.BlockSpec((1, pixels // steps), lambda i: (0, i)),
            pl.BlockSpec((1, pixels // steps), lambda i: (0, i)),
        ],
        out_specs=pl.BlockSpec((pixels // steps, count), lambda i: (i, 0)),
        cost_estimate=cost(4),
        compiler_params=pltpu.CompilerParams(vmem_limit_bytes=SMALL * MIB),
        name="pixels",
    )(patterns, detector_gain.reshape(1, pixels), background.reshape(1, pixels))
    corrected = corrected.reshape(tiles, TILE, count)
    bins = bin_map.reshape(tiles // 16, 16, 16, 16).transpose(0, 2, 1, 3).reshape(tiles, TILE)
    table, slot_rows, span = pl.pallas_call(
        slots_kernel,
        out_shape=(
            jax.ShapeDtypeStruct((RAD // 2, PAIR), jnp.int32),
            jax.ShapeDtypeStruct((tiles, TILE), jnp.int32),
            jax.ShapeDtypeStruct((tiles, 128), jnp.int32),
        ),
        in_specs=[vmem()] * 3,
        out_specs=(vmem(),) * 3,
        cost_estimate=cost(3),
        compiler_params=pltpu.CompilerParams(vmem_limit_bytes=SMALL * MIB),
        name="slots",
    )(present, other, bins)
    mine, theirs = pl.pallas_call(
        binning_kernel,
        out_shape=(
            jax.ShapeDtypeStruct((half, ROOM), F32),
            jax.ShapeDtypeStruct((half, ROOM), BF16),
        ),
        in_specs=[smem(), smem(), vmem(), vmem()],
        out_specs=(vmem(),) * 2,
        scratch_shapes=[pltpu.VMEM((ROOM + WINDOW, count), F32), pltpu.VMEM((count, ROOM), F32)],
        compiler_params=pltpu.CompilerParams(vmem_limit_bytes=GRANT * MIB),
        cost_estimate=cost(6),
        name="binning",
    )(core, span, slot_rows, corrected)
    message, spare = pl.pallas_call(
        combine_kernel,
        out_shape=(
            jax.ShapeDtypeStruct((half, SEG + PAIR), BF16),
            jax.ShapeDtypeStruct((half, ROOM - SEG), BF16),
        ),
        in_specs=[vmem()] * 3,
        out_specs=(vmem(),) * 2,
        cost_estimate=cost(1),
        compiler_params=pltpu.CompilerParams(vmem_limit_bytes=SMALL * MIB),
        name="combine",
    )(mine, swap(theirs), table)

    messages = [along(message, by) for by in range(1, chips)]
    step = hops(spare, [(1, 0), (2, 3)])
    traded = hops(spare, [(1, 2), (2, 1)])
    far_part = hops(spare, [(1, 3), (2, 0)])

    def spread(group):
        return group, across(group, 1), across(group, 2)

    def diagonal(held, after):
        upper, lower = halves(held[1], held[2], after)
        return (*held, across(upper, 2), across(lower, 1)), [upper, lower]

    size = best_picks.shape[0] * count
    turned, local, ranks, crowd = pl.pallas_call(
        picks_kernel,
        out_shape=(
            jax.ShapeDtypeStruct((2 * KEPT, BINS), BF16),
            jax.ShapeDtypeStruct((8, 4 * half), jnp.int32),
            jax.ShapeDtypeStruct((8, 4 * half), jnp.int32),
            jax.ShapeDtypeStruct((8, 128), jnp.int32),
        ),
        in_specs=[smem()] + [vmem()] * 4,
        out_specs=(vmem(),) * 4,
        compiler_params=pltpu.CompilerParams(vmem_limit_bytes=GRANT * MIB),
        cost_estimate=cost(30),
        name="picks",
    )(place, best_picks.reshape(1, size), best_picks.reshape(size, 1), templates, spare)
    group, tables, windows, ranges, full = arrive(
        True, chip, table, [message, messages[0], messages[2]], spare, step, [], [crowd]
    )
    near = spread(group)
    own, token = columns(len(GROUPS[0]), ranges, tables, templates, turned, [])
    near, gate = diagonal(near, [token])
    group, tables_far, windows_far, ranges, full = arrive(
        False, chip, tables, [messages[1]], traded, far_part, [full, crowd], [token]
    )
    far = spread(group)
    own_far, token = columns(len(GROUPS[1]), ranges, tables_far, templates, turned, gate)
    squares = pl.pallas_call(
        squares_kernel,
        out_shape=jax.ShapeDtypeStruct((8, half), F32),
        in_specs=[smem()] * 3 + [vmem()] * 5,
        out_specs=vmem(),
        scratch_shapes=[pltpu.VMEM((RAD // 8, half, PAIR), F32)],
        compiler_params=pltpu.CompilerParams(vmem_limit_bytes=GRANT * MIB),
        cost_estimate=cost(2),
        name="squares",
    )(place, windows, windows_far, tables, tables_far, near[0], far[0], token)
    far, gate = diagonal(far, [squares])
    total = score(True, False, rows, own, swap(own), near, None, (), gate, 60)
    blocks = score(
        False, True, rows, own_far, swap(own_far), far, total, (place, local, ranks, squares), (), 5
    )
    blocks = lax.all_to_all(blocks, ("section", "orient"), 0, 0)
    top, refined = pl.pallas_call(
        final_kernel,
        out_shape=(
            jax.ShapeDtypeStruct((1, count, TOPK), F32),
            jax.ShapeDtypeStruct((1, count // orients, 3), F32),
        ),
        in_specs=[smem(), vmem()],
        out_specs=(vmem(), vmem()),
        scratch_shapes=[pltpu.VMEM((TOPK, count), F32), pltpu.VMEM((count, TOPK), F32)],
        cost_estimate=cost(2),
        compiler_params=pltpu.CompilerParams(vmem_limit_bytes=SMALL * MIB),
        name="final",
    )(place, blocks)

    return lax.cond(
        full[0, 0] > 0,
        lambda: dense_body(
            patterns, detector_gain, background, bin_map, templates, best_picks
        ),
        lambda: (top, refined),
    )


def solution(mesh):
    sizes = dict(mesh.shape)
    fits = sizes["section"] == 4 and sizes["orient"] == 8
    return jax.shard_map(
        compact_body if fits else dense_body,
        mesh=mesh,
        in_specs=(
            P("section", None, "orient"),
            P("orient"),
            P("orient"),
            P("orient"),
            P(("section", "orient"), None),
            P(),
        ),
        out_specs=(P("section", None, None), P("section", "orient", None)),
        check_vma=False,
    )
```

```python
import functools

import jax
import jax.numpy as jnp
from jax import lax
from jax.experimental import pallas as pl
from jax.experimental.pallas import tpu as pltpu
from jax.sharding import PartitionSpec as P

RAD = 64
ANG = 192
TOPK = 8
REACH = 1


EPS = 1e-06
BLOCK_ROWS = 512


def shifted(x, axis, by):
    count = lax.axis_size(axis)
    return lax.ppermute(x, axis, [(i, (i + by) % count) for i in range(count)])


def merged_2(part, axis, combine):
    gathered = lax.all_gather(part, axis)

    def take(source):
        return lax.dynamic_index_in_dim(gathered, source, 0, False)

    return lax.fori_loop(
        1, lax.axis_size(axis), lambda source, state: combine(state, take(source)), take(0)
    )


def bin_block(corrected, bin_map, first, length):
    targets = first + lax.iota(jnp.int32, length)
    onehot = (bin_map[None, :] == targets[:, None]).astype(jnp.bfloat16)
    return lax.dot_general(
        onehot, corrected, (((1,), (1,)), ((), ())), preferred_element_type=jnp.float32
    )


def bin_rows(corrected, bin_map, length):
    blocks = 1
    while length // blocks > BLOCK_ROWS and length % (2 * blocks) == 0:
        blocks = blocks * 2
    height = length // blocks
    starts = height * lax.iota(jnp.int32, blocks)
    stacked = lax.map(lambda begin: bin_block(corrected, bin_map, begin, height), starts)
    return stacked.reshape(length, corrected.shape[0])


def merge_best(first_best, second_best):
    return lax.top_k(jnp.concatenate([first_best, second_best], axis=-1), TOPK)[0]


def score_batch(features, templates, wanted, group_base):
    scores = lax.dot_general(
        features, templates, (((0,), (1,)), ((), ())), preferred_element_type=jnp.float32
    )
    best = lax.top_k(scores, TOPK)[0]
    local = wanted - group_base
    count = templates.shape[0]
    owned = (local >= 0) & (local < count)
    chosen = jnp.take(templates, jnp.clip(local, 0, count - 1), axis=0)
    width = features.shape[1]
    chosen = chosen.reshape(width, RAD, ANG)
    grid = features.T.reshape(width, RAD, ANG)
    columns = []
    for offset in range(-REACH, REACH + 1):
        rolled = jnp.roll(chosen, -offset, axis=2)
        columns.append(jnp.sum(grid.astype(jnp.float32) * rolled.astype(jnp.float32), axis=(1, 2)))
    refined = jnp.where(owned[:, None], jnp.stack(columns, axis=1), 0.0)
    return (best, refined)


def dense_body(patterns, detector_gain, background, bin_map, templates, best_picks):
    sections = lax.axis_size("section")
    orients = lax.axis_size("orient")
    section_index = lax.axis_index("section")
    orient_index = lax.axis_index("orient")
    features_total = RAD * ANG
    corrected = ((patterns[0].astype(jnp.float32) - background) * detector_gain).astype(
        jnp.bfloat16
    )
    whole = lax.psum(bin_rows(corrected, bin_map, features_total), "orient")
    squares = jnp.sum(whole * whole, axis=0)
    features = (whole * lax.rsqrt(squares / features_total + EPS)).astype(jnp.bfloat16)
    group_base = (section_index * orients + orient_index) * templates.shape[0]
    held = features
    running_best = None
    running_refined = None
    for turn in range(sections):
        batch = (section_index + sections - turn) % sections
        wanted = lax.dynamic_index_in_dim(best_picks, batch, 0, keepdims=False)
        best, refined = score_batch(held, templates, wanted, group_base)
        if turn > 0:
            best = merge_best(running_best, best)
            refined = running_refined + refined
        packed = shifted(jnp.concatenate([best, refined], axis=1), "section", 1)
        running_best = packed[:, :TOPK]
        running_refined = packed[:, TOPK:]
        if turn + 1 < sections:
            held = shifted(held, "section", 1)
    merged = merged_2(running_best, "orient", merge_best)
    shares = lax.psum_scatter(running_refined, "orient", scatter_dimension=0, tiled=True)
    return (merged[None], shares[None])


BINS = RAD * ANG
SEG = 1792
SEGS = 6
ROOM = 2 * SEG
TILE = 256
WINDOW = 512
GROUPS = ((0, 1, 3), (2, 4, 5))
KEPT = 32
SQUARE = 384
GRANT = 22
SMALL = 10
PAIR = 2 * ANG
MIB = 1 << 20
F32 = jnp.float32
BF16 = jnp.bfloat16


def vmem():
    return pl.BlockSpec(memory_space=pltpu.VMEM)


def smem():
    return pl.BlockSpec(memory_space=pltpu.SMEM)


def cost(micros):
    return pl.CostEstimate(
        flops=int(micros * 1.1e9), bytes_accessed=int(micros * 1e6), transcendentals=0
    )


def dot_nt(a, b):
    return lax.dot_general(a, b, (((1,), (1,)), ((), ())), preferred_element_type=F32)


def dot_nn(a, b):
    return lax.dot_general(a, b, (((1,), (0,)), ((), ())), preferred_element_type=F32)


def polar(row):
    value = row.astype(F32)
    radial = jnp.floor((value + 0.5) * (1.0 / ANG))
    return radial, value - radial * ANG


def members(values, count):
    ids = lax.broadcasted_iota(jnp.int32, (count, values.shape[1]), 0).astype(F32)
    return ids == values


def presence_kernel(bins_ref, counts_ref):
    counts = jnp.zeros((ANG, RAD), F32)
    for line in range(0, bins_ref.shape[0], 2):
        parts = [bins_ref[line : line + 1, :], bins_ref[line + 1 : line + 2, :]]
        radial, angle = polar(jnp.concatenate(parts, axis=1))
        counts += dot_nt(
            members(angle, ANG).astype(BF16), members(radial, RAD).astype(BF16)
        )
    counts_ref[...] = (counts > 0.5).astype(F32)


def below(size):
    rows = lax.broadcasted_iota(jnp.int32, (size, size), 0)
    cols = lax.broadcasted_iota(jnp.int32, (size, size), 1)
    return rows, cols


def edges(table, offset):
    pairs = table.shape[0]
    valid = (table >= 0).astype(F32).astype(BF16)
    count = dot_nn(valid, jnp.ones((PAIR, 128), BF16))
    rows, cols = below(pairs)
    low_end = count - 256 * jnp.floor(count * (1.0 / 256))
    high_end = jnp.floor(count * (1.0 / 256))
    sums = (cols <= rows).astype(BF16)
    ends = 256 * dot_nn(sums, high_end.astype(BF16)) + dot_nn(sums, low_end.astype(BF16))
    begins = ends - count
    lane = lax.broadcasted_iota(jnp.int32, count.shape, 1)
    wide = SEG // 128
    first = jnp.clip(jnp.floor((begins - offset) * (1.0 / 128)), 0, wide - SQUARE // 128)
    last = jnp.clip(jnp.floor((ends - offset + 127) * (1.0 / 128)), 0, wide)
    windows = jnp.where(lane == 0, first, jnp.where(count > 0, last, 0.0))
    at = (lane % 64).astype(F32) * 256 + offset
    found = jnp.where(lane < 64, (ends <= at).astype(F32), (begins < at + 256).astype(F32))
    ranges = jnp.sum(found, axis=0, keepdims=True)
    ranges = jnp.where(lane[:1] == 127, ends[pairs - 1 :], ranges)
    return windows.astype(jnp.int32), ranges.astype(jnp.int32), ends


def slots_kernel(own_ref, other_ref, bins_ref, table_ref, rows_ref, span_ref):
    present = jnp.maximum(own_ref[...], other_ref[...])
    held = present.astype(BF16)
    rows, cols = below(ANG)
    within = dot_nn((cols < rows).astype(BF16), held)
    totals = dot_nn(jnp.ones((ANG, ANG), BF16), held)
    rows, cols = below(RAD)
    before = dot_nn(totals.astype(BF16), (rows < cols).astype(BF16))
    slots = within + before
    high = jnp.floor(slots * (1.0 / 64))
    low = slots - 64 * high
    high = high.astype(BF16)
    low = low.astype(BF16)
    both = jnp.concatenate([high, low])
    line = lax.broadcasted_iota(jnp.int32, (RAD // 2, RAD), 0)
    ring = lax.broadcasted_iota(jnp.int32, (RAD // 2, RAD), 1)
    for side in range(2):
        pick = (ring == 2 * line + side).astype(BF16)
        turned = 64 * dot_nt(pick, high) + dot_nt(pick, low)
        table_ref[:, side * ANG : (side + 1) * ANG] = jnp.where(
            dot_nt(pick, held) > 0.5, turned, -1.0
        ).astype(jnp.int32)
    for tile in range(bins_ref.shape[0]):
        radial, angle = polar(bins_ref[tile : tile + 1, :])
        ring = members(radial, RAD).astype(BF16)
        value = dot_nn(both, ring)
        value = 64 * value[:ANG] + value[ANG:]
        value = jnp.sum(jnp.where(members(angle, ANG), value, 0.0), axis=0, keepdims=True)
        rows_ref[tile : tile + 1, :] = value.astype(jnp.int32)
    found = rows_ref[...]
    first = jnp.min(found, axis=1, keepdims=True)
    last = jnp.max(found, axis=1, keepdims=True)
    lane = lax.broadcasted_iota(jnp.int32, (found.shape[0], 128), 1)
    span_ref[...] = jnp.where(lane == 0, first, last)


def pixels_kernel(patterns_ref, gain_ref, background_ref, out_ref):
    value = (patterns_ref[0].astype(F32) - background_ref[...]) * gain_ref[...]
    out_ref[...] = value.astype(BF16).T


def binning_kernel(
    core_ref, span_ref, rows_ref, pixels_ref, mine_ref, theirs_ref, sums, turned
):
    sums[...] = jnp.zeros_like(sums)
    across = 256 // 16

    def add(tile, at):
        down = (tile // across) * 16
        right = (tile % across) * 16
        block = pixels_ref[pl.ds(down, 16), pl.ds(right, 16), :].reshape(TILE, 128)
        row = rows_ref[pl.ds(tile, 1), :]
        ids = lax.broadcasted_iota(jnp.int32, (WINDOW, TILE), 0)
        hits = (ids == row - at).astype(BF16)
        sums[pl.ds(at, WINDOW), :] += dot_nn(hits, block)

    def base_of(tile):
        return pl.multiple_of(jnp.minimum(span_ref[tile, 0], ROOM) // 8 * 8, 8)

    tiles = rows_ref.shape[0]
    for tile in range(tiles):
        add(tile, base_of(tile))

    def one_tile(tile, _):
        base = base_of(tile)
        stop = jnp.minimum(span_ref[tile, 1] + 1, ROOM)

        def one_window(step, _):
            add(tile, pl.multiple_of(base + step * WINDOW, 8))
            return 0

        lax.fori_loop(1, (stop - base + WINDOW - 1) // WINDOW, one_window, 0)
        return 0

    lax.fori_loop(0, tiles, one_tile, 0)
    for block in range(ROOM // 128):
        turned[:, block * 128 : (block + 1) * 128] = sums[
            block * 128 : (block + 1) * 128, :
        ].T
    core = core_ref[0]
    half = turned.shape[0] // 2
    mine_ref[...] = turned[pl.ds(pl.multiple_of(core * half, half), half), :]
    theirs_ref[...] = turned[
        pl.ds(pl.multiple_of((1 - core) * half, half), half), :
    ].astype(BF16)


def combine_kernel(
    mine_ref, theirs_ref, table_ref, message_ref, spare_ref
):
    total = (mine_ref[...] + theirs_ref[...].astype(F32)).astype(BF16)
    spare_ref[...] = total[:, SEG:]
    message_ref[:, :SEG] = total[:, :SEG]
    table = table_ref[...].astype(F32)
    high = jnp.floor(table * (1.0 / 64))
    pairs = table.shape[0]
    message_ref[:pairs, SEG:] = high.astype(BF16)
    message_ref[pairs:, SEG:] = (table - 64 * high).astype(BF16)


def sum_rows(mask, value):
    return jnp.sum(jnp.where(mask, value, 0.0), axis=0, keepdims=True)


def sum_lanes(mask, value):
    return jnp.sum(jnp.where(mask, value, 0.0), axis=1, keepdims=True)


def place_picks(place_ref, row_ref, col_ref, rows, local_ref, rank_ref, crowd_ref):
    section, orient, orients = place_ref[0], place_ref[1], place_ref[2]
    row = row_ref[...].astype(F32)
    col = col_ref[...].astype(F32)
    size = row.shape[1]
    i = lax.broadcasted_iota(jnp.int32, (size, size), 0)
    j = lax.broadcasted_iota(jnp.int32, (size, size), 1)
    equal = col == row
    first_row = (sum_rows(equal & (i < j), 1.0) == 0).astype(F32)
    first_col = (sum_lanes(equal & (j < i), 1.0) == 0).astype(F32)
    owner_row = jnp.floor((row + 0.5) * (1.0 / rows))
    owner_col = jnp.floor((col + 0.5) * (1.0 / rows))
    same = owner_col == owner_row
    rank_row = sum_rows(same & (i < j), first_col)
    rank_col = sum_lanes(same & (j < i), first_row)
    rank_of = sum_rows(equal, first_col * rank_col)
    crowd_ref[...] = jnp.broadcast_to(
        jnp.max(rank_of, axis=1, keepdims=True), crowd_ref.shape
    ).astype(jnp.int32)
    me = section * orients + orient
    base = (me * rows).astype(F32)
    ids = lax.broadcasted_iota(jnp.int32, (KEPT, size), 0).astype(F32)
    chosen = (first_row > 0) & (owner_row == me.astype(F32)) & (rank_row == ids)
    wanted = sum_lanes(chosen, row - base + 1) - 1
    half = 64
    core = orient % 2
    local_ref[...] = jnp.zeros_like(local_ref)
    rank_ref[...] = jnp.zeros_like(rank_ref)
    lanes = lax.broadcasted_iota(jnp.int32, (1, size), 1)
    for by in range(4):
        start = (section ^ by) * 2 * half + core * half
        shift = (size - start) % size
        there = slice(by * half, (by + 1) * half)
        local_ref[2:3, there] = pltpu.roll(row, shift, 1)[:, :half].astype(jnp.int32)
        rank_ref[2:3, there] = pltpu.roll(rank_of, shift, 1)[:, :half].astype(jnp.int32)
    for side in range(2):
        owner = section * orients + (orient ^ side)
        local = local_ref[2:3, :] - owner * rows
        held = (local >= 0) & (local < rows)
        local_ref[side : side + 1, :] = jnp.where(held, local, -1)
        rank_ref[side : side + 1, :] = jnp.where(held, rank_ref[2:3, :], -1)
    return wanted


def turn_picks(wanted, templates_ref, out_ref):
    rows = templates_ref.shape[0]
    ids = lax.broadcasted_iota(jnp.int32, (KEPT, rows), 1).astype(F32)
    select = (ids == wanted).astype(BF16)
    lane = lax.broadcasted_iota(jnp.int32, (KEPT, PAIR), 1)
    for pair in range(RAD // 2):
        cols = slice(pair * PAIR, (pair + 1) * PAIR)
        taken = dot_nn(select, templates_ref[:, cols])
        later = jnp.where(
            lane % ANG == 0, pltpu.roll(taken, ANG + 1, 1), pltpu.roll(taken, 1, 1)
        )
        sooner = jnp.where(
            lane % ANG == ANG - 1,
            pltpu.roll(taken, ANG - 1, 1),
            pltpu.roll(taken, PAIR - 1, 1),
        )
        out_ref[:KEPT, cols] = later.astype(BF16)
        out_ref[KEPT:, cols] = sooner.astype(BF16)


def permute_columns(seg, offset, range_ref, table_ref, templates_ref, turned_ref, out_ref):
    wide = 5

    def block(pair, pairs):
        col = pl.ds(pl.multiple_of(pair * PAIR, 128), pairs * PAIR)
        return jnp.concatenate([templates_ref[:, col], turned_ref[:, col]], axis=0)

    def hits(pair, at):
        row = table_ref[seg, pl.ds(pair, 1), :]
        ids = lax.broadcasted_iota(jnp.int32, (256, PAIR), 0)
        return (ids == row - at).astype(BF16)

    def start_of(window):
        return jnp.minimum(range_ref[seg, window], RAD // 2 - wide)

    for window in range(SEG // 256):
        at = offset + window * 256
        start = start_of(window)
        mask = jnp.concatenate([hits(start + i, at) for i in range(wide)], axis=1)
        out_ref[0, :, window * 256 : (window + 1) * 256] = dot_nt(
            block(start, wide), mask
        ).astype(BF16)

    def one_window(window, _):
        to = pl.ds(pl.multiple_of(window * 256, 256), 256)

        def one_pair(pair, _):
            more = dot_nt(block(pair, 1), hits(pair, offset + window * 256))
            out_ref[0, :, to] = (out_ref[0, :, to].astype(F32) + more).astype(BF16)
            return 0

        lax.fori_loop(start_of(window) + wide, range_ref[seg, 64 + window], one_pair, 0)
        return 0

    more = 0
    for window in range(SEG // 256):
        more = jnp.maximum(more, range_ref[seg, 64 + window] - start_of(window))

    @pl.when(more > wide)
    def _():
        lax.fori_loop(0, SEG // 256, one_window, 0)


def picks_kernel(
    place_ref, row_ref, col_ref, templates_ref, _, turned_ref, local_ref, rank_ref, crowd_ref
):
    rows = templates_ref.shape[0]
    wanted = place_picks(place_ref, row_ref, col_ref, rows, local_ref, rank_ref, crowd_ref)
    turn_picks(wanted, templates_ref, turned_ref)


def columns_kernel(bases, range_ref, table_ref, templates_ref, turned_ref, *refs):
    out_ref, token_ref, held_ref, arrived = refs[-4:]
    seg = pl.program_id(0)

    @pl.when(seg == 0)
    def _():
        copy = pltpu.make_async_copy(templates_ref, held_ref, arrived)
        copy.start()
        token_ref[...] = jnp.zeros_like(token_ref)
        copy.wait()

    offset = jnp.where(seg >= bases, SEG, 0)
    permute_columns(seg, offset, range_ref, table_ref, held_ref, turned_ref, out_ref)


def whole(shape):
    return pl.BlockSpec(shape, lambda i: (0,) * len(shape))


def each(shape):
    return pl.BlockSpec((1, *shape), lambda i: (i,) + (0,) * len(shape))


def columns(segs, ranges, tables, templates, turned, after):
    height = templates.shape[0] + turned.shape[0]
    count = len(segs)
    return pl.pallas_call(
        functools.partial(columns_kernel, sum(seg < 4 for seg in segs)),
        grid=(count,),
        out_shape=(
            jax.ShapeDtypeStruct((count, height, SEG), BF16),
            jax.ShapeDtypeStruct((8, 128), F32),
        ),
        in_specs=[
            smem(),
            whole(tables.shape),
            pl.BlockSpec(memory_space=pl.ANY),
            whole(turned.shape),
        ]
        + [vmem()] * len(after),
        out_specs=(each((height, SEG)), whole((8, 128))),
        scratch_shapes=[pltpu.VMEM(templates.shape, BF16), pltpu.SemaphoreType.DMA],
        compiler_params=pltpu.CompilerParams(vmem_limit_bytes=GRANT * MIB),
        cost_estimate=cost(30 * count),
        name="columns",
    )(ranges, tables, templates, turned, *after)


def arrive_kernel(first, chip_ref, held_ref, *refs):
    group_ref, table_ref, window_ref, range_ref, full_ref = refs[-5:]
    messages = refs[:3] if first else refs[:1]
    pairs = table_ref.shape[1]
    chip = chip_ref[0]
    for at, ref in enumerate(messages):
        group_ref[at] = ref[:, :SEG]
        high = ref[:pairs, SEG:].astype(F32)
        low = ref[pairs:, SEG:].astype(F32)
        table_ref[at] = (64 * high + low).astype(jnp.int32)
    bases = len(messages)
    if not first:
        mine_ref, step_ref, traded_ref, far_ref = refs[1:5]
        inner = (chip == 1) | (chip == 2)

        @pl.when(inner)
        def _():
            group_ref[1] = mine_ref[...]
            group_ref[2] = traded_ref[...]

        @pl.when(jnp.logical_not(inner))
        def _():
            group_ref[1] = step_ref[...]
            group_ref[2] = far_ref[...]

        table_ref[1] = jnp.where(
            chip == 0, held_ref[2], jnp.where(chip == 3, held_ref[1], held_ref[0])
        )
        table_ref[2] = jnp.where(
            chip == 1, held_ref[2], jnp.where(chip == 2, held_ref[1], table_ref[0])
        )
    range_ref[...] = jnp.zeros_like(range_ref)
    for at in range(table_ref.shape[0]):
        windows, ranges, _ = edges(table_ref[at], SEG if at >= bases else 0)
        window_ref[at] = windows
        range_ref[at : at + 1, :] = ranges
    chips = [chip, (chip + 3) % 4, (chip + 1) % 4] if first else [(chip + 2) % 4]
    totals = [range_ref[at : at + 1, :] for at in range(len(chips))]
    full = jnp.zeros((1, 128), jnp.int32)
    for held, total in zip(chips, totals, strict=True):
        room = jnp.where((held == 1) | (held == 2), ROOM, SEG)
        full = jnp.maximum(full, (total > room).astype(jnp.int32))
    if not first:
        near_ref, crowd_ref = refs[5:7]
        full = jnp.maximum(full, near_ref[0:1, :])
        full = jnp.maximum(full, (crowd_ref[0:1, :] >= KEPT).astype(jnp.int32))
    lane = lax.broadcasted_iota(jnp.int32, (8, 128), 1)
    full = jnp.where(lane == 127, jnp.broadcast_to(full, (8, 128)), 0)
    full_ref[...] = jnp.broadcast_to(jnp.max(full, axis=1, keepdims=True), (8, 128))


def arrive(first, chip, held, parts, extra, after):
    count = 3
    half = parts[0].shape[0]
    pairs = RAD // 2
    return pl.pallas_call(
        functools.partial(arrive_kernel, first),
        out_shape=(
            jax.ShapeDtypeStruct((count, half, SEG), BF16),
            jax.ShapeDtypeStruct((count, pairs, PAIR), jnp.int32),
            jax.ShapeDtypeStruct((count, pairs, 128), jnp.int32),
            jax.ShapeDtypeStruct((8, 128), jnp.int32),
            jax.ShapeDtypeStruct((8, 128), jnp.int32),
        ),
        in_specs=[smem()] + [vmem()] * (1 + len(parts) + len(extra) + len(after)),
        out_specs=(vmem(),) * 5,
        cost_estimate=cost(1),
        compiler_params=pltpu.CompilerParams(vmem_limit_bytes=SMALL * MIB),
        name="arrive",
    )(chip, held, *parts, *extra, *after)


def halves_kernel(x_ref, y_ref, *refs):
    upper_ref, lower_ref = refs[-2:]
    size = upper_ref.shape[1]
    upper_ref[...] = x_ref[:, :size]
    lower_ref[...] = y_ref[:, size:]


def halves(x, y, after):
    shape = jax.ShapeDtypeStruct((x.shape[0], x.shape[1] // 2, x.shape[2]), x.dtype)
    return pl.pallas_call(
        halves_kernel,
        out_shape=(shape, shape),
        in_specs=[vmem(), vmem()] + [vmem()] * len(after),
        out_specs=(vmem(), vmem()),
        cost_estimate=cost(1),
        compiler_params=pltpu.CompilerParams(vmem_limit_bytes=SMALL * MIB),
        name="halves",
    )(x, y, *after)


def squares_kernel(place_ref, *refs):
    count = len(GROUPS)
    windows, tables, lists = refs[:count], refs[count : 2 * count], refs[2 * count : 3 * count]
    out_ref, dense_ref = refs[-2:]
    share = tables[0].shape[1] // 4
    half = lists[0].shape[1]
    first = place_ref[1] // 2 * share
    parts = [
        (windows[group], tables[group], lists[group], at, 0 if seg < 4 else SEG)
        for group, segs in enumerate(GROUPS)
        for at, seg in enumerate(segs)
    ]

    def hits(table, at, offset, pair, begin, size):
        ids = lax.broadcasted_iota(jnp.int32, (size, PAIR), 0)
        return (ids == table[at, pl.ds(pair, 1), :] - offset - begin).astype(BF16)

    for step in range(share):
        pair = first + step
        masks = []
        values = []
        for window, table, ref, at, offset in parts:
            begin = pl.multiple_of(window[at, pair, 0] * 128, 128)
            masks.append(hits(table, at, offset, pair, begin, SQUARE))
            values.append(ref[at, :, pl.ds(begin, SQUARE)])
        dense_ref[step] = dot_nn(jnp.concatenate(values, axis=1), jnp.concatenate(masks, axis=0))

    def one_pair(step, _):
        pair = first + step
        more = 0
        for window, _, _, at, _ in parts:
            more = jnp.maximum(more, window[at, pair, 1] - window[at, pair, 0])

        @pl.when(more > SQUARE // 128)
        def _():
            for window, table, ref, at, offset in parts:

                def one_window(index, _):
                    begin = pl.multiple_of(index * 128, 128)
                    dense_ref[step] += dot_nn(
                        ref[at, :, pl.ds(begin, 128)], hits(table, at, offset, pair, begin, 128)
                    )
                    return 0

                lax.fori_loop(
                    window[at, pair, 0] + SQUARE // 128, window[at, pair, 1], one_window, 0
                )

        return 0

    lax.fori_loop(0, share, one_pair, 0)
    ones = jnp.ones((8, PAIR), BF16)
    total = jnp.zeros((8, half), F32)
    for step in range(share):
        square = dense_ref[step] * dense_ref[step]
        high = square.astype(BF16)
        low = (square - high.astype(F32)).astype(BF16)
        total = total + dot_nt(ones, high) + dot_nt(ones, low)
    out_ref[...] = total


def insert_sorted(best, value):
    out = []
    for held in best:
        out.append(jnp.maximum(held, value))
        value = jnp.minimum(held, value)
    return out


def merge_sorted(first, second):
    count = len(first)
    both = [jnp.maximum(first[i], second[count - 1 - i]) for i in range(count)]
    gap = count // 2
    while gap:
        for i in range(count):
            if i & gap == 0:
                high = jnp.maximum(both[i], both[i + gap])
                low = jnp.minimum(both[i], both[i + gap])
                both[i], both[i + gap] = high, low
        gap //= 2
    return both


def score_kernel(first, last, rows, *refs):
    count = 0 if first else 1
    own_ref, pair_ref, z_ref, x_ref, y_ref, d_ref, e_ref = refs[:7]
    rest = refs[7:]
    if not first:
        so_far_ref, rest = rest[0], rest[1:]
    if last:
        place_ref, local_ref, rank_ref, squares_ref, out_ref, total, lists, packed = rest
    else:
        out_ref, lists = rest[-2:]
        total = out_ref
    half = z_ref.shape[1]
    lists[0:half, :] = z_ref[0]
    lists[half : 2 * half, :] = x_ref[0]
    lists[2 * half : 3 * half, :] = y_ref[0]
    lists[3 * half : 3 * half + half // 2, :] = d_ref[0]
    lists[3 * half + half // 2 :, :] = e_ref[0]

    @pl.when(pl.program_id(0) == 0)
    def _():
        total[...] = jnp.zeros_like(total) if first else so_far_ref[...]

    for side, ref in enumerate((own_ref, pair_ref)):
        total[side] += dot_nt(ref[0], lists[...])
    if last:

        @pl.when(pl.program_id(0) == pl.num_programs(0) - 1)
        def _():
            pick_out(
                rows, half, total, place_ref, local_ref, rank_ref, squares_ref, out_ref, packed
            )


def pick_out(rows, half, total, place_ref, local_ref, rank_ref, squares_ref, out_ref, packed):
    width = total.shape[2]
    low = jnp.full((8, width), -jnp.inf, F32)
    best = [low] * TOPK
    for side in range(2):
        def step(at, best):
            return tuple(
                insert_sorted(best, total[side, pl.ds(pl.multiple_of(at * 8, 8), 8), :])
            )

        best = lax.fori_loop(0, rows // 8, step, tuple(best), unroll=2)
    for turn in (4, 2, 1):
        best = merge_sorted(best, [pltpu.roll(part, turn, 0) for part in best])
    for place in range(TOPK):
        packed[place : place + 1, :] = best[place][0:1, :]
    picked = [jnp.zeros((1, width), F32) for _ in range(3)]
    for side in range(2):
        ids = lax.broadcasted_iota(jnp.int32, (rows, width), 0)
        picked[1] += jnp.sum(
            jnp.where(ids == local_ref[side : side + 1, :], total[side, :rows, :], 0.0),
            axis=0,
            keepdims=True,
        )
        ids = lax.broadcasted_iota(jnp.int32, (KEPT, width), 0)
        hit = ids == rank_ref[side : side + 1, :]
        picked[0] += jnp.sum(
            jnp.where(hit, total[side, rows : rows + KEPT, :], 0.0), axis=0, keepdims=True
        )
        picked[2] += jnp.sum(
            jnp.where(hit, total[side, rows + KEPT :, :], 0.0), axis=0, keepdims=True
        )
    packed[TOPK:, :] = jnp.zeros((8, width), F32)
    for place in range(3):
        packed[TOPK + place : TOPK + place + 1, :] = picked[place]
    packed[TOPK + 3 : TOPK + 4, :half] = squares_ref[0:1, :]
    section, core, orients = place_ref[0], place_ref[1] % 2, place_ref[2]
    for by in range(4):
        there = slice(by * half, (by + 1) * half)
        block = jnp.concatenate([packed[:TOPK, there], packed[TOPK:, there]], axis=1)
        block = pltpu.roll(block, core * half, 1)
        for orient in range(8):
            out_ref[(section ^ by) * orients + orient] = block


def score(first, last, rows, own, pair, lists, so_far, extra, after, micros):
    count, height, _ = own.shape
    width = 4 * lists[0].shape[1]
    scratch = [pltpu.VMEM((width, SEG), BF16)]
    if last:
        scratch = [pltpu.VMEM((2, height, width), F32)] + scratch
        scratch.append(pltpu.VMEM((16, width), F32))
        shape = (32, TOPK, 128)
    else:
        shape = (2, height, width)
    args = [own, pair, *lists]
    specs = [each(arg.shape[1:]) for arg in args]
    if not first:
        args.append(so_far)
        specs.append(whole(so_far.shape))
    if last:
        specs = specs + [smem()] + [vmem()] * 3
    args.extend(extra)
    return pl.pallas_call(
        functools.partial(score_kernel, first, last, rows),
        grid=(count,),
        out_shape=jax.ShapeDtypeStruct(shape, F32),
        in_specs=specs + [vmem()] * len(after),
        out_specs=whole(shape),
        scratch_shapes=scratch,
        compiler_params=pltpu.CompilerParams(vmem_limit_bytes=GRANT * MIB),
        cost_estimate=cost(micros),
        name="score",
    )(*args, *after)


def final_kernel(
    place_ref, blocks_ref, full_ref, other_top_ref, other_refined_ref,
    top_ref, refined_ref, lines, turned,
):
    count = blocks_ref.shape[0]
    source = lax.broadcasted_iota(jnp.int32, (count, 128), 0)
    lane = lax.broadcasted_iota(jnp.int32, (count, 128), 1)
    best_here = (source % 2) == (lane // 64)
    best = []
    rest = []
    for place in range(TOPK):
        row = blocks_ref[:, place, :]
        best.append(jnp.where(best_here, row, -jnp.inf))
        if place < 4:
            rest.append(jnp.sum(jnp.where(best_here, 0.0, row), axis=0, keepdims=True))
    while count > 8:
        count //= 2
        best = merge_sorted([part[:count] for part in best], [part[count:] for part in best])
    for turn in (4, 2, 1):
        best = merge_sorted(best, [pltpu.roll(part, turn, 0) for part in best])
    rest = [pltpu.roll(row, 64, 1) for row in rest]
    factor = lax.rsqrt(rest[3] / BINS + EPS)
    for place in range(TOPK):
        lines[place : place + 1, :] = best[place][0:1, :] * factor
    full = jnp.broadcast_to(full_ref[0:1, 0:1], (top_ref.shape[1], TOPK)) > 0
    top_ref[0] = jnp.where(full, other_top_ref[0], lines[...].T)
    for place in range(3):
        lines[place : place + 1, :] = rest[place] * factor
    turned[...] = lines[...].T
    share = refined_ref.shape[1]
    first = pl.multiple_of(place_ref[1] * share, share)
    full = jnp.broadcast_to(full_ref[0:1, 0:1], (share, 3)) > 0
    refined_ref[0] = jnp.where(full, other_refined_ref[0], turned[pl.ds(first, share), :3])


def compact_body(patterns, detector_gain, background, bin_map, templates, best_picks):
    orients = lax.axis_size("orient")
    chips = orients // 2
    section = lax.axis_index("section")
    orient = lax.axis_index("orient")
    place = jnp.stack([section, orient, jnp.full_like(orient, orients)]).astype(jnp.int32)
    core = (orient % 2).reshape(1).astype(jnp.int32)
    chip = (orient // 2).reshape(1).astype(jnp.int32)
    rows = templates.shape[0]
    count = patterns.shape[1]
    half = count // 2
    pixels = patterns.shape[2]

    def swap(x):
        return lax.ppermute(x, "orient", [(i, i ^ 1) for i in range(orients)])

    def along(x, by):
        return lax.ppermute(x, "orient", [(i, (i + 2 * by) % orients) for i in range(orients)])

    def hops(x, pairs):
        return lax.ppermute(
            x, "orient", [(2 * i + c, 2 * j + c) for i, j in pairs for c in range(2)]
        )

    def across(x, by):
        return lax.ppermute(x, "section", [(i, i ^ by) for i in range(4)])

    tiles = pixels // TILE
    lines = bin_map.reshape(2 * tiles, TILE // 2)
    present = pl.pallas_call(
        presence_kernel,
        out_shape=jax.ShapeDtypeStruct((ANG, RAD), F32),
        in_specs=[vmem()],
        out_specs=vmem(),
        cost_estimate=cost(2),
        compiler_params=pltpu.CompilerParams(vmem_limit_bytes=SMALL * MIB),
        name="presence",
    )(lines)
    other = swap(present)
    steps = 8
    corrected = pl.pallas_call(
        pixels_kernel,
        grid=(steps,),
        out_shape=jax.ShapeDtypeStruct((pixels, count), BF16),
        in_specs=[
            pl.BlockSpec((1, count, pixels // steps), lambda i: (0, 0, i)),
            pl.BlockSpec((1, pixels // steps), lambda i: (0, i)),
            pl.BlockSpec((1, pixels // steps), lambda i: (0, i)),
        ],
        out_specs=pl.BlockSpec((pixels // steps, count), lambda i: (i, 0)),
        cost_estimate=cost(4),
        compiler_params=pltpu.CompilerParams(vmem_limit_bytes=SMALL * MIB),
        name="pixels",
    )(patterns, detector_gain.reshape(1, pixels), background.reshape(1, pixels))
    corrected = corrected.reshape(tiles, TILE, count)
    bins = bin_map.reshape(tiles // 16, 16, 16, 16).transpose(0, 2, 1, 3).reshape(tiles, TILE)
    table, slot_rows, span = pl.pallas_call(
        slots_kernel,
        out_shape=(
            jax.ShapeDtypeStruct((RAD // 2, PAIR), jnp.int32),
            jax.ShapeDtypeStruct((tiles, TILE), jnp.int32),
            jax.ShapeDtypeStruct((tiles, 128), jnp.int32),
        ),
        in_specs=[vmem()] * 3,
        out_specs=(vmem(),) * 3,
        cost_estimate=cost(3),
        compiler_params=pltpu.CompilerParams(vmem_limit_bytes=SMALL * MIB),
        name="slots",
    )(present, other, bins)
    mine, theirs = pl.pallas_call(
        binning_kernel,
        out_shape=(
            jax.ShapeDtypeStruct((half, ROOM), F32),
            jax.ShapeDtypeStruct((half, ROOM), BF16),
        ),
        in_specs=[smem(), smem(), vmem(), vmem()],
        out_specs=(vmem(),) * 2,
        scratch_shapes=[pltpu.VMEM((ROOM + WINDOW, count), F32), pltpu.VMEM((count, ROOM), F32)],
        compiler_params=pltpu.CompilerParams(vmem_limit_bytes=14 * MIB),
        cost_estimate=cost(6),
        name="binning",
    )(core, span, slot_rows, corrected)
    message, spare = pl.pallas_call(
        combine_kernel,
        out_shape=(
            jax.ShapeDtypeStruct((half, SEG + PAIR), BF16),
            jax.ShapeDtypeStruct((half, ROOM - SEG), BF16),
        ),
        in_specs=[vmem()] * 3,
        out_specs=(vmem(),) * 2,
        cost_estimate=cost(1),
        compiler_params=pltpu.CompilerParams(vmem_limit_bytes=SMALL * MIB),
        name="combine",
    )(mine, swap(theirs), table)

    messages = [along(message, by) for by in range(1, chips)]
    step = hops(spare, [(1, 0), (2, 3)])
    traded = hops(spare, [(1, 2), (2, 1)])
    far_part = hops(spare, [(1, 3), (2, 0)])

    def spread(group):
        return group, across(group, 1), across(group, 2)

    def diagonal(held, after):
        upper, lower = halves(held[1], held[2], after)
        return (*held, across(upper, 2), across(lower, 1)), [upper, lower]

    size = best_picks.shape[0] * count
    turned, local, ranks, crowd = pl.pallas_call(
        picks_kernel,
        out_shape=(
            jax.ShapeDtypeStruct((2 * KEPT, BINS), BF16),
            jax.ShapeDtypeStruct((8, 4 * half), jnp.int32),
            jax.ShapeDtypeStruct((8, 4 * half), jnp.int32),
            jax.ShapeDtypeStruct((8, 128), jnp.int32),
        ),
        in_specs=[smem()] + [vmem()] * 4,
        out_specs=(vmem(),) * 4,
        compiler_params=pltpu.CompilerParams(vmem_limit_bytes=GRANT * MIB),
        cost_estimate=cost(30),
        name="picks",
    )(place, best_picks.reshape(1, size), best_picks.reshape(size, 1), templates, spare)
    group, tables, windows, ranges, full = arrive(
        True, chip, table, [message, messages[0], messages[2]], [], [crowd]
    )
    near = spread(group)
    own, token = columns(GROUPS[0], ranges, tables, templates, turned, [])
    near, gate = diagonal(near, [token])
    group, tables_far, windows_far, ranges, full = arrive(
        False, chip, tables, [messages[1], spare, step, traded, far_part], [full, crowd], [token]
    )
    far = spread(group)
    own_far, token = columns(GROUPS[1], ranges, tables_far, templates, turned, gate)
    squares = pl.pallas_call(
        squares_kernel,
        out_shape=jax.ShapeDtypeStruct((8, half), F32),
        in_specs=[smem()] * 3 + [vmem()] * 5,
        out_specs=vmem(),
        scratch_shapes=[pltpu.VMEM((RAD // 8, half, PAIR), F32)],
        compiler_params=pltpu.CompilerParams(vmem_limit_bytes=GRANT * MIB),
        cost_estimate=cost(2),
        name="squares",
    )(place, windows, windows_far, tables, tables_far, near[0], far[0], token)
    far, gate = diagonal(far, [squares])
    total = score(True, False, rows, own, swap(own), near, None, (), gate, 60)
    blocks = score(
        False, True, rows, own_far, swap(own_far), far, total, (place, local, ranks, squares), (), 5
    )
    blocks = lax.all_to_all(blocks, ("section", "orient"), 0, 0)
    other_top, other_refined = lax.cond(
        full[0, 0] > 0,
        lambda: dense_body(
            patterns, detector_gain, background, bin_map, templates, best_picks
        ),
        lambda: (
            jnp.zeros((1, count, TOPK), F32),
            jnp.zeros((1, count // orients, 3), F32),
        ),
    )
    return pl.pallas_call(
        final_kernel,
        out_shape=(
            jax.ShapeDtypeStruct((1, count, TOPK), F32),
            jax.ShapeDtypeStruct((1, count // orients, 3), F32),
        ),
        in_specs=[smem()] + [vmem()] * 4,
        out_specs=(vmem(), vmem()),
        scratch_shapes=[pltpu.VMEM((TOPK, count), F32), pltpu.VMEM((count, TOPK), F32)],
        cost_estimate=cost(2),
        compiler_params=pltpu.CompilerParams(vmem_limit_bytes=SMALL * MIB),
        name="final",
    )(place, blocks, full, other_top, other_refined)


def solution(mesh):
    sizes = dict(mesh.shape)
    fits = sizes["section"] == 4 and sizes["orient"] == 8
    return jax.shard_map(
        compact_body if fits else dense_body,
        mesh=mesh,
        in_specs=(
            P("section", None, "orient"),
            P("orient"),
            P("orient"),
            P("orient"),
            P(("section", "orient"), None),
            P(),
        ),
        out_specs=(P("section", None, None), P("section", "orient", None)),
        check_vma=False,
    )
```

```python
import functools

import jax
import jax.numpy as jnp
from jax import lax
from jax.experimental import pallas as pl
from jax.experimental.pallas import tpu as pltpu
from jax.sharding import PartitionSpec as P

RAD = 64
ANG = 192
TOPK = 8
REACH = 1


EPS = 1e-06
BLOCK_ROWS = 512


def shifted(x, axis, by):
    count = lax.axis_size(axis)
    return lax.ppermute(x, axis, [(i, (i + by) % count) for i in range(count)])


def merged_2(part, axis, combine):
    gathered = lax.all_gather(part, axis)

    def take(source):
        return lax.dynamic_index_in_dim(gathered, source, 0, False)

    return lax.fori_loop(
        1, lax.axis_size(axis), lambda source, state: combine(state, take(source)), take(0)
    )


def bin_block(corrected, bin_map, first, length):
    targets = first + lax.iota(jnp.int32, length)
    onehot = (bin_map[None, :] == targets[:, None]).astype(jnp.bfloat16)
    return lax.dot_general(
        onehot, corrected, (((1,), (1,)), ((), ())), preferred_element_type=jnp.float32
    )


def bin_rows(corrected, bin_map, length):
    blocks = 1
    while length // blocks > BLOCK_ROWS and length % (2 * blocks) == 0:
        blocks = blocks * 2
    height = length // blocks
    starts = height * lax.iota(jnp.int32, blocks)
    stacked = lax.map(lambda begin: bin_block(corrected, bin_map, begin, height), starts)
    return stacked.reshape(length, corrected.shape[0])


def merge_best(first_best, second_best):
    return lax.top_k(jnp.concatenate([first_best, second_best], axis=-1), TOPK)[0]


def score_batch(features, templates, wanted, group_base):
    scores = lax.dot_general(
        features, templates, (((0,), (1,)), ((), ())), preferred_element_type=jnp.float32
    )
    best = lax.top_k(scores, TOPK)[0]
    local = wanted - group_base
    count = templates.shape[0]
    owned = (local >= 0) & (local < count)
    chosen = jnp.take(templates, jnp.clip(local, 0, count - 1), axis=0)
    width = features.shape[1]
    chosen = chosen.reshape(width, RAD, ANG)
    grid = features.T.reshape(width, RAD, ANG)
    columns = []
    for offset in range(-REACH, REACH + 1):
        rolled = jnp.roll(chosen, -offset, axis=2)
        columns.append(jnp.sum(grid.astype(jnp.float32) * rolled.astype(jnp.float32), axis=(1, 2)))
    refined = jnp.where(owned[:, None], jnp.stack(columns, axis=1), 0.0)
    return (best, refined)


def dense_body(patterns, detector_gain, background, bin_map, templates, best_picks):
    sections = lax.axis_size("section")
    orients = lax.axis_size("orient")
    section_index = lax.axis_index("section")
    orient_index = lax.axis_index("orient")
    features_total = RAD * ANG
    corrected = ((patterns[0].astype(jnp.float32) - background) * detector_gain).astype(
        jnp.bfloat16
    )
    whole = lax.psum(bin_rows(corrected, bin_map, features_total), "orient")
    squares = jnp.sum(whole * whole, axis=0)
    features = (whole * lax.rsqrt(squares / features_total + EPS)).astype(jnp.bfloat16)
    group_base = (section_index * orients + orient_index) * templates.shape[0]
    held = features
    running_best = None
    running_refined = None
    for turn in range(sections):
        batch = (section_index + sections - turn) % sections
        wanted = lax.dynamic_index_in_dim(best_picks, batch, 0, keepdims=False)
        best, refined = score_batch(held, templates, wanted, group_base)
        if turn > 0:
            best = merge_best(running_best, best)
            refined = running_refined + refined
        packed = shifted(jnp.concatenate([best, refined], axis=1), "section", 1)
        running_best = packed[:, :TOPK]
        running_refined = packed[:, TOPK:]
        if turn + 1 < sections:
            held = shifted(held, "section", 1)
    merged = merged_2(running_best, "orient", merge_best)
    shares = lax.psum_scatter(running_refined, "orient", scatter_dimension=0, tiled=True)
    return (merged[None], shares[None])


BINS = RAD * ANG
SEG = 1792
SEGS = 6
ROOM = 2 * SEG
TILE = 256
WINDOW = 512
GROUPS = ((0, 1, 3), (2, 4, 5))
KEPT = 32
SQUARE = 384
GRANT = 22
SMALL = 10
PAIR = 2 * ANG
MIB = 1 << 20
F32 = jnp.float32
BF16 = jnp.bfloat16


def vmem():
    return pl.BlockSpec(memory_space=pltpu.VMEM)


def smem():
    return pl.BlockSpec(memory_space=pltpu.SMEM)


def cost(micros):
    return pl.CostEstimate(
        flops=int(micros * 1.1e9), bytes_accessed=int(micros * 1e6), transcendentals=0
    )


def dot_nt(a, b):
    return lax.dot_general(a, b, (((1,), (1,)), ((), ())), preferred_element_type=F32)


def dot_nn(a, b):
    return lax.dot_general(a, b, (((1,), (0,)), ((), ())), preferred_element_type=F32)


def polar(row):
    value = row.astype(F32)
    radial = jnp.floor((value + 0.5) * (1.0 / ANG))
    return radial, value - radial * ANG


def members(values, count):
    ids = lax.broadcasted_iota(jnp.int32, (count, values.shape[1]), 0).astype(F32)
    return ids == values


def presence_kernel(bins_ref, counts_ref):
    counts = jnp.zeros((ANG, RAD), F32)
    for line in range(0, bins_ref.shape[0], 2):
        parts = [bins_ref[line : line + 1, :], bins_ref[line + 1 : line + 2, :]]
        radial, angle = polar(jnp.concatenate(parts, axis=1))
        counts += dot_nt(
            members(angle, ANG).astype(BF16), members(radial, RAD).astype(BF16)
        )
    counts_ref[...] = (counts > 0.5).astype(F32)


def below(size):
    rows = lax.broadcasted_iota(jnp.int32, (size, size), 0)
    cols = lax.broadcasted_iota(jnp.int32, (size, size), 1)
    return rows, cols


def edges(table, offset):
    pairs = table.shape[0]
    valid = (table >= 0).astype(F32).astype(BF16)
    count = dot_nn(valid, jnp.ones((PAIR, 128), BF16))
    rows, cols = below(pairs)
    low_end = count - 256 * jnp.floor(count * (1.0 / 256))
    high_end = jnp.floor(count * (1.0 / 256))
    sums = (cols <= rows).astype(BF16)
    ends = 256 * dot_nn(sums, high_end.astype(BF16)) + dot_nn(sums, low_end.astype(BF16))
    begins = ends - count
    lane = lax.broadcasted_iota(jnp.int32, count.shape, 1)
    wide = SEG // 128
    first = jnp.clip(jnp.floor((begins - offset) * (1.0 / 128)), 0, wide - SQUARE // 128)
    last = jnp.clip(jnp.floor((ends - offset + 127) * (1.0 / 128)), 0, wide)
    windows = jnp.where(lane == 0, first, jnp.where(count > 0, last, 0.0))
    at = (lane % 64).astype(F32) * 256 + offset
    found = jnp.where(lane < 64, (ends <= at).astype(F32), (begins < at + 256).astype(F32))
    ranges = jnp.sum(found, axis=0, keepdims=True)
    ranges = jnp.where(lane[:1] == 127, ends[pairs - 1 :], ranges)
    return windows.astype(jnp.int32), ranges.astype(jnp.int32), ends


def slots_kernel(own_ref, other_ref, bins_ref, table_ref, rows_ref, span_ref):
    present = jnp.maximum(own_ref[...], other_ref[...])
    held = present.astype(BF16)
    rows, cols = below(ANG)
    within = dot_nn((cols < rows).astype(BF16), held)
    totals = dot_nn(jnp.ones((ANG, ANG), BF16), held)
    rows, cols = below(RAD)
    before = dot_nn(totals.astype(BF16), (rows < cols).astype(BF16))
    slots = within + before
    high = jnp.floor(slots * (1.0 / 64))
    low = slots - 64 * high
    high = high.astype(BF16)
    low = low.astype(BF16)
    both = jnp.concatenate([high, low])
    line = lax.broadcasted_iota(jnp.int32, (RAD // 2, RAD), 0)
    ring = lax.broadcasted_iota(jnp.int32, (RAD // 2, RAD), 1)
    for side in range(2):
        pick = (ring == 2 * line + side).astype(BF16)
        turned = 64 * dot_nt(pick, high) + dot_nt(pick, low)
        table_ref[:, side * ANG : (side + 1) * ANG] = jnp.where(
            dot_nt(pick, held) > 0.5, turned, -1.0
        ).astype(jnp.int32)
    for tile in range(bins_ref.shape[0]):
        radial, angle = polar(bins_ref[tile : tile + 1, :])
        ring = members(radial, RAD).astype(BF16)
        value = dot_nn(both, ring)
        value = 64 * value[:ANG] + value[ANG:]
        value = jnp.sum(jnp.where(members(angle, ANG), value, 0.0), axis=0, keepdims=True)
        rows_ref[tile : tile + 1, :] = value.astype(jnp.int32)
    found = rows_ref[...]
    first = jnp.min(found, axis=1, keepdims=True)
    last = jnp.max(found, axis=1, keepdims=True)
    lane = lax.broadcasted_iota(jnp.int32, (found.shape[0], 128), 1)
    span_ref[...] = jnp.where(lane == 0, first, last)


def pixels_kernel(patterns_ref, gain_ref, background_ref, out_ref):
    value = (patterns_ref[0].astype(F32) - background_ref[...]) * gain_ref[...]
    out_ref[...] = value.astype(BF16).T


def binning_kernel(
    core_ref, span_ref, rows_ref, pixels_ref, mine_ref, theirs_ref, sums, turned
):
    sums[...] = jnp.zeros_like(sums)
    across = 256 // 16

    def add(tile, at):
        down = (tile // across) * 16
        right = (tile % across) * 16
        block = pixels_ref[pl.ds(down, 16), pl.ds(right, 16), :].reshape(TILE, 128)
        row = rows_ref[pl.ds(tile, 1), :]
        ids = lax.broadcasted_iota(jnp.int32, (WINDOW, TILE), 0)
        hits = (ids == row - at).astype(BF16)
        sums[pl.ds(at, WINDOW), :] += dot_nn(hits, block)

    def base_of(tile):
        return pl.multiple_of(jnp.minimum(span_ref[tile, 0], ROOM) // 8 * 8, 8)

    tiles = rows_ref.shape[0]
    for tile in range(tiles):
        add(tile, base_of(tile))

    def one_tile(tile, _):
        base = base_of(tile)
        stop = jnp.minimum(span_ref[tile, 1] + 1, ROOM)

        def one_window(step, _):
            add(tile, pl.multiple_of(base + step * WINDOW, 8))
            return 0

        lax.fori_loop(1, (stop - base + WINDOW - 1) // WINDOW, one_window, 0)
        return 0

    lax.fori_loop(0, tiles, one_tile, 0)
    for block in range(ROOM // 128):
        turned[:, block * 128 : (block + 1) * 128] = sums[
            block * 128 : (block + 1) * 128, :
        ].T
    core = core_ref[0]
    half = turned.shape[0] // 2
    mine_ref[...] = turned[pl.ds(pl.multiple_of(core * half, half), half), :]
    theirs_ref[...] = turned[
        pl.ds(pl.multiple_of((1 - core) * half, half), half), :
    ].astype(BF16)


def combine_kernel(
    mine_ref, theirs_ref, table_ref, message_ref, spare_ref
):
    total = (mine_ref[...] + theirs_ref[...].astype(F32)).astype(BF16)
    spare_ref[...] = total[:, SEG:]
    message_ref[:, :SEG] = total[:, :SEG]
    table = table_ref[...].astype(F32)
    high = jnp.floor(table * (1.0 / 64))
    pairs = table.shape[0]
    message_ref[:pairs, SEG:] = high.astype(BF16)
    message_ref[pairs:, SEG:] = (table - 64 * high).astype(BF16)


def sum_rows(mask, value):
    return jnp.sum(jnp.where(mask, value, 0.0), axis=0, keepdims=True)


def sum_lanes(mask, value):
    return jnp.sum(jnp.where(mask, value, 0.0), axis=1, keepdims=True)


def place_picks(place_ref, row_ref, col_ref, rows, local_ref, rank_ref, crowd_ref):
    section, orient, orients = place_ref[0], place_ref[1], place_ref[2]
    row = row_ref[...].astype(F32)
    col = col_ref[...].astype(F32)
    size = row.shape[1]
    i = lax.broadcasted_iota(jnp.int32, (size, size), 0)
    j = lax.broadcasted_iota(jnp.int32, (size, size), 1)
    equal = col == row
    first_row = (sum_rows(equal & (i < j), 1.0) == 0).astype(F32)
    first_col = (sum_lanes(equal & (j < i), 1.0) == 0).astype(F32)
    owner_row = jnp.floor((row + 0.5) * (1.0 / rows))
    owner_col = jnp.floor((col + 0.5) * (1.0 / rows))
    same = owner_col == owner_row
    rank_row = sum_rows(same & (i < j), first_col)
    rank_col = sum_lanes(same & (j < i), first_row)
    rank_of = sum_rows(equal, first_col * rank_col)
    crowd_ref[...] = jnp.broadcast_to(
        jnp.max(rank_of, axis=1, keepdims=True), crowd_ref.shape
    ).astype(jnp.int32)
    me = section * orients + orient
    base = (me * rows).astype(F32)
    ids = lax.broadcasted_iota(jnp.int32, (KEPT, size), 0).astype(F32)
    chosen = (first_row > 0) & (owner_row == me.astype(F32)) & (rank_row == ids)
    wanted = sum_lanes(chosen, row - base + 1) - 1
    half = 64
    core = orient % 2
    local_ref[...] = jnp.zeros_like(local_ref)
    rank_ref[...] = jnp.zeros_like(rank_ref)
    lanes = lax.broadcasted_iota(jnp.int32, (1, size), 1)
    for by in range(4):
        start = (section ^ by) * 2 * half + core * half
        shift = (size - start) % size
        there = slice(by * half, (by + 1) * half)
        local_ref[2:3, there] = pltpu.roll(row, shift, 1)[:, :half].astype(jnp.int32)
        rank_ref[2:3, there] = pltpu.roll(rank_of, shift, 1)[:, :half].astype(jnp.int32)
    for side in range(2):
        owner = section * orients + (orient ^ side)
        local = local_ref[2:3, :] - owner * rows
        held = (local >= 0) & (local < rows)
        local_ref[side : side + 1, :] = jnp.where(held, local, -1)
        rank_ref[side : side + 1, :] = jnp.where(held, rank_ref[2:3, :], -1)
    return wanted


def turn_picks(wanted, templates_ref, out_ref):
    rows = templates_ref.shape[0]
    ids = lax.broadcasted_iota(jnp.int32, (KEPT, rows), 1).astype(F32)
    select = (ids == wanted).astype(BF16)
    lane = lax.broadcasted_iota(jnp.int32, (KEPT, PAIR), 1)
    for pair in range(RAD // 2):
        cols = slice(pair * PAIR, (pair + 1) * PAIR)
        taken = dot_nn(select, templates_ref[:, cols])
        later = jnp.where(
            lane % ANG == 0, pltpu.roll(taken, ANG + 1, 1), pltpu.roll(taken, 1, 1)
        )
        sooner = jnp.where(
            lane % ANG == ANG - 1,
            pltpu.roll(taken, ANG - 1, 1),
            pltpu.roll(taken, PAIR - 1, 1),
        )
        out_ref[:KEPT, cols] = later.astype(BF16)
        out_ref[KEPT:, cols] = sooner.astype(BF16)


def permute_columns(seg, offset, range_ref, table_ref, templates_ref, turned_ref, out_ref):
    wide = 5

    def block(pair, pairs):
        col = pl.ds(pl.multiple_of(pair * PAIR, 128), pairs * PAIR)
        return jnp.concatenate([templates_ref[:, col], turned_ref[:, col]], axis=0)

    def hits(pair, at):
        row = table_ref[seg, pl.ds(pair, 1), :]
        ids = lax.broadcasted_iota(jnp.int32, (256, PAIR), 0)
        return (ids == row - at).astype(BF16)

    def start_of(window):
        return jnp.minimum(range_ref[seg, window], RAD // 2 - wide)

    for window in range(SEG // 256):
        at = offset + window * 256
        start = start_of(window)
        mask = jnp.concatenate([hits(start + i, at) for i in range(wide)], axis=1)
        out_ref[0, :, window * 256 : (window + 1) * 256] = dot_nt(
            block(start, wide), mask
        ).astype(BF16)

    def one_window(window, _):
        to = pl.ds(pl.multiple_of(window * 256, 256), 256)

        def one_pair(pair, _):
            more = dot_nt(block(pair, 1), hits(pair, offset + window * 256))
            out_ref[0, :, to] = (out_ref[0, :, to].astype(F32) + more).astype(BF16)
            return 0

        lax.fori_loop(start_of(window) + wide, range_ref[seg, 64 + window], one_pair, 0)
        return 0

    more = 0
    for window in range(SEG // 256):
        more = jnp.maximum(more, range_ref[seg, 64 + window] - start_of(window))

    @pl.when(more > wide)
    def _():
        lax.fori_loop(0, SEG // 256, one_window, 0)


def picks_kernel(
    place_ref, row_ref, col_ref, templates_ref, _, turned_ref, local_ref, rank_ref, crowd_ref
):
    rows = templates_ref.shape[0]
    wanted = place_picks(place_ref, row_ref, col_ref, rows, local_ref, rank_ref, crowd_ref)
    turn_picks(wanted, templates_ref, turned_ref)


def columns_kernel(bases, range_ref, table_ref, templates_ref, turned_ref, *refs):
    out_ref, token_ref, held_ref, arrived = refs[-4:]
    seg = pl.program_id(0)

    @pl.when(seg == 0)
    def _():
        copy = pltpu.make_async_copy(templates_ref, held_ref, arrived)
        copy.start()
        token_ref[...] = jnp.zeros_like(token_ref)
        copy.wait()

    offset = jnp.where(seg >= bases, SEG, 0)
    permute_columns(seg, offset, range_ref, table_ref, held_ref, turned_ref, out_ref)


def whole(shape):
    return pl.BlockSpec(shape, lambda i: (0,) * len(shape))


def each(shape):
    return pl.BlockSpec((1, *shape), lambda i: (i,) + (0,) * len(shape))


def columns(segs, ranges, tables, templates, turned, after):
    height = templates.shape[0] + turned.shape[0]
    count = len(segs)
    return pl.pallas_call(
        functools.partial(columns_kernel, sum(seg < 4 for seg in segs)),
        grid=(count,),
        out_shape=(
            jax.ShapeDtypeStruct((count, height, SEG), BF16),
            jax.ShapeDtypeStruct((8, 128), F32),
        ),
        in_specs=[
            smem(),
            whole(tables.shape),
            pl.BlockSpec(memory_space=pl.ANY),
            whole(turned.shape),
        ]
        + [vmem()] * len(after),
        out_specs=(each((height, SEG)), whole((8, 128))),
        scratch_shapes=[pltpu.VMEM(templates.shape, BF16), pltpu.SemaphoreType.DMA],
        compiler_params=pltpu.CompilerParams(vmem_limit_bytes=GRANT * MIB),
        cost_estimate=cost(30 * count),
        name="columns",
    )(ranges, tables, templates, turned, *after)


def arrive_kernel(first, chip_ref, held_ref, *refs):
    group_ref, table_ref, window_ref, range_ref, full_ref = refs[-5:]
    messages = refs[:3] if first else refs[:1]
    pairs = table_ref.shape[1]
    chip = chip_ref[0]
    for at, ref in enumerate(messages):
        group_ref[at] = ref[:, :SEG]
        high = ref[:pairs, SEG:].astype(F32)
        low = ref[pairs:, SEG:].astype(F32)
        table_ref[at] = (64 * high + low).astype(jnp.int32)
    bases = len(messages)
    if not first:
        mine_ref, step_ref, traded_ref, far_ref = refs[1:5]
        inner = (chip == 1) | (chip == 2)

        @pl.when(inner)
        def _():
            group_ref[1] = mine_ref[...]
            group_ref[2] = traded_ref[...]

        @pl.when(jnp.logical_not(inner))
        def _():
            group_ref[1] = step_ref[...]
            group_ref[2] = far_ref[...]

        table_ref[1] = jnp.where(
            chip == 0, held_ref[2], jnp.where(chip == 3, held_ref[1], held_ref[0])
        )
        table_ref[2] = jnp.where(
            chip == 1, held_ref[2], jnp.where(chip == 2, held_ref[1], table_ref[0])
        )
    range_ref[...] = jnp.zeros_like(range_ref)
    for at in range(table_ref.shape[0]):
        windows, ranges, _ = edges(table_ref[at], SEG if at >= bases else 0)
        window_ref[at] = windows
        range_ref[at : at + 1, :] = ranges
    chips = [chip, (chip + 3) % 4, (chip + 1) % 4] if first else [(chip + 2) % 4]
    totals = [range_ref[at : at + 1, :] for at in range(len(chips))]
    full = jnp.zeros((1, 128), jnp.int32)
    for held, total in zip(chips, totals, strict=True):
        room = jnp.where((held == 1) | (held == 2), ROOM, SEG)
        full = jnp.maximum(full, (total > room).astype(jnp.int32))
    if not first:
        near_ref, crowd_ref = refs[5:7]
        full = jnp.maximum(full, near_ref[0:1, :])
        full = jnp.maximum(full, (crowd_ref[0:1, :] >= KEPT).astype(jnp.int32))
    lane = lax.broadcasted_iota(jnp.int32, (8, 128), 1)
    full = jnp.where(lane == 127, jnp.broadcast_to(full, (8, 128)), 0)
    full_ref[...] = jnp.broadcast_to(jnp.max(full, axis=1, keepdims=True), (8, 128))


def arrive(first, chip, held, parts, extra, after):
    count = 3
    half = parts[0].shape[0]
    pairs = RAD // 2
    return pl.pallas_call(
        functools.partial(arrive_kernel, first),
        out_shape=(
            jax.ShapeDtypeStruct((count, half, SEG), BF16),
            jax.ShapeDtypeStruct((count, pairs, PAIR), jnp.int32),
            jax.ShapeDtypeStruct((count, pairs, 128), jnp.int32),
            jax.ShapeDtypeStruct((8, 128), jnp.int32),
            jax.ShapeDtypeStruct((8, 128), jnp.int32),
        ),
        in_specs=[smem()] + [vmem()] * (1 + len(parts) + len(extra) + len(after)),
        out_specs=(vmem(),) * 5,
        cost_estimate=cost(1),
        compiler_params=pltpu.CompilerParams(vmem_limit_bytes=SMALL * MIB),
        name="arrive",
    )(chip, held, *parts, *extra, *after)


def halves_kernel(x_ref, y_ref, *refs):
    upper_ref, lower_ref = refs[-2:]
    size = upper_ref.shape[1]
    upper_ref[...] = x_ref[:, :size]
    lower_ref[...] = y_ref[:, size:]


def halves(x, y, after):
    shape = jax.ShapeDtypeStruct((x.shape[0], x.shape[1] // 2, x.shape[2]), x.dtype)
    return pl.pallas_call(
        halves_kernel,
        out_shape=(shape, shape),
        in_specs=[vmem(), vmem()] + [vmem()] * len(after),
        out_specs=(vmem(), vmem()),
        cost_estimate=cost(1),
        compiler_params=pltpu.CompilerParams(vmem_limit_bytes=SMALL * MIB),
        name="halves",
    )(x, y, *after)


def squares_kernel(place_ref, *refs):
    count = len(GROUPS)
    windows, tables, lists = refs[:count], refs[count : 2 * count], refs[2 * count : 3 * count]
    out_ref, dense_ref = refs[-2:]
    share = tables[0].shape[1] // 4
    half = lists[0].shape[1]
    first = place_ref[1] // 2 * share
    parts = [
        (windows[group], tables[group], lists[group], at, 0 if seg < 4 else SEG)
        for group, segs in enumerate(GROUPS)
        for at, seg in enumerate(segs)
    ]

    def hits(table, at, offset, pair, begin, size):
        ids = lax.broadcasted_iota(jnp.int32, (size, PAIR), 0)
        return (ids == table[at, pl.ds(pair, 1), :] - offset - begin).astype(BF16)

    for step in range(share):
        pair = first + step
        masks = []
        values = []
        for window, table, ref, at, offset in parts:
            begin = pl.multiple_of(window[at, pair, 0] * 128, 128)
            masks.append(hits(table, at, offset, pair, begin, SQUARE))
            values.append(ref[at, :, pl.ds(begin, SQUARE)])
        dense_ref[step] = dot_nn(jnp.concatenate(values, axis=1), jnp.concatenate(masks, axis=0))

    def one_pair(step, _):
        pair = first + step
        more = 0
        for window, _, _, at, _ in parts:
            more = jnp.maximum(more, window[at, pair, 1] - window[at, pair, 0])

        @pl.when(more > SQUARE // 128)
        def _():
            for window, table, ref, at, offset in parts:

                def one_window(index, _):
                    begin = pl.multiple_of(index * 128, 128)
                    dense_ref[step] += dot_nn(
                        ref[at, :, pl.ds(begin, 128)], hits(table, at, offset, pair, begin, 128)
                    )
                    return 0

                lax.fori_loop(
                    window[at, pair, 0] + SQUARE // 128, window[at, pair, 1], one_window, 0
                )

        return 0

    lax.fori_loop(0, share, one_pair, 0)
    ones = jnp.ones((8, PAIR), BF16)
    total = jnp.zeros((8, half), F32)
    for step in range(share):
        square = dense_ref[step] * dense_ref[step]
        high = square.astype(BF16)
        low = (square - high.astype(F32)).astype(BF16)
        total = total + dot_nt(ones, high) + dot_nt(ones, low)
    out_ref[...] = total


def insert_sorted(best, value):
    out = []
    for held in best:
        out.append(jnp.maximum(held, value))
        value = jnp.minimum(held, value)
    return out


def merge_sorted(first, second):
    count = len(first)
    both = [jnp.maximum(first[i], second[count - 1 - i]) for i in range(count)]
    gap = count // 2
    while gap:
        for i in range(count):
            if i & gap == 0:
                high = jnp.maximum(both[i], both[i + gap])
                low = jnp.minimum(both[i], both[i + gap])
                both[i], both[i + gap] = high, low
        gap //= 2
    return both


def score_kernel(first, last, rows, *refs):
    count = 0 if first else 1
    own_ref, pair_ref, z_ref, x_ref, y_ref, d_ref, e_ref = refs[:7]
    rest = refs[7:]
    if not first:
        so_far_ref, rest = rest[0], rest[1:]
    if last:
        place_ref, local_ref, rank_ref, squares_ref, out_ref, total, lists, packed = rest
    else:
        out_ref, lists = rest[-2:]
        total = out_ref
    half = z_ref.shape[1]
    lists[0:half, :] = z_ref[0]
    lists[half : 2 * half, :] = x_ref[0]
    lists[2 * half : 3 * half, :] = y_ref[0]
    lists[3 * half : 3 * half + half // 2, :] = d_ref[0]
    lists[3 * half + half // 2 :, :] = e_ref[0]

    @pl.when(pl.program_id(0) == 0)
    def _():
        total[...] = jnp.zeros_like(total) if first else so_far_ref[...]

    for side, ref in enumerate((own_ref, pair_ref)):
        total[side] += dot_nt(ref[0], lists[...])
    if last:

        @pl.when(pl.program_id(0) == pl.num_programs(0) - 1)
        def _():
            pick_out(
                rows, half, total, place_ref, local_ref, rank_ref, squares_ref, out_ref, packed
            )


def pick_out(rows, half, total, place_ref, local_ref, rank_ref, squares_ref, out_ref, packed):
    width = total.shape[2]
    low = jnp.full((8, width), -jnp.inf, F32)
    best = [low] * TOPK
    for side in range(2):
        def step(at, best):
            return tuple(
                insert_sorted(best, total[side, pl.ds(pl.multiple_of(at * 8, 8), 8), :])
            )

        best = lax.fori_loop(0, rows // 8, step, tuple(best), unroll=2)
    for turn in (4, 2, 1):
        best = merge_sorted(best, [pltpu.roll(part, turn, 0) for part in best])
    for place in range(TOPK):
        packed[place : place + 1, :] = best[place][0:1, :]
    picked = [jnp.zeros((1, width), F32) for _ in range(3)]
    for side in range(2):
        ids = lax.broadcasted_iota(jnp.int32, (rows, width), 0)
        picked[1] += jnp.sum(
            jnp.where(ids == local_ref[side : side + 1, :], total[side, :rows, :], 0.0),
            axis=0,
            keepdims=True,
        )
        ids = lax.broadcasted_iota(jnp.int32, (KEPT, width), 0)
        hit = ids == rank_ref[side : side + 1, :]
        picked[0] += jnp.sum(
            jnp.where(hit, total[side, rows : rows + KEPT, :], 0.0), axis=0, keepdims=True
        )
        picked[2] += jnp.sum(
            jnp.where(hit, total[side, rows + KEPT :, :], 0.0), axis=0, keepdims=True
        )
    packed[TOPK:, :] = jnp.zeros((8, width), F32)
    for place in range(3):
        packed[TOPK + place : TOPK + place + 1, :] = picked[place]
    packed[TOPK + 3 : TOPK + 4, :half] = squares_ref[0:1, :]
    section, core, orients = place_ref[0], place_ref[1] % 2, place_ref[2]
    for by in range(4):
        there = slice(by * half, (by + 1) * half)
        block = jnp.concatenate([packed[:TOPK, there], packed[TOPK:, there]], axis=1)
        block = pltpu.roll(block, core * half, 1)
        for orient in range(8):
            out_ref[(section ^ by) * orients + orient] = block


def score(first, last, rows, own, pair, lists, so_far, extra, after, micros):
    count, height, _ = own.shape
    width = 4 * lists[0].shape[1]
    scratch = [pltpu.VMEM((width, SEG), BF16)]
    if last:
        scratch = [pltpu.VMEM((2, height, width), F32)] + scratch
        scratch.append(pltpu.VMEM((16, width), F32))
        shape = (32, TOPK, 128)
    else:
        shape = (2, height, width)
    args = [own, pair, *lists]
    specs = [each(arg.shape[1:]) for arg in args]
    if not first:
        args.append(so_far)
        specs.append(whole(so_far.shape))
    if last:
        specs = specs + [smem()] + [vmem()] * 3
    args.extend(extra)
    return pl.pallas_call(
        functools.partial(score_kernel, first, last, rows),
        grid=(count,),
        out_shape=jax.ShapeDtypeStruct(shape, F32),
        in_specs=specs + [vmem()] * len(after),
        out_specs=whole(shape),
        scratch_shapes=scratch,
        compiler_params=pltpu.CompilerParams(vmem_limit_bytes=GRANT * MIB),
        cost_estimate=cost(micros),
        name="score",
    )(*args, *after)


def final_kernel(place_ref, blocks_ref, top_ref, refined_ref, lines, turned):
    count = blocks_ref.shape[0]
    source = lax.broadcasted_iota(jnp.int32, (count, 128), 0)
    lane = lax.broadcasted_iota(jnp.int32, (count, 128), 1)
    best_here = (source % 2) == (lane // 64)
    best = []
    rest = []
    for place in range(TOPK):
        row = blocks_ref[:, place, :]
        best.append(jnp.where(best_here, row, -jnp.inf))
        if place < 4:
            rest.append(jnp.sum(jnp.where(best_here, 0.0, row), axis=0, keepdims=True))
    while count > 8:
        count //= 2
        best = merge_sorted([part[:count] for part in best], [part[count:] for part in best])
    for turn in (4, 2, 1):
        best = merge_sorted(best, [pltpu.roll(part, turn, 0) for part in best])
    rest = [pltpu.roll(row, 64, 1) for row in rest]
    factor = lax.rsqrt(rest[3] / BINS + EPS)
    for place in range(TOPK):
        lines[place : place + 1, :] = best[place][0:1, :] * factor
    top_ref[0] = lines[...].T
    for place in range(3):
        lines[place : place + 1, :] = rest[place] * factor
    turned[...] = lines[...].T
    share = refined_ref.shape[1]
    first = pl.multiple_of(place_ref[1] * share, share)
    refined_ref[0] = turned[pl.ds(first, share), :3]


def compact_body(patterns, detector_gain, background, bin_map, templates, best_picks):
    orients = lax.axis_size("orient")
    chips = orients // 2
    section = lax.axis_index("section")
    orient = lax.axis_index("orient")
    place = jnp.stack([section, orient, jnp.full_like(orient, orients)]).astype(jnp.int32)
    core = (orient % 2).reshape(1).astype(jnp.int32)
    chip = (orient // 2).reshape(1).astype(jnp.int32)
    rows = templates.shape[0]
    count = patterns.shape[1]
    half = count // 2
    pixels = patterns.shape[2]

    def swap(x):
        return lax.ppermute(x, "orient", [(i, i ^ 1) for i in range(orients)])

    def along(x, by):
        return lax.ppermute(x, "orient", [(i, (i + 2 * by) % orients) for i in range(orients)])

    def hops(x, pairs):
        return lax.ppermute(
            x, "orient", [(2 * i + c, 2 * j + c) for i, j in pairs for c in range(2)]
        )

    def across(x, by):
        return lax.ppermute(x, "section", [(i, i ^ by) for i in range(4)])

    tiles = pixels // TILE
    lines = bin_map.reshape(2 * tiles, TILE // 2)
    present = pl.pallas_call(
        presence_kernel,
        out_shape=jax.ShapeDtypeStruct((ANG, RAD), F32),
        in_specs=[vmem()],
        out_specs=vmem(),
        cost_estimate=cost(2),
        compiler_params=pltpu.CompilerParams(vmem_limit_bytes=SMALL * MIB),
        name="presence",
    )(lines)
    other = swap(present)
    steps = 8
    corrected = pl.pallas_call(
        pixels_kernel,
        grid=(steps,),
        out_shape=jax.ShapeDtypeStruct((pixels, count), BF16),
        in_specs=[
            pl.BlockSpec((1, count, pixels // steps), lambda i: (0, 0, i)),
            pl.BlockSpec((1, pixels // steps), lambda i: (0, i)),
            pl.BlockSpec((1, pixels // steps), lambda i: (0, i)),
        ],
        out_specs=pl.BlockSpec((pixels // steps, count), lambda i: (i, 0)),
        cost_estimate=cost(4),
        compiler_params=pltpu.CompilerParams(vmem_limit_bytes=SMALL * MIB),
        name="pixels",
    )(patterns, detector_gain.reshape(1, pixels), background.reshape(1, pixels))
    corrected = corrected.reshape(tiles, TILE, count)
    bins = bin_map.reshape(tiles // 16, 16, 16, 16).transpose(0, 2, 1, 3).reshape(tiles, TILE)
    table, slot_rows, span = pl.pallas_call(
        slots_kernel,
        out_shape=(
            jax.ShapeDtypeStruct((RAD // 2, PAIR), jnp.int32),
            jax.ShapeDtypeStruct((tiles, TILE), jnp.int32),
            jax.ShapeDtypeStruct((tiles, 128), jnp.int32),
        ),
        in_specs=[vmem()] * 3,
        out_specs=(vmem(),) * 3,
        cost_estimate=cost(3),
        compiler_params=pltpu.CompilerParams(vmem_limit_bytes=SMALL * MIB),
        name="slots",
    )(present, other, bins)
    mine, theirs = pl.pallas_call(
        binning_kernel,
        out_shape=(
            jax.ShapeDtypeStruct((half, ROOM), F32),
            jax.ShapeDtypeStruct((half, ROOM), BF16),
        ),
        in_specs=[smem(), smem(), vmem(), vmem()],
        out_specs=(vmem(),) * 2,
        scratch_shapes=[pltpu.VMEM((ROOM + WINDOW, count), F32), pltpu.VMEM((count, ROOM), F32)],
        compiler_params=pltpu.CompilerParams(vmem_limit_bytes=14 * MIB),
        cost_estimate=cost(6),
        name="binning",
    )(core, span, slot_rows, corrected)
    message, spare = pl.pallas_call(
        combine_kernel,
        out_shape=(
            jax.ShapeDtypeStruct((half, SEG + PAIR), BF16),
            jax.ShapeDtypeStruct((half, ROOM - SEG), BF16),
        ),
        in_specs=[vmem()] * 3,
        out_specs=(vmem(),) * 2,
        cost_estimate=cost(1),
        compiler_params=pltpu.CompilerParams(vmem_limit_bytes=SMALL * MIB),
        name="combine",
    )(mine, swap(theirs), table)

    messages = [along(message, by) for by in range(1, chips)]
    step = hops(spare, [(1, 0), (2, 3)])
    traded = hops(spare, [(1, 2), (2, 1)])
    far_part = hops(spare, [(1, 3), (2, 0)])

    def spread(group):
        return group, across(group, 1), across(group, 2)

    def diagonal(held, after):
        upper, lower = halves(held[1], held[2], after)
        return (*held, across(upper, 2), across(lower, 1)), [upper, lower]

    size = best_picks.shape[0] * count
    turned, local, ranks, crowd = pl.pallas_call(
        picks_kernel,
        out_shape=(
            jax.ShapeDtypeStruct((2 * KEPT, BINS), BF16),
            jax.ShapeDtypeStruct((8, 4 * half), jnp.int32),
            jax.ShapeDtypeStruct((8, 4 * half), jnp.int32),
            jax.ShapeDtypeStruct((8, 128), jnp.int32),
        ),
        in_specs=[smem()] + [vmem()] * 4,
        out_specs=(vmem(),) * 4,
        compiler_params=pltpu.CompilerParams(vmem_limit_bytes=GRANT * MIB),
        cost_estimate=cost(30),
        name="picks",
    )(place, best_picks.reshape(1, size), best_picks.reshape(size, 1), templates, spare)
    group, tables, windows, ranges, full = arrive(
        True, chip, table, [message, messages[0], messages[2]], [], [crowd]
    )
    near = spread(group)
    own, token = columns(GROUPS[0], ranges, tables, templates, turned, [])
    near, gate = diagonal(near, [token])
    group, tables_far, windows_far, ranges, full = arrive(
        False, chip, tables, [messages[1], spare, step, traded, far_part], [full, crowd], [token]
    )
    far = spread(group)
    own_far, token = columns(GROUPS[1], ranges, tables_far, templates, turned, gate)
    squares = pl.pallas_call(
        squares_kernel,
        out_shape=jax.ShapeDtypeStruct((8, half), F32),
        in_specs=[smem()] * 3 + [vmem()] * 5,
        out_specs=vmem(),
        scratch_shapes=[pltpu.VMEM((RAD // 8, half, PAIR), F32)],
        compiler_params=pltpu.CompilerParams(vmem_limit_bytes=GRANT * MIB),
        cost_estimate=cost(2),
        name="squares",
    )(place, windows, windows_far, tables, tables_far, near[0], far[0], token)
    far, gate = diagonal(far, [squares])
    total = score(True, False, rows, own, swap(own), near, None, (), gate, 60)
    blocks = score(
        False, True, rows, own_far, swap(own_far), far, total, (place, local, ranks, squares), (), 5
    )
    blocks = lax.all_to_all(blocks, ("section", "orient"), 0, 0)
    top, refined = pl.pallas_call(
        final_kernel,
        out_shape=(
            jax.ShapeDtypeStruct((1, count, TOPK), F32),
            jax.ShapeDtypeStruct((1, count // orients, 3), F32),
        ),
        in_specs=[smem(), vmem()],
        out_specs=(vmem(), vmem()),
        scratch_shapes=[pltpu.VMEM((TOPK, count), F32), pltpu.VMEM((count, TOPK), F32)],
        cost_estimate=cost(2),
        compiler_params=pltpu.CompilerParams(vmem_limit_bytes=SMALL * MIB),
        name="final",
    )(place, blocks)

    return lax.cond(
        full[0, 0] > 0,
        lambda: dense_body(
            patterns, detector_gain, background, bin_map, templates, best_picks
        ),
        lambda: (top, refined),
    )


def solution(mesh):
    sizes = dict(mesh.shape)
    fits = sizes["section"] == 4 and sizes["orient"] == 8
    return jax.shard_map(
        compact_body if fits else dense_body,
        mesh=mesh,
        in_specs=(
            P("section", None, "orient"),
            P("orient"),
            P("orient"),
            P("orient"),
            P(("section", "orient"), None),
            P(),
        ),
        out_specs=(P("section", None, None), P("section", "orient", None)),
        check_vma=False,
    )
```
